128 devices in a mesh: dp: 8 (over z_hi, x), mp: 16 (over z_lo, y, core).
Axes of the slice: x: 4, y: 4, z: 4 (z_hi: 2, z_lo: 2; z = z_hi * 2 + z_lo), core: 2. Of those that a mesh axis runs over, the one named last changes fastest.
Arguments:
- tokens: bfloat16 [6144, 8192], P('dp', 'mp'), may hold values from -6 to 6
- out_grad: bfloat16 [6144, 8192], P('dp', 'mp'), may hold values from -6 to 6
- first_blocks: bfloat16 [64, 5, 256, 256], P('mp'), may hold values from -0.15625 to 0.15625
- first_index: int32 [64, 5], P('mp'), may hold values from 0 to 1
- second_blocks: bfloat16 [32, 5, 256, 256], P('mp'), may hold values from -0.15625 to 0.15625
- second_index: int32 [32, 5], P('mp'), may hold values from 0 to 3
- first_left: bfloat16 [8192, 512], P('mp'), may hold values from -0.0625 to 0.0625
- first_right: bfloat16 [512, 16384], P(None, 'mp'), may hold values from -0.25 to 0.25
- second_left: bfloat16 [16384, 512], P('mp'), may hold values from -0.046875 to 0.046875
- second_right: bfloat16 [512, 8192], P(None, 'mp'), may hold values from -0.25 to 0.25
Outputs:
- output: bfloat16 [6144, 8192], P('dp', 'mp')
- tokens_grad: bfloat16 [6144, 8192], P('dp', 'mp')
- first_blocks_grad: bfloat16 [64, 5, 256, 256], P('mp')
- first_left_grad: bfloat16 [8192, 512], P('mp')
- first_right_grad: bfloat16 [512, 16384], P(None, 'mp')
- second_blocks_grad: bfloat16 [32, 5, 256, 256], P('mp')
- second_left_grad: bfloat16 [16384, 512], P('mp')
- second_right_grad: bfloat16 [512, 8192], P(None, 'mp')
The draws below stay inside these ranges and needn't reach their ends.
All inputs are finite; a program needn't handle non-finite values.
Results may differ from the reference program's by a relative error of at most 0.015.
Values may be sent and summed in bfloat16 or wider, within the bound.
A program may use at most 128 MiB of HBM per device.

```python
import jax
import jax.numpy as jnp
import numpy as np
from jax import lax

D = 8192
FF = 16384
RANK = 512
BLK = 256
TOK_DEV = 768
LEVELS = 4
TOKENS = 6144
N_DP = 8
N_MP = 16


def set_ends(values, rng, smallest, largest):
    shape = values.shape
    place = [jax.random.randint(jax.random.fold_in(rng, axis), (), 0, shape[axis]) for axis in range(len(shape))]
    values = values.at[tuple(place)].set(smallest)
    longest = shape.index(max(shape))
    place[longest] = (place[longest] + 1) % shape[longest]
    return values.at[tuple(place)].set(largest)


def shard_levels(rng, extent, shards, least, largest):
    factor_of, own = 1.0, jax.random.fold_in(rng, 6)
    for axis_at, blocks in shards:
        heights = jnp.exp(jax.random.uniform(jax.random.fold_in(own, axis_at), (blocks,), jnp.float32, least / len(shards), largest / len(shards)))
        factor_of = factor_of * jnp.repeat(heights, extent[axis_at] // blocks).reshape([-1 if axis == axis_at else 1 for axis in range(len(extent))])
    return factor_of


def bell_draw(own_key, extent, width, bound, pieces=(), kind=jnp.bfloat16):
    drawn = width * jax.random.normal(own_key, extent, jnp.float32)
    if pieces:
        drawn = drawn * shard_levels(own_key, extent, pieces, -0.22, 0.18)
    return jnp.clip(drawn, -bound, bound).astype(kind)


def setup_inputs(seed: int = 0) -> dict:
    splits = jax.random.split(jax.random.key(seed), 11)
    tokens = bell_draw(splits[0], (TOKENS, D), 1.0, 6.0, ((0, 8), (1, 16)))
    out_grad = bell_draw(splits[1], (TOKENS, D), 1.0, 6.0, ((0, 8), (1, 16)))
    first_blocks = bell_draw(splits[2], (FF // BLK, LEVELS + 1, BLK, BLK), (BLK * (LEVELS + 1)) ** -0.5, 0.15625, ((0, 16),))
    first_index = set_ends(jax.random.randint(splits[3], (FF // BLK, LEVELS + 1), 0, D // (N_MP * BLK)), jax.random.fold_in(splits[3], 1), 0, (D // (N_MP * BLK)) - 1).astype(jnp.int32)
    second_blocks = bell_draw(splits[4], (D // BLK, LEVELS + 1, BLK, BLK), (BLK * (LEVELS + 1)) ** -0.5, 0.15625, ((0, 16),))
    second_index = set_ends(jax.random.randint(splits[5], (D // BLK, LEVELS + 1), 0, FF // (N_MP * BLK)), jax.random.fold_in(splits[5], 1), 0, (FF // (N_MP * BLK)) - 1).astype(jnp.int32)
    first_left = bell_draw(splits[6], (D, RANK), D ** -0.5, 0.0625, ((0, 16),))
    first_right = bell_draw(splits[7], (RANK, FF), RANK ** -0.5, 0.25, ((1, 16),))
    second_left = bell_draw(splits[8], (FF, RANK), FF ** -0.5, 0.046875, ((0, 16),))
    second_right = bell_draw(splits[9], (RANK, D), RANK ** -0.5, 0.25, ((1, 16),))
    return {"tokens": tokens, "out_grad": out_grad, "first_blocks": first_blocks, "first_index": first_index, "second_blocks": second_blocks, "second_index": second_index, "first_left": first_left, "first_right": first_right, "second_left": second_left, "second_right": second_right}


def one_hot(index, count):
    return (index[..., None] == jnp.arange(count, dtype=jnp.int32)).astype(jnp.float32)

def rounded(values):
    return lax.optimization_barrier(values.astype(jnp.bfloat16)).astype(jnp.float32)

def partner_table():
    rows = [[device] + [device ^ 1 << level for level in range(LEVELS)] for device in range(N_MP)]
    return jnp.asarray(np.array(rows, dtype=np.int32))

def data_sum(terms):
    return lax.optimization_barrier(jnp.sum(terms, axis=0)).astype(jnp.bfloat16)

def grouped(values):
    return values.astype(jnp.float32).reshape((N_DP, TOK_DEV) + values.shape[1:])

def joined(stacked):
    return jnp.transpose(stacked, (1, 0, 2)).reshape(TOKENS, -1)

def reference(tokens, out_grad, first_blocks, first_index, second_blocks, second_index, first_left, first_right, second_left, second_right):
    table = partner_table()
    sources = LEVELS + 1
    model_count = D // (N_MP * BLK)
    hidden_count = FF // (N_MP * BLK)
    devices = jnp.arange(N_MP, dtype=jnp.int32)
    token_split = tokens.reshape(TOKENS, N_MP, model_count, BLK)
    grad_split = out_grad.reshape(TOKENS, N_MP, model_count, BLK)
    first_w = first_blocks.reshape(N_MP, hidden_count, sources, BLK, BLK)
    second_w = second_blocks.reshape(N_MP, model_count, sources, BLK, BLK)
    first_pattern = first_index.reshape(N_MP, hidden_count, sources)
    second_pattern = second_index.reshape(N_MP, model_count, sources)
    first_cols = first_right.reshape(RANK, N_MP, hidden_count * BLK)
    second_cols = second_right.reshape(RANK, N_MP, model_count * BLK)
    rank_first = jnp.dot(tokens, first_left, preferred_element_type=jnp.float32).astype(jnp.bfloat16)

    def first_pick(device):
        x_all = jnp.take(token_split, table[device], axis=1).astype(jnp.float32)
        return jnp.einsum('tkdi,fkd->tfki', x_all, one_hot(first_pattern[device], model_count))

    def first_forward(device):
        block = jnp.einsum('tfki,fkio->tfo', first_pick(device), first_w[device].astype(jnp.float32))
        return block.reshape(TOKENS, -1) + jnp.dot(rank_first, first_cols[:, device], preferred_element_type=jnp.float32)
    pre = joined(lax.map(first_forward, devices))
    hidden = jax.nn.silu(pre).astype(jnp.bfloat16)
    hidden_split = hidden.reshape(TOKENS, N_MP, hidden_count, BLK)
    rank_second = jnp.dot(hidden, second_left, preferred_element_type=jnp.float32).astype(jnp.bfloat16)

    def second_pick(device):
        h_all = jnp.take(hidden_split, table[device], axis=1).astype(jnp.float32)
        return jnp.einsum('tkdj,ekd->tekj', h_all, one_hot(second_pattern[device], hidden_count))

    def second_forward(device):
        block = jnp.einsum('tekj,ekjo->teo', second_pick(device), second_w[device].astype(jnp.float32))
        return block.reshape(TOKENS, -1) + jnp.dot(rank_second, second_cols[:, device], preferred_element_type=jnp.float32)
    output = joined(lax.map(second_forward, devices)).astype(jnp.bfloat16)

    def second_weight_grad(device):
        pick = second_pick(device).reshape(N_DP, TOK_DEV, model_count, sources, BLK)
        grads = jnp.take(grad_split, device, axis=1).astype(jnp.float32).reshape(N_DP, TOK_DEV, model_count, BLK)
        return data_sum(jnp.einsum('gtekj,gteo->gekjo', pick, grads))
    second_blocks_grad = lax.map(second_weight_grad, devices).reshape(D // BLK, sources, BLK, BLK)
    second_right_grad = data_sum(jnp.einsum('gtr,gto->gro', grouped(rank_second), grouped(out_grad)))
    back_second = jnp.dot(out_grad, second_right.T, preferred_element_type=jnp.float32).astype(jnp.bfloat16)
    second_left_grad = data_sum(jnp.einsum('gtf,gtr->gfr', grouped(hidden), grouped(back_second)))

    def hidden_back(owner):
        total = jnp.zeros((TOKENS, hidden_count, BLK), jnp.float32)
        for source in range(sources):
            other = table[owner, source]
            grads = jnp.take(grad_split, other, axis=1).astype(jnp.float32)
            weights = second_w[other, :, source].astype(jnp.float32)
            flow = jnp.einsum('teo,ejo->tej', grads, weights)
            hot = one_hot(second_pattern[other, :, source], hidden_count)
            total = total + rounded(jnp.einsum('tej,ed->tdj', flow, hot))
        return total.reshape(TOKENS, -1)
    hidden_grad = joined(lax.map(hidden_back, devices)) + jnp.dot(back_second, second_left.T, preferred_element_type=jnp.float32)
    sigma = jax.nn.sigmoid(pre)
    pre_grad = (hidden_grad * sigma * (1.0 + pre * (1.0 - sigma))).astype(jnp.bfloat16)
    pre_split = pre_grad.reshape(TOKENS, N_MP, hidden_count, BLK)

    def first_weight_grad(device):
        pick = first_pick(device).reshape(N_DP, TOK_DEV, hidden_count, sources, BLK)
        grads = jnp.take(pre_split, device, axis=1).astype(jnp.float32).reshape(N_DP, TOK_DEV, hidden_count, BLK)
        return data_sum(jnp.einsum('gtfki,gtfo->gfkio', pick, grads))
    first_blocks_grad = lax.map(first_weight_grad, devices).reshape(FF // BLK, sources, BLK, BLK)
    first_right_grad = data_sum(jnp.einsum('gtr,gtf->grf', grouped(rank_first), grouped(pre_grad)))
    back_first = jnp.dot(pre_grad, first_right.T, preferred_element_type=jnp.float32).astype(jnp.bfloat16)
    first_left_grad = data_sum(jnp.einsum('gtd,gtr->gdr', grouped(tokens), grouped(back_first)))

    def token_back(owner):
        total = jnp.zeros((TOKENS, model_count, BLK), jnp.float32)
        for source in range(sources):
            other = table[owner, source]
            grads = jnp.take(pre_split, other, axis=1).astype(jnp.float32)
            weights = first_w[other, :, source].astype(jnp.float32)
            flow = jnp.einsum('tfo,fio->tfi', grads, weights)
            hot = one_hot(first_pattern[other, :, source], model_count)
            total = total + rounded(jnp.einsum('tfi,fd->tdi', flow, hot))
        return total.reshape(TOKENS, -1)
    tokens_grad = (joined(lax.map(token_back, devices)) + jnp.dot(back_first, first_left.T, preferred_element_type=jnp.float32)).astype(jnp.bfloat16)
    return (output, tokens_grad, first_blocks_grad, first_left_grad, first_right_grad, second_blocks_grad, second_left_grad, second_right_grad)
```

```python
import jax
import jax.numpy as jnp
from jax import lax
from jax.experimental import pallas as pl
from jax.experimental.pallas import tpu as pltpu
from jax.sharding import PartitionSpec as P

BF = jnp.bfloat16
F32 = jnp.float32
CHUNKS = 4


def nn(left, right):
    return jnp.dot(left, right, preferred_element_type=F32)


def nt(left, right):
    return lax.dot_general(left, right, (((1,), (1,)), ((), ())), preferred_element_type=F32)


def flip(bit, by):
    return 1 - bit if by else bit


def tile_of(index, at):
    hot = (index == at).astype(F32)
    return jnp.broadcast_to(hot, (16, 128)).astype(BF)


def masked(weights, tiles):
    parts = []
    for weight, tile in zip(weights, tiles):
        wide = jnp.concatenate([tile, tile], axis=1)
        tall = weight.reshape(weight.shape[0] // 16, 16, weight.shape[1])
        parts.append((tall * wide[None]).reshape(weight.shape))
    return jnp.concatenate(parts, axis=1)


class Place:
    def __init__(self):
        self.dp = lax.axis_index("dp")
        self.mp = lax.axis_index("mp")
        self.core = lax.rem(self.mp, 2)
        chip = lax.div(self.mp, 2)
        self.chip = chip
        self.y0 = lax.rem(chip, 2)
        self.y1 = lax.rem(lax.div(chip, 2), 2)
        self.z = lax.div(chip, 4)
        self.x0 = lax.rem(self.dp, 2)
        self.x1 = lax.rem(lax.div(self.dp, 2), 2)
        self.z_hi = lax.div(self.dp, 4)

    def mp_peer(self, chip_bits, core_bit=0):
        y0 = flip(self.y0, chip_bits & 1)
        y1 = flip(self.y1, chip_bits & 2)
        z = flip(self.z, chip_bits & 4)
        return (self.dp, ((z * 2 + y1) * 2 + y0) * 2 + flip(self.core, core_bit))

    def chip_peer(self, chip_bits):
        y0 = flip(self.y0, chip_bits & 1)
        y1 = flip(self.y1, chip_bits & 2)
        z = flip(self.z, chip_bits & 4)
        return (z * 2 + y1) * 2 + y0

    def dp_peer(self, bits):
        x0 = flip(self.x0, bits & 1)
        x1 = flip(self.x1, bits & 2)
        z = flip(self.z_hi, bits & 4)
        return ((z * 2 + x1) * 2 + x0, self.mp)

    def level(self, level):
        return [None, self.mp_peer(0, 1), self.mp_peer(1), self.mp_peer(2), self.mp_peer(4)][level]


def greet(peers):
    barrier = pltpu.get_barrier_semaphore()
    for peer in peers:
        pl.semaphore_signal(barrier, inc=1, device_id=peer, device_id_type=pl.DeviceIdType.MESH)
    pl.semaphore_wait(barrier, len(peers))


def remote(src, dst, sems, at, peer):
    send, recv = sems
    return pltpu.make_async_remote_copy(
        src_ref=src,
        dst_ref=dst,
        send_sem=send.at[at],
        recv_sem=recv.at[at],
        device_id=peer,
        device_id_type=pl.DeviceIdType.MESH,
    )


class RankSum:
    def __init__(self, place, rows, half, result, own, away, near, chip_sum, far, sems):
        self.place, self.result, self.sems = place, result, sems
        self.own, self.away, self.near, self.chip_sum, self.far = own, away, near, chip_sum, far
        self.part = rows // 8
        self.half = half
        self.columns = pl.ds(pl.multiple_of(place.core * half, half), half)
        self.rows = pl.ds(pl.multiple_of(place.chip * self.part, self.part), self.part)
        sibling = place.mp_peer(0, 1)
        self.cores = remote(away, near, sems, 0, sibling)
        self.scatter = []
        self.gather = []
        for bits in range(1, 8):
            other = pl.ds(pl.multiple_of(place.chip_peer(bits) * self.part, self.part), self.part)
            peer = place.mp_peer(bits)
            self.scatter.append(
                remote(chip_sum.at[:, other, :], far.at[bits - 1], sems, bits, peer)
            )
            mine = result.at[:, self.rows, self.columns]
            self.gather.append(remote(mine, mine, sems, 7 + bits, peer))
        whole = result.at[:, :, self.columns]
        self.back = remote(whole, whole, sems, 15, sibling)

    def set(self, which, own, away):
        self.own[which] = own
        self.away[which] = away.astype(BF)

    def start(self):
        self.cores.start()

    def step_chip(self):
        self.cores.wait()
        for which in range(2):
            self.chip_sum[which] = (self.own[which] + self.near[which].astype(F32)).astype(BF)
        for copy in self.scatter:
            copy.start()

    def step_sum(self):
        total = self.chip_sum[:, self.rows, :].astype(F32)
        for copy in self.scatter:
            copy.wait()
        for bits in range(7):
            total = total + self.far[bits].astype(F32)
        self.result[:, self.rows, self.columns] = total.astype(BF)
        for copy in self.gather:
            copy.start()

    def step_back(self):
        for copy in self.gather:
            copy.wait()
        self.back.start()

    def finish(self):
        self.back.wait()


class Spread:
    def __init__(self, place, src, dst, sems):
        blocked = len(src.shape) == 3
        blocks = src.shape[0] if blocked else 1
        rows = src.shape[-2]
        step = rows * blocks // CHUNKS

        def source(part, block):
            return src.at[block, part, :] if blocked else src.at[part, :]

        def target(slot, part, block):
            return dst.at[slot, block, part, :] if blocked else dst.at[slot, part, :]

        self.direct = [
            remote(src, dst.at[slot], sems, at, place.level(level))
            for at, (slot, level) in enumerate(((3, 4), (0, 1)))
        ]
        self.near = []
        self.onward = []
        at = 2
        for block in range(blocks):
            for start in range(0, rows, step):
                part = pl.ds(start, step)
                self.near.append(
                    remote(source(part, block), target(1, part, block), sems, at, place.level(2))
                )
                self.onward.append(
                    remote(
                        target(1, part, block),
                        target(2, part, block),
                        sems,
                        at + CHUNKS,
                        place.mp_peer(3),
                    )
                )
                at = at + 1

    def start_direct(self):
        for copy in self.direct:
            copy.start()

    def start_near(self, chunk):
        self.near[chunk].start()

    def pass_on(self, chunk):
        self.near[chunk].wait_recv()
        self.onward[chunk].start()

    def wait_direct(self):
        for copy in self.direct:
            copy.wait_recv()

    def wait_onward(self):
        for copy in self.onward:
            copy.wait_recv()

    def close(self):
        for copy in self.direct + self.near + self.onward:
            copy.wait_send()


class Reduced:
    def __init__(self, place, grad, lead, first, second, third, sems, credit, at):
        self.credit, self.at, self.lead = credit, at, lead
        blocks = pl.ds(lead, first.shape[1])
        self.grad, self.bufs = grad, (first, second, third)
        rows = grad.shape[2]
        x0, x1, z = place.x0, place.x1, place.z_hi
        cross = x0 + x1 - 2 * x0 * x1
        near, back, far = place.dp_peer(1), place.dp_peer(3), place.dp_peer(4)
        self.greeted = (near, back, far)
        self.steps = [[] for _ in range(6)]
        self.kept = [[] for _ in range(3)]
        for h in range(2):
            keys = (cross, x1, z) if h == 0 else (x1, x0, z)
            peers = (near, back, far) if h == 0 else (back, near, far)
            offset, size = 0, rows
            for step in range(3):
                size = size // 2
                keep = pl.ds(pl.multiple_of(offset + keys[step] * size, size), size)
                send = pl.ds(pl.multiple_of(offset + (1 - keys[step]) * size, size), size)
                self.kept[step].append(keep)
                self.steps[step].append(
                    remote(
                        grad.at[h, blocks, send, :],
                        self.bufs[step].at[h],
                        sems,
                        (at, h, step),
                        peers[step],
                    )
                )
                own = grad.at[h, blocks, keep, :]
                self.steps[5 - step].append(
                    remote(own, own, sems, (at, h, 5 - step), peers[step])
                )
                offset = offset + keys[step] * size

    def free(self, kind, peer):
        pl.semaphore_signal(
            self.credit.at[self.at, kind],
            inc=1,
            device_id=peer,
            device_id_type=pl.DeviceIdType.MESH,
        )

    def start(self, step):
        if step == 3:
            pl.semaphore_wait(self.credit.at[self.at, 1], 1)
        if step == 4:
            pl.semaphore_wait(self.credit.at[self.at, 0], 2)
        for copy in self.steps[step]:
            copy.start()

    def turn(self, step):
        self.wait(step)
        self.start(step + 1)

    def wait(self, step):
        for h, copy in enumerate(self.steps[step]):
            copy.wait()
            if step < 3:
                keep = self.kept[step][h]
                for n in range(self.bufs[step].shape[1]):
                    self.grad[h, self.lead + n, keep, :] = (
                        self.grad[h, self.lead + n, keep, :].astype(F32)
                        + self.bufs[step][h, n].astype(F32)
                    ).astype(BF)
        if step == 1:
            self.free(0, self.greeted[0])
            self.free(0, self.greeted[1])
        if step == 2:
            self.free(1, self.greeted[2])


def layer_kernel(
    tokens,
    out_grad,
    w1,
    index1,
    index1_rows,
    w2,
    index2,
    index2_sent,
    first_left,
    first_right,
    second_left,
    second_right,
    output,
    tokens_grad,
    g_w1,
    g_fl,
    g_fr,
    g_w2,
    g_sl,
    g_sr,
    tokens_own,
    tokens_in,
    grads_in,
    w2_in,
    index_in,
    index_smem,
    hidden,
    hidden_t,
    pre_grad,
    tokens_t,
    rank_first_t,
    slope,
    own,
    away,
    chip_sum,
    near_a,
    far_a,
    ranks_a,
    near_b,
    far_b,
    ranks_b,
    swap,
    sent,
    out_in,
    *rest,
):
    bufs, rest = rest[:21], rest[21:]
    (
        tok_send,
        tok_recv,
        grad_send,
        grad_recv,
        rank_send_a,
        rank_recv_a,
        rank_send_b,
        rank_recv_b,
        w_send,
        w_recv,
        i_send,
        i_recv,
        dp_send,
        dp_recv,
        credit,
        swap_send,
        swap_recv,
        x_send,
        x_recv,
        inbox_free,
        local,
    ) = rest
    place = Place()
    rows = pre_grad.shape[0]
    half = first_left.shape[1] // 2
    width = w1.shape[2]
    mine = pl.ds(pl.multiple_of(place.core * half, half), half)
    other = pl.ds(pl.multiple_of((1 - place.core) * half, half), half)

    loads = [
        pltpu.make_async_copy(
            tokens.at[:, pl.ds(d * width, width)], tokens_own.at[d], local.at[d]
        )
        for d in range(2)
    ]
    for load in loads:
        load.start()
    greet(
        [place.mp_peer(bits) for bits in range(1, 8)]
        + [place.mp_peer(0, 1)]
        + [place.dp_peer(bits) for bits in (1, 3, 4)]
    )
    spread_tok = Spread(place, tokens_own, tokens_in, (tok_send, tok_recv))
    spread_grad = Spread(place, out_grad, grads_in, (grad_send, grad_recv))
    sums_a = RankSum(
        place, rows, half, ranks_a, own, away, near_a, chip_sum, far_a, (rank_send_a, rank_recv_a)
    )
    sums_b = RankSum(
        place, rows, half, ranks_b, own, away, near_b, chip_sum, far_b, (rank_send_b, rank_recv_b)
    )
    w_copies = [
        remote(w2.at[:, level], w2_in.at[level - 1], (w_send, w_recv), level - 1, place.level(level))
        for level in (4, 2, 3, 1)
    ]
    i_copies = [
        remote(
            index2_sent.at[level],
            index_in.at[level - 1],
            (i_send, i_recv),
            level - 1,
            place.level(level),
        )
        for level in range(1, 5)
    ]
    dp_sems = (dp_send, dp_recv)
    grads = ((g_w2, 0), (g_sl, 0), (g_w1, 0), (g_w1, 5), (g_fr, 0), (g_sr, 0), (g_fl, 0))
    r_w2, r_sl, r_w1a, r_w1b, r_fr, r_sr, r_fl = [
        Reduced(place, grad, lead, *bufs[3 * at : 3 * at + 3], dp_sems, credit, at)
        for at, (grad, lead) in enumerate(grads)
    ]

    for load in loads:
        load.wait()
    for chunk in range(CHUNKS):
        spread_tok.start_near(chunk)
    spread_tok.start_direct()
    for copy in i_copies:
        copy.start()
    both = jnp.concatenate([tokens_own[0], tokens_own[1]], axis=1)
    sums_a.set(0, nn(both, first_left[:, mine]), nn(both, first_left[:, other]))
    sums_a.set(1, nt(out_grad[...], second_right[mine, :]), nt(out_grad[...], second_right[other, :]))
    sums_a.start()
    for d in range(2):
        tokens_t[0, d] = tokens_own[d].T
    spread_tok.pass_on(0)
    sums_a.step_chip()
    spread_grad.start_near(0)
    spread_grad.start_near(1)
    spread_tok.pass_on(1)
    spread_grad.start_direct()
    spread_tok.pass_on(2)
    spread_grad.start_near(2)
    spread_grad.start_near(3)
    spread_tok.pass_on(3)
    for copy in w_copies:
        copy.start()
    sums_a.step_sum()
    spread_tok.wait_direct()
    for level in (1, 4):
        for d in range(2):
            tokens_t[level, d] = tokens_in[level - 1, d].T
    sums_a.step_back()
    for d in range(2):
        tokens_t[2, d] = tokens_in[1, d].T
    spread_grad.pass_on(0)
    spread_tok.wait_onward()
    for d in range(2):
        tokens_t[3, d] = tokens_in[2, d].T
    sums_a.finish()
    rank_first_t[...] = ranks_a[0].T

    for f in range(4):
        columns = pl.ds(f * width, width)
        picks = []
        for level in range(5):
            at = index1[f, level]
            picks.append(tokens_own[at] if level == 0 else tokens_in[level - 1, at])
        pre = nn(jnp.concatenate(picks, axis=1), w1[f].reshape(5 * width, width))
        pre = pre + nn(ranks_a[0], first_right[:, columns])
        sigma = 1.0 / (1.0 + jnp.exp(-pre))
        active = (pre * sigma).astype(BF)
        hidden[f] = active
        hidden_t[f] = active.T
        slope[f] = sigma * (1.0 + pre * (1.0 - sigma))
        if f < 3:
            spread_grad.pass_on(f + 1)
    spread_tok.close()
    for peer in (place.level(1), place.level(2), place.mp_peer(3), place.level(4)):
        pl.semaphore_signal(inbox_free, inc=1, device_id=peer, device_id_type=pl.DeviceIdType.MESH)

    for copy in i_copies + w_copies:
        copy.wait()
    fetch = pltpu.make_async_copy(index_in, index_smem, local.at[0])
    fetch.start()
    fetch.wait()
    spread_grad.wait_direct()

    def index_of(level, e):
        return index2[e, 0] if level == 0 else index_smem[level - 1, 0, e]

    def weight_of(level, e):
        return w2[e, 0] if level == 0 else w2_in[level - 1, e]

    def second_grads(level):
        for e in range(2):
            columns = pl.ds(e * width, width)
            flow = out_grad[:, columns] if level == 0 else grads_in[level - 1, :, columns]
            g_w2[e, level] = nn(hidden_t[index_of(level, e)], flow).astype(BF)

    for d in range(4):
        part = pl.ds(d % 2 * width, width)
        g_sl[d // 2, 0, part, :] = nn(hidden_t[d], ranks_a[1]).astype(BF)
    r_sl.start(0)
    for level in (0, 1, 4, 2):
        second_grads(level)
    spread_grad.wait_onward()
    second_grads(3)
    r_w2.start(0)

    for d in range(4):
        columns = pl.ds(d * width, width)
        total = nt(ranks_a[1], second_left[columns, :])
        for level in range(5):
            weights = [weight_of(level, e) for e in range(2)]
            row = index2_sent if level == 0 else index_in
            at = max(level - 1, 0)
            tiles = [tile_of(row[at, 0:1, e : e + 1], d) for e in range(2)]
            flow = out_grad[...] if level == 0 else grads_in[level - 1]
            total = total + nt(flow, masked(weights, tiles))
        pre_grad[:, columns] = (total * slope[d]).astype(BF)
    spread_grad.close()
    r_sl.turn(0)
    r_w2.turn(0)

    units = jnp.concatenate([hidden[d] for d in range(4)], axis=1)
    sums_b.set(0, nn(units, second_left[:, mine]), nn(units, second_left[:, other]))
    sums_b.set(1, nt(pre_grad[...], first_right[mine, :]), nt(pre_grad[...], first_right[other, :]))
    sums_b.start()

    def first_grads(f):
        for level in range(5):
            g_w1[f // 2, (f % 2) * 5 + level] = nn(
                tokens_t[level, index1[f, level]], pre_grad[:, f * width : f * width + width]
            ).astype(BF)

    first_grads(0)
    first_grads(2)
    r_w1a.start(0)
    sums_b.step_chip()
    first_grads(1)
    first_grads(3)
    r_w1b.start(0)
    for h in range(2):
        g_fr[h, 0] = nn(rank_first_t[h * 256 : h * 256 + 256, :], pre_grad[...]).astype(BF)
    r_fr.start(0)
    r_sl.turn(1)
    r_w2.turn(1)

    def out_part(level, e):
        return nn(hidden[index_of(level, e)], weight_of(level, e))

    def tok_part(level, d):
        weights = [w1[f, level] for f in range(4)]
        tiles = [tile_of(index1_rows[f : f + 1, level : level + 1], d) for f in range(4)]
        return nt(pre_grad[...], masked(weights, tiles))

    def out_box(slot, block):
        return out_in[slot, :, pl.ds(block * width, width)]

    def tok_box(slot, block):
        return tokens_in[slot, block]

    copies = []
    for side, inbox in enumerate((out_in, tokens_in)):
        copies.append([])
        for level, peer in enumerate((None, place.level(1), place.level(2), place.mp_peer(3), place.level(4))):
            if peer is None:
                copies[side].append(None)
                continue
            at = level - 1
            copies[side].append(
                [
                    remote(
                        sent.at[at, block],
                        inbox.at[at, block] if side else inbox.at[at, :, pl.ds(block * width, width)],
                        (x_send, x_recv),
                        (side, at, block),
                        peer,
                    )
                    for block in range(2)
                ]
            )

    parts = (out_part, tok_part)
    boxes = (out_box, tok_box)

    def send_parts(side):
        for level in (3, 4, 1):
            for block in range(2):
                if side:
                    copies[0][level][block].wait_send()
                sent[level - 1, block] = parts[side](level, block).astype(BF)
                copies[side][level][block].start()

    def send_joined(side):
        for block in range(2):
            copies[side][3][block].wait_recv()
            if side:
                copies[0][2][block].wait_send()
            joined = parts[side](2, block) + boxes[side](2, block).astype(F32)
            sent[1, block] = joined.astype(BF)
            copies[side][2][block].start()

    def join(side, rank_part, result):
        for block in range(2):
            total = parts[side](0, block) + rank_part(block)
            for level in (1, 4, 2):
                copies[side][level][block].wait_recv()
                total = total + boxes[side](level - 1, block).astype(F32)
            result[:, block * width : block * width + width] = total.astype(BF)

    send_parts(0)
    r_w1a.turn(0)
    sums_b.step_sum()
    send_joined(0)
    pl.semaphore_wait(inbox_free, 4)
    send_parts(1)
    r_sl.turn(2)
    r_w2.wait(2)
    eighth = r_w2.kept[2]
    swaps = [
        remote(
            g_w2.at[h, level, eighth[h], :],
            swap.at[h, level - 1],
            (swap_send, swap_recv),
            (h, level - 1),
            place.level(level),
        )
        for h in range(2)
        for level in range(1, 5)
    ]
    for copy in swaps:
        copy.start()
    r_w1b.turn(0)
    sums_b.step_back()
    r_w1a.turn(1)
    r_fr.turn(0)
    for copy in swaps:
        copy.wait()
    for h in range(2):
        for level in range(1, 5):
            g_w2[h, level, eighth[h], :] = swap[h, level - 1]
    r_w2.start(3)
    r_sl.turn(3)
    sums_b.finish()
    rank_second_t = ranks_b[0].T
    for h in range(2):
        g_sr[h, 0] = nn(rank_second_t[h * 256 : h * 256 + 256, :], out_grad[...]).astype(BF)
        g_fl[h, 0] = nn(tokens_t[0, h], ranks_b[1]).astype(BF)
    r_sr.start(0)
    r_fl.start(0)
    r_w1b.turn(1)
    send_joined(1)
    r_w2.turn(3)
    r_fr.turn(1)
    r_w1a.turn(2)
    r_sr.turn(0)
    r_fl.turn(0)
    join(0, lambda e: nn(ranks_b[0], second_right[:, e * width : e * width + width]), output)
    r_sl.turn(4)
    r_w2.turn(4)
    r_w1b.turn(2)
    r_w1a.turn(3)
    r_fr.turn(2)
    r_sr.turn(1)
    r_fl.turn(1)
    join(1, lambda d: nt(ranks_b[1], first_left[d * width : d * width + width, :]), tokens_grad)
    r_w1b.turn(3)
    r_w1a.turn(4)
    r_fr.turn(3)
    r_sr.turn(2)
    r_fl.turn(2)
    r_w1b.turn(4)
    r_fr.turn(4)
    r_sr.turn(3)
    r_fl.turn(3)
    r_sr.turn(4)
    r_fl.turn(4)
    for grad in (r_sl, r_w2, r_w1a, r_w1b, r_fr, r_sr, r_fl):
        grad.wait(5)
    for level in range(1, 5):
        for block in range(2):
            copies[1][level][block].wait_send()


def copy_kernel(*refs):
    count = (len(refs) - 1) // 2
    sems = refs[-1]
    copies = []
    for at in range(count):
        src, dst = refs[at], refs[count + at]
        step = src.shape[0] // 2
        for h in range(2):
            part = pl.ds(h * step, step)
            copies.append(
                pltpu.make_async_copy(src.at[part], dst.at[part], sems.at[len(copies)])
            )
    for copy in copies:
        copy.start()
    for copy in copies:
        copy.wait()


def body(
    tokens,
    out_grad,
    first_blocks,
    first_index,
    second_blocks,
    second_index,
    first_left,
    first_right,
    second_left,
    second_right,
):
    rows, features = tokens.shape
    rank = first_left.shape[1]
    units = first_right.shape[1]
    width = first_blocks.shape[2]
    vmem = pl.BlockSpec(memory_space=pltpu.VMEM)
    smem = pl.BlockSpec(memory_space=pltpu.SMEM)
    anywhere = pl.BlockSpec(memory_space=pl.ANY)
    dma = pltpu.SemaphoreType.DMA

    def shape(*extent):
        return jax.ShapeDtypeStruct(extent, BF)

    half = rank // 2
    index_sent = jnp.pad(second_index.T[:, None, :], ((0, 0), (0, 7), (0, 126)))
    grads = [
        (2, 5, width, width),
        (2, 1, units // 2, rank),
        (2, 10, width, width),
        (2, 1, rank // 2, units),
        (2, 1, rank // 2, features),
        (2, 1, features // 2, rank),
    ]
    pieces = grads[:2] + [(2, 5, width, width)] * 2 + grads[3:]
    inboxes = []
    for two, count, tall, wide in pieces:
        for step in (2, 4, 8):
            inboxes.append(pltpu.VMEM((two, count, tall // step, wide), BF))
    scratch = [
        pltpu.VMEM((features // width, rows, width), BF),
        pltpu.VMEM((4, features // width, rows, width), BF),
        pltpu.VMEM((4, rows, features), BF),
        pltpu.VMEM((4, 2, width, width), BF),
        pltpu.VMEM((4, 8, 128), jnp.int32),
        pltpu.SMEM((4, 8, 128), jnp.int32),
        pltpu.VMEM((units // width, rows, width), BF),
        pltpu.VMEM((units // width, width, rows), BF),
        pltpu.VMEM((rows, units), BF),
        pltpu.VMEM((5, features // width, width, rows), BF),
        pltpu.VMEM((rank, rows), BF),
        pltpu.VMEM((units // width, rows, width), F32),
        pltpu.VMEM((2, rows, half), F32),
        pltpu.VMEM((2, rows, half), BF),
        pltpu.VMEM((2, rows, half), BF),
    ]
    for _ in range(2):
        scratch += [
            pltpu.VMEM((2, rows, half), BF),
            pltpu.VMEM((7, 2, rows // 8, half), BF),
            pltpu.VMEM((2, rows, rank), BF),
        ]
    scratch += [
        pltpu.VMEM((2, 4, width // 8, width), BF),
        pltpu.VMEM((4, features // width, rows, width), BF),
        pltpu.VMEM((4, rows, features), BF),
    ]
    semaphores = [dma((2 + 2 * CHUNKS,))] * 4 + [dma((16,))] * 4 + [dma((4,))] * 4
    semaphores += [dma((7, 2, 6))] * 2 + [pltpu.SemaphoreType.REGULAR((7, 2))]
    semaphores += [dma((2, 4))] * 2 + [dma((2, 4, 2))] * 2
    semaphores += [pltpu.SemaphoreType.REGULAR, dma((2,))]
    results = pl.pallas_call(
        layer_kernel,
        out_shape=[shape(rows, features), shape(rows, features)]
        + [shape(*grads[at]) for at in (2, 5, 3, 0, 1, 4)],
        in_specs=[anywhere, vmem, vmem, smem, vmem, vmem, smem] + [vmem] * 5,
        out_specs=[vmem] * 8,
        scratch_shapes=scratch + inboxes + semaphores,
        compiler_params=pltpu.CompilerParams(
            collective_id=0, has_side_effects=True, vmem_limit_bytes=63 * 2**20
        ),
        name="layer_kernel",
    )(
        tokens,
        out_grad,
        first_blocks,
        first_index,
        first_index,
        second_blocks,
        second_index,
        index_sent,
        first_left,
        first_right,
        second_left,
        second_right,
    )
    output, tokens_grad, g_w1, g_fl, g_fr, g_w2, g_sl, g_sr = pl.pallas_call(
        copy_kernel,
        out_shape=[shape(*result.shape) for result in results],
        in_specs=[anywhere] * 8,
        out_specs=[anywhere] * 8,
        scratch_shapes=[dma((16,))],
        name="copy_kernel",
    )(*results)
    return (
        output,
        tokens_grad,
        g_w1.reshape(first_blocks.shape),
        g_fl.reshape(first_left.shape),
        g_fr.reshape(first_right.shape),
        g_w2.reshape(second_blocks.shape),
        g_sl.reshape(second_left.shape),
        g_sr.reshape(second_right.shape),
    )


def solution(mesh):
    placed = (
        P("dp", "mp"),
        P("dp", "mp"),
        P("mp", None, None, None),
        P("mp", None),
        P("mp", None, None, None),
        P("mp", None),
        P("mp", None),
        P(None, "mp"),
        P("mp", None),
        P(None, "mp"),
    )
    return jax.shard_map(
        body,
        mesh=mesh,
        in_specs=placed,
        out_specs=(
            P("dp", "mp"),
            P("dp", "mp"),
            P("mp", None, None, None),
            P("mp", None),
            P(None, "mp"),
            P("mp", None, None, None),
            P("mp", None),
            P(None, "mp"),
        ),
        check_vma=False,
    )
```

```python
import jax
import jax.numpy as jnp
from jax import lax
from jax.experimental import pallas as pl
from jax.experimental.pallas import tpu as pltpu
from jax.sharding import PartitionSpec as P

BF = jnp.bfloat16
F32 = jnp.float32
CHUNKS = 4


def nn(left, right):
    return jnp.dot(left, right, preferred_element_type=F32)


def nt(left, right):
    return lax.dot_general(left, right, (((1,), (1,)), ((), ())), preferred_element_type=F32)


def flip(bit, by):
    return 1 - bit if by else bit


def tile_of(index, at):
    hot = (index == at).astype(F32)
    return jnp.broadcast_to(hot, (16, 128)).astype(BF)


def masked(weights, tiles):
    parts = []
    for weight, tile in zip(weights, tiles):
        wide = jnp.concatenate([tile, tile], axis=1)
        tall = weight.reshape(weight.shape[0] // 16, 16, weight.shape[1])
        parts.append((tall * wide[None]).reshape(weight.shape))
    return jnp.concatenate(parts, axis=1)


class Place:
    def __init__(self):
        self.dp = lax.axis_index("dp")
        self.mp = lax.axis_index("mp")
        self.core = lax.rem(self.mp, 2)
        chip = lax.div(self.mp, 2)
        self.chip = chip
        self.y0 = lax.rem(chip, 2)
        self.y1 = lax.rem(lax.div(chip, 2), 2)
        self.z = lax.div(chip, 4)
        self.x0 = lax.rem(self.dp, 2)
        self.x1 = lax.rem(lax.div(self.dp, 2), 2)
        self.z_hi = lax.div(self.dp, 4)

    def mp_peer(self, chip_bits, core_bit=0):
        y0 = flip(self.y0, chip_bits & 1)
        y1 = flip(self.y1, chip_bits & 2)
        z = flip(self.z, chip_bits & 4)
        return (self.dp, ((z * 2 + y1) * 2 + y0) * 2 + flip(self.core, core_bit))

    def chip_peer(self, chip_bits):
        y0 = flip(self.y0, chip_bits & 1)
        y1 = flip(self.y1, chip_bits & 2)
        z = flip(self.z, chip_bits & 4)
        return (z * 2 + y1) * 2 + y0

    def dp_peer(self, bits):
        x0 = flip(self.x0, bits & 1)
        x1 = flip(self.x1, bits & 2)
        z = flip(self.z_hi, bits & 4)
        return ((z * 2 + x1) * 2 + x0, self.mp)

    def level(self, level):
        return [None, self.mp_peer(0, 1), self.mp_peer(1), self.mp_peer(2), self.mp_peer(4)][level]


def greet(peers):
    barrier = pltpu.get_barrier_semaphore()
    for peer in peers:
        pl.semaphore_signal(barrier, inc=1, device_id=peer, device_id_type=pl.DeviceIdType.MESH)
    pl.semaphore_wait(barrier, len(peers))


def remote(src, dst, sems, at, peer):
    send, recv = sems
    return pltpu.make_async_remote_copy(
        src_ref=src,
        dst_ref=dst,
        send_sem=send.at[at],
        recv_sem=recv.at[at],
        device_id=peer,
        device_id_type=pl.DeviceIdType.MESH,
    )


def at_ds(index, size):
    return pl.ds(pl.multiple_of(index * size, size), size)


def repeat(count, step):
    lax.fori_loop(0, count, lambda at, carry: (step(at), carry)[1], 0)


class RankSum:
    def __init__(self, place, rows, half, result, own, away, near, chip_sum, far, sems):
        self.place, self.result, self.sems = place, result, sems
        self.own, self.away, self.near, self.chip_sum, self.far = own, away, near, chip_sum, far
        self.part = rows // 8
        self.half = half
        self.columns = pl.ds(pl.multiple_of(place.core * half, half), half)
        self.rows = pl.ds(pl.multiple_of(place.chip * self.part, self.part), self.part)
        sibling = place.mp_peer(0, 1)
        self.cores = remote(away, near, sems, 0, sibling)
        self.scatter = []
        self.gather = []
        for bits in range(1, 8):
            other = pl.ds(pl.multiple_of(place.chip_peer(bits) * self.part, self.part), self.part)
            peer = place.mp_peer(bits)
            self.scatter.append(
                remote(chip_sum.at[:, other, :], far.at[bits - 1], sems, bits, peer)
            )
            mine = result.at[:, self.rows, self.columns]
            self.gather.append(remote(mine, mine, sems, 7 + bits, peer))
        whole = result.at[:, :, self.columns]
        self.back = remote(whole, whole, sems, 15, sibling)

    def set(self, which, own, away):
        self.own[which] = own
        self.away[which] = away.astype(BF)

    def start(self):
        self.cores.start()

    def step_chip(self):
        self.cores.wait()
        for which in range(2):
            self.chip_sum[which] = (self.own[which] + self.near[which].astype(F32)).astype(BF)
        for copy in self.scatter:
            copy.start()

    def step_sum(self):
        total = self.chip_sum[:, self.rows, :].astype(F32)
        for copy in self.scatter:
            copy.wait()
        for bits in range(7):
            total = total + self.far[bits].astype(F32)
        self.result[:, self.rows, self.columns] = total.astype(BF)
        for copy in self.gather:
            copy.start()

    def step_back(self):
        for copy in self.gather:
            copy.wait()
        self.back.start()

    def finish(self):
        self.back.wait()


class Spread:
    def __init__(self, place, held, sems):
        self.held, self.sems = held, sems
        self.blocked = len(held.shape) == 4
        self.rows = held.shape[-2] * (2 if self.blocked else 1) // CHUNKS
        self.one, self.two, self.three = place.level(1), place.level(2), place.mp_peer(3)
        self.four = place.level(4)
        self.direct = [
            remote(held.at[0], held.at[level], sems, at, peer)
            for at, (level, peer) in enumerate(((4, self.four), (1, self.one)))
        ]

    def piece(self, slot, chunk):
        if self.blocked:
            return self.held.at[slot, lax.div(chunk, 2), at_ds(lax.rem(chunk, 2), self.rows), :]
        return self.held.at[slot, at_ds(chunk, self.rows), :]

    def near(self, chunk):
        return remote(
            self.piece(0, chunk), self.piece(2, chunk), self.sems, 2 + chunk, self.two
        )

    def onward(self, chunk):
        return remote(
            self.piece(2, chunk), self.piece(3, chunk), self.sems, 2 + CHUNKS + chunk, self.three
        )

    def start_direct(self):
        for copy in self.direct:
            copy.start()

    def start_near(self, first, count):
        repeat(count, lambda at: self.near(first + at).start())

    def pass_on(self, chunk):
        chunk = jnp.int32(chunk)
        self.near(chunk).wait_recv()
        self.onward(chunk).start()

    def wait_direct(self):
        for copy in self.direct:
            copy.wait_recv()

    def wait_onward(self):
        repeat(CHUNKS, lambda chunk: self.onward(chunk).wait_recv())

    def close(self):
        for copy in self.direct:
            copy.wait_send()

        def finish(chunk):
            self.near(chunk).wait_send()
            self.onward(chunk).wait_send()

        repeat(CHUNKS, finish)


class Reduced:
    def __init__(self, place, grad, lead, first, second, third, sems, credit, at):
        self.credit, self.at, self.lead = credit, at, lead
        blocks = pl.ds(lead, first.shape[1])
        self.grad, self.bufs = grad, (first, second, third)
        rows = grad.shape[2]
        x0, x1 = place.x0, place.x1
        cross = x0 + x1 - 2 * x0 * x1
        near, back, far = place.dp_peer(1), place.dp_peer(3), place.dp_peer(4)
        self.greeted = (near, back)
        self.steps = [[] for _ in range(5)]
        self.kept = [[] for _ in range(3)]
        for h in range(2):
            keys = (cross, x1) if h == 0 else (x1, x0)
            peers = (near, back) if h == 0 else (back, near)
            offset, size = 0, rows
            for step in range(2):
                size = size // 2
                keep = pl.ds(pl.multiple_of(offset + keys[step] * size, size), size)
                send = pl.ds(pl.multiple_of(offset + (1 - keys[step]) * size, size), size)
                self.kept[step].append(keep)
                self.steps[step].append(
                    remote(
                        grad.at[h, blocks, send, :],
                        self.bufs[step].at[h],
                        sems,
                        (at, h, step),
                        peers[step],
                    )
                )
                own = grad.at[h, blocks, keep, :]
                self.steps[4 - step].append(
                    remote(own, own, sems, (at, h, 4 - step), peers[step])
                )
                offset = offset + keys[step] * size
            self.kept[2].append(self.kept[1][h])
            self.steps[2].append(
                remote(
                    grad.at[h, blocks, self.kept[1][h], :],
                    self.bufs[2].at[h],
                    sems,
                    (at, h, 2),
                    far,
                )
            )

    def start(self, step):
        if step == 3:
            pl.semaphore_wait(self.credit.at[self.at], 2)
        for copy in self.steps[step]:
            copy.start()

    def turn(self, step):
        self.wait(step)
        self.start(step + 1)

    def wait(self, step):
        for h, copy in enumerate(self.steps[step]):
            copy.wait()
            if step < 3:
                keep, buf = self.kept[step][h], self.bufs[step]

                def add(n):
                    self.grad[h, self.lead + n, keep, :] = (
                        self.grad[h, self.lead + n, keep, :].astype(F32) + buf[h, n].astype(F32)
                    ).astype(BF)

                repeat(buf.shape[1], add)
        if step == 1:
            for peer in self.greeted:
                pl.semaphore_signal(
                    self.credit.at[self.at],
                    inc=1,
                    device_id=peer,
                    device_id_type=pl.DeviceIdType.MESH,
                )


def layer_kernel(
    tokens,
    out_grad,
    w1,
    index1,
    index1_rows,
    w2,
    index2_sent,
    first_left,
    first_right,
    second_left,
    second_right,
    output,
    tokens_grad,
    g_w1,
    g_fl,
    g_fr,
    g_w2,
    g_sl,
    g_sr,
    tokens_all,
    grads_all,
    w2_all,
    index_all,
    index_smem,
    hidden,
    hidden_t,
    pre_grad,
    tokens_t,
    rank_first_t,
    slope,
    own,
    away,
    chip_sum,
    near_a,
    far_a,
    ranks_a,
    near_b,
    far_b,
    ranks_b,
    swap,
    sent,
    out_in,
    *rest,
):
    bufs, rest = rest[:21], rest[21:]
    (
        tok_send,
        tok_recv,
        grad_send,
        grad_recv,
        rank_send_a,
        rank_recv_a,
        rank_send_b,
        rank_recv_b,
        w_send,
        w_recv,
        i_send,
        i_recv,
        dp_send,
        dp_recv,
        credit,
        swap_send,
        swap_recv,
        x_send,
        x_recv,
        inbox_free,
        local,
    ) = rest
    place = Place()
    rows = pre_grad.shape[0]
    half = first_left.shape[1] // 2
    width = w1.shape[2]
    mine = pl.ds(pl.multiple_of(place.core * half, half), half)
    other = pl.ds(pl.multiple_of((1 - place.core) * half, half), half)

    loads = [
        pltpu.make_async_copy(
            tokens.at[:, pl.ds(d * width, width)], tokens_all.at[0, d], local.at[d]
        )
        for d in range(2)
    ]
    loads.append(pltpu.make_async_copy(out_grad, grads_all.at[0], local.at[2]))
    loads.append(pltpu.make_async_copy(w2.at[:, 0], w2_all.at[0], local.at[3]))
    loads.append(pltpu.make_async_copy(index2_sent.at[0], index_all.at[0], local.at[4]))
    for load in loads:
        load.start()
    greet(
        [place.mp_peer(bits) for bits in range(1, 8)]
        + [place.mp_peer(0, 1)]
        + [place.dp_peer(bits) for bits in (1, 3, 4)]
    )
    spread_tok = Spread(place, tokens_all, (tok_send, tok_recv))
    spread_grad = Spread(place, grads_all, (grad_send, grad_recv))
    sums_a = RankSum(
        place, rows, half, ranks_a, own, away, near_a, chip_sum, far_a, (rank_send_a, rank_recv_a)
    )
    sums_b = RankSum(
        place, rows, half, ranks_b, own, away, near_b, chip_sum, far_b, (rank_send_b, rank_recv_b)
    )
    w_copies = [
        remote(w2.at[:, level], w2_all.at[level], (w_send, w_recv), level - 1, place.level(level))
        for level in (4, 2, 3, 1)
    ]
    i_copies = [
        remote(
            index2_sent.at[level],
            index_all.at[level],
            (i_send, i_recv),
            level - 1,
            place.level(level),
        )
        for level in range(1, 5)
    ]
    dp_sems = (dp_send, dp_recv)
    grads = ((g_w2, 0), (g_sl, 0), (g_w1, 0), (g_w1, 5), (g_fr, 0), (g_sr, 0), (g_fl, 0))
    r_w2, r_sl, r_w1a, r_w1b, r_fr, r_sr, r_fl = [
        Reduced(place, grad, lead, *bufs[3 * at : 3 * at + 3], dp_sems, credit, at)
        for at, (grad, lead) in enumerate(grads)
    ]

    def turn_tokens(level):
        def step(d):
            tokens_t[level, d] = tokens_all[level, d].T

        repeat(2, step)

    for load in loads:
        load.wait()
    spread_tok.start_near(0, CHUNKS)
    spread_tok.start_direct()
    for copy in i_copies:
        copy.start()
    both = jnp.concatenate([tokens_all[0, 0], tokens_all[0, 1]], axis=1)
    sums_a.set(0, nn(both, first_left[:, mine]), nn(both, first_left[:, other]))
    flow = grads_all[0]
    sums_a.set(1, nt(flow, second_right[mine, :]), nt(flow, second_right[other, :]))
    sums_a.start()
    turn_tokens(0)
    spread_tok.pass_on(0)
    sums_a.step_chip()
    spread_tok.pass_on(1)
    spread_tok.pass_on(2)
    spread_grad.start_near(0, 2)
    spread_grad.start_direct()
    spread_tok.pass_on(3)
    spread_grad.start_near(2, 2)
    for copy in w_copies:
        copy.start()
    sums_a.step_sum()
    spread_tok.wait_direct()
    turn_tokens(1)
    turn_tokens(4)
    sums_a.step_back()
    turn_tokens(2)
    spread_grad.pass_on(0)
    spread_tok.wait_onward()
    turn_tokens(3)
    sums_a.finish()
    rank_first_t[...] = ranks_a[0].T

    def forward(f):
        columns = at_ds(f, width)
        picks = [tokens_all[level, index1[f, level]] for level in range(5)]
        pre = nn(jnp.concatenate(picks, axis=1), w1[f].reshape(5 * width, width))
        pre = pre + nn(ranks_a[0], first_right[:, columns])
        sigma = 1.0 / (1.0 + jnp.exp(-pre))
        active = (pre * sigma).astype(BF)
        hidden[f] = active
        hidden_t[f] = active.T
        slope[f] = sigma * (1.0 + pre * (1.0 - sigma))

    def forward_and_pass(f):
        forward(f)
        spread_grad.pass_on(f + 1)

    repeat(3, forward_and_pass)
    forward(jnp.int32(3))
    spread_tok.close()
    for peer in (place.level(1), place.level(2), place.mp_peer(3), place.level(4)):
        pl.semaphore_signal(inbox_free, inc=1, device_id=peer, device_id_type=pl.DeviceIdType.MESH)

    for copy in i_copies + w_copies:
        copy.wait()
    fetch = pltpu.make_async_copy(index_all, index_smem, local.at[0])
    fetch.start()
    fetch.wait()
    spread_grad.wait_direct()

    def second_left_part(d):
        g_sl[lax.div(d, 2), 0, at_ds(lax.rem(d, 2), width), :] = nn(hidden_t[d], ranks_a[1]).astype(BF)

    repeat(4, second_left_part)
    r_sl.start(0)

    def second_grads(at):
        level = at + lax.div(at, 3)
        for e in range(2):
            flow = grads_all[level, :, e * width : e * width + width]
            g_w2[e, level] = nn(hidden_t[index_smem[level, 0, e]], flow).astype(BF)

    repeat(4, second_grads)
    spread_grad.wait_onward()
    for e in range(2):
        flow = grads_all[3, :, e * width : e * width + width]
        g_w2[e, 3] = nn(hidden_t[index_smem[3, 0, e]], flow).astype(BF)
    r_w2.start(0)

    def hidden_back(d):
        total = nt(ranks_a[1], second_left[at_ds(d, width), :])
        for level in range(5):
            weights = [w2_all[level, e] for e in range(2)]
            tiles = [tile_of(index_all[level, 0:1, e : e + 1], d) for e in range(2)]
            total = total + nt(grads_all[level], masked(weights, tiles))
        pre_grad[:, at_ds(d, width)] = (total * slope[d]).astype(BF)

    repeat(4, hidden_back)
    spread_grad.close()
    r_sl.turn(0)
    r_w2.turn(0)

    units = jnp.concatenate([hidden[d] for d in range(4)], axis=1)
    sums_b.set(0, nn(units, second_left[:, mine]), nn(units, second_left[:, other]))
    sums_b.set(1, nt(pre_grad[...], first_right[mine, :]), nt(pre_grad[...], first_right[other, :]))
    sums_b.start()

    def first_grads(part):
        def step(h):
            f = 2 * h + part
            picks = [tokens_t[level, index1[f, level]] for level in range(5)]
            product = nn(
                jnp.concatenate(picks + [rank_first_t[...]], axis=0),
                pre_grad[:, at_ds(f, width)],
            ).astype(BF)
            for level in range(5):
                g_w1[h, part * 5 + level] = product[level * width : level * width + width]
            for r in range(2):
                low = (5 + r) * width
                g_fr[r, 0, :, at_ds(f, width)] = product[low : low + width]

        repeat(2, step)

    first_grads(0)
    r_w1a.start(0)
    sums_b.step_chip()
    first_grads(1)
    r_w1b.start(0)
    r_fr.start(0)
    r_sl.turn(1)
    r_w2.turn(1)

    def out_part(level, e):
        return nn(hidden[index_smem[level, 0, e]], w2_all[level, e])

    def tok_part(level, d):
        weights = [w1[f, level] for f in range(4)]
        tiles = [tile_of(index1_rows[level, 0:1, pl.ds(f, 1)], d) for f in range(4)]
        return nt(pre_grad[...], masked(weights, tiles))

    parts = (out_part, tok_part)

    def box(side, slot, block):
        return tokens_all.at[slot, block] if side else out_in.at[slot, block]

    def remote_part(side, level, peer):
        return remote(
            sent.at[level],
            tokens_all.at[level] if side else out_in.at[level],
            (x_send, x_recv),
            (side, level),
            peer,
        )

    peers = {1: place.level(1), 2: place.level(2), 3: place.mp_peer(3), 4: place.level(4)}
    copies = [
        {level: remote_part(side, level, peer) for level, peer in peers.items()}
        for side in range(2)
    ]

    def send_parts(side):
        for level in (3, 4, 1):
            if side:
                copies[0][level].wait_send()

            def step(block, level=level):
                sent[level, block] = parts[side](level, block).astype(BF)

            repeat(2, step)
            copies[side][level].start()

    def send_joined(side):
        copies[side][3].wait_recv()
        if side:
            copies[0][2].wait_send()

        def step(block):
            joined = parts[side](2, block) + box(side, 3, block)[...].astype(F32)
            sent[2, block] = joined.astype(BF)

        repeat(2, step)
        copies[side][2].start()

    def join(side, rank_part, result):
        for level in (1, 4, 2):
            copies[side][level].wait_recv()

        def step(block):
            total = parts[side](0, block) + rank_part(block)
            for level in (1, 4, 2):
                total = total + box(side, level, block)[...].astype(F32)
            result[:, at_ds(block, width)] = total.astype(BF)

        repeat(2, step)

    send_parts(0)
    r_w1a.turn(0)
    sums_b.step_sum()
    send_joined(0)
    pl.semaphore_wait(inbox_free, 4)
    r_sl.turn(2)
    r_w2.wait(2)
    quarter = r_w2.kept[2]
    swaps = [
        remote(
            g_w2.at[h, level, quarter[h], :],
            swap.at[h, level - 1],
            (swap_send, swap_recv),
            (h, level - 1),
            place.level(level),
        )
        for h in range(2)
        for level in range(1, 5)
    ]
    for copy in swaps:
        copy.start()
    send_parts(1)
    r_w1b.turn(0)
    sums_b.step_back()
    r_w1a.turn(1)
    r_fr.turn(0)
    for copy in swaps:
        copy.wait()
    for h in range(2):
        for level in range(1, 5):
            g_w2[h, level, quarter[h], :] = swap[h, level - 1]
    r_w2.start(3)
    sums_b.finish()
    rank_second_t = ranks_b[0].T
    for h in range(2):
        g_sr[h, 0] = nn(rank_second_t[h * 256 : h * 256 + 256, :], grads_all[0]).astype(BF)
        g_fl[h, 0] = nn(tokens_t[0, h], ranks_b[1]).astype(BF)
    r_sr.start(0)
    r_fl.start(0)
    r_w1b.turn(1)
    r_sl.turn(3)
    send_joined(1)
    r_fr.turn(1)
    r_w1a.turn(2)
    r_w2.turn(3)
    r_sr.turn(0)
    r_fl.turn(0)
    join(0, lambda e: nn(ranks_b[0], second_right[:, at_ds(e, width)]), output)
    r_w1b.turn(2)
    r_sr.turn(1)
    r_fl.turn(1)
    r_fr.turn(2)
    r_w1a.turn(3)
    join(1, lambda d: nt(ranks_b[1], first_left[at_ds(d, width), :]), tokens_grad)
    r_sr.turn(2)
    r_fl.turn(2)
    r_w1b.turn(3)
    r_fr.turn(3)
    r_sr.turn(3)
    r_fl.turn(3)
    for grad in (r_sl, r_w2, r_w1a, r_w1b, r_fr, r_sr, r_fl):
        grad.wait(4)
    for level in range(1, 5):
        copies[1][level].wait_send()


def copy_kernel(*refs):
    count = len(refs) // 2
    for at in range(count):
        refs[count + at][...] = refs[at][...]


def body(
    tokens,
    out_grad,
    first_blocks,
    first_index,
    second_blocks,
    second_index,
    first_left,
    first_right,
    second_left,
    second_right,
):
    rows, features = tokens.shape
    rank = first_left.shape[1]
    units = first_right.shape[1]
    width = first_blocks.shape[2]
    vmem = pl.BlockSpec(memory_space=pltpu.VMEM)
    smem = pl.BlockSpec(memory_space=pltpu.SMEM)
    anywhere = pl.BlockSpec(memory_space=pl.ANY)
    dma = pltpu.SemaphoreType.DMA

    def shape(*extent):
        return jax.ShapeDtypeStruct(extent, BF)

    half = rank // 2

    def rows_of(index):
        wide = 128 - index.shape[0]
        return jnp.pad(index.T[:, None, :], ((0, 0), (0, 7), (0, wide)))

    grads = [
        (2, 5, width, width),
        (2, 1, units // 2, rank),
        (2, 10, width, width),
        (2, 1, rank // 2, units),
        (2, 1, rank // 2, features),
        (2, 1, features // 2, rank),
    ]
    pieces = grads[:2] + [(2, 5, width, width)] * 2 + grads[3:]
    inboxes = []
    for two, count, tall, wide in pieces:
        for step in (2, 4, 4):
            inboxes.append(pltpu.VMEM((two, count, tall // step, wide), BF))
    scratch = [
        pltpu.VMEM((5, features // width, rows, width), BF),
        pltpu.VMEM((5, rows, features), BF),
        pltpu.VMEM((5, 2, width, width), BF),
        pltpu.VMEM((5, 8, 128), jnp.int32),
        pltpu.SMEM((5, 8, 128), jnp.int32),
        pltpu.VMEM((units // width, rows, width), BF),
        pltpu.VMEM((units // width, width, rows), BF),
        pltpu.VMEM((rows, units), BF),
        pltpu.VMEM((5, features // width, width, rows), BF),
        pltpu.VMEM((rank, rows), BF),
        pltpu.VMEM((units // width, rows, width), F32),
        pltpu.VMEM((2, rows, half), F32),
        pltpu.VMEM((2, rows, half), BF),
        pltpu.VMEM((2, rows, half), BF),
    ]
    for _ in range(2):
        scratch += [
            pltpu.VMEM((2, rows, half), BF),
            pltpu.VMEM((7, 2, rows // 8, half), BF),
            pltpu.VMEM((2, rows, rank), BF),
        ]
    scratch += [
        pltpu.VMEM((2, 4, width // 4, width), BF),
        pltpu.VMEM((5, features // width, rows, width), BF),
        pltpu.VMEM((5, features // width, rows, width), BF),
    ]
    semaphores = [dma((2 + 2 * CHUNKS,))] * 4 + [dma((16,))] * 4 + [dma((4,))] * 4
    semaphores += [dma((7, 2, 5))] * 2 + [pltpu.SemaphoreType.REGULAR((7,))]
    semaphores += [dma((2, 4))] * 2 + [dma((2, 5))] * 2
    semaphores += [pltpu.SemaphoreType.REGULAR, dma((5,))]
    order = (2, 5, 3, 0, 1, 4)
    results = pl.pallas_call(
        layer_kernel,
        out_shape=[shape(rows, features), shape(rows, features)]
        + [shape(*grads[at]) for at in order],
        in_specs=[anywhere, anywhere, vmem, smem, vmem, anywhere, anywhere] + [vmem] * 4,
        out_specs=[vmem] * 8,
        scratch_shapes=scratch + inboxes + semaphores,
        compiler_params=pltpu.CompilerParams(
            collective_id=0, has_side_effects=True, vmem_limit_bytes=63 * 2**20
        ),
        name="layer_kernel",
    )(
        tokens,
        out_grad,
        first_blocks,
        first_index,
        rows_of(first_index),
        second_blocks,
        rows_of(second_index),
        first_left,
        first_right,
        second_left,
        second_right,
    )
    flat = [result.reshape(-1, result.shape[-1]) for result in results]
    steps = 4
    specs = [
        pl.BlockSpec((result.shape[0] // steps, result.shape[1]), lambda at: (at, 0))
        for result in flat
    ]
    output, tokens_grad, g_w1, g_fl, g_fr, g_w2, g_sl, g_sr = pl.pallas_call(
        copy_kernel,
        out_shape=[shape(*result.shape) for result in flat],
        grid=(steps,),
        in_specs=specs,
        out_specs=specs,
        compiler_params=pltpu.CompilerParams(vmem_limit_bytes=32 * 2**20),
        name="copy_kernel",
    )(*flat)
    return (
        output,
        tokens_grad,
        g_w1.reshape(first_blocks.shape),
        g_fl.reshape(first_left.shape),
        g_fr.reshape(first_right.shape),
        g_w2.reshape(second_blocks.shape),
        g_sl.reshape(second_left.shape),
        g_sr.reshape(second_right.shape),
    )


def solution(mesh):
    placed = (
        P("dp", "mp"),
        P("dp", "mp"),
        P("mp", None, None, None),
        P("mp", None),
        P("mp", None, None, None),
        P("mp", None),
        P("mp", None),
        P(None, "mp"),
        P("mp", None),
        P(None, "mp"),
    )
    return jax.shard_map(
        body,
        mesh=mesh,
        in_specs=placed,
        out_specs=(
            P("dp", "mp"),
            P("dp", "mp"),
            P("mp", None, None, None),
            P("mp", None),
            P(None, "mp"),
            P("mp", None, None, None),
            P("mp", None),
            P(None, "mp"),
        ),
        check_vma=False,
    )
```

```python
import jax
import jax.numpy as jnp
from jax import lax
from jax.experimental import pallas as pl
from jax.experimental.pallas import tpu as pltpu
from jax.sharding import PartitionSpec as P

BF = jnp.bfloat16
F32 = jnp.float32
CHUNKS = 4


def nn(left, right):
    return jnp.dot(left, right, preferred_element_type=F32)


def nt(left, right):
    return lax.dot_general(left, right, (((1,), (1,)), ((), ())), preferred_element_type=F32)


def flip(bit, by):
    return 1 - bit if by else bit


def tile_of(index, at):
    hot = (index == at).astype(F32)
    return jnp.broadcast_to(hot, (16, 128)).astype(BF)


def masked(weights, tiles):
    parts = []
    for weight, tile in zip(weights, tiles):
        wide = jnp.concatenate([tile, tile], axis=1)
        tall = weight.reshape(weight.shape[0] // 16, 16, weight.shape[1])
        parts.append((tall * wide[None]).reshape(weight.shape))
    return jnp.concatenate(parts, axis=1)


class Place:
    def __init__(self):
        self.dp = lax.axis_index("dp")
        self.mp = lax.axis_index("mp")
        self.core = lax.rem(self.mp, 2)
        chip = lax.div(self.mp, 2)
        self.chip = chip
        self.y0 = lax.rem(chip, 2)
        self.y1 = lax.rem(lax.div(chip, 2), 2)
        self.z = lax.div(chip, 4)
        self.x0 = lax.rem(self.dp, 2)
        self.x1 = lax.rem(lax.div(self.dp, 2), 2)
        self.z_hi = lax.div(self.dp, 4)

    def mp_peer(self, chip_bits, core_bit=0):
        y0 = flip(self.y0, chip_bits & 1)
        y1 = flip(self.y1, chip_bits & 2)
        z = flip(self.z, chip_bits & 4)
        return (self.dp, ((z * 2 + y1) * 2 + y0) * 2 + flip(self.core, core_bit))

    def chip_peer(self, chip_bits):
        y0 = flip(self.y0, chip_bits & 1)
        y1 = flip(self.y1, chip_bits & 2)
        z = flip(self.z, chip_bits & 4)
        return (z * 2 + y1) * 2 + y0

    def dp_peer(self, bits):
        x0 = flip(self.x0, bits & 1)
        x1 = flip(self.x1, bits & 2)
        z = flip(self.z_hi, bits & 4)
        return ((z * 2 + x1) * 2 + x0, self.mp)

    def far_z(self):
        return (self.dp_peer(4)[0], self.mp_peer(4)[1])

    def level(self, level):
        return [None, self.mp_peer(0, 1), self.mp_peer(1), self.mp_peer(2), self.mp_peer(4)][level]


def greet(peers):
    barrier = pltpu.get_barrier_semaphore()
    for peer in peers:
        pl.semaphore_signal(barrier, inc=1, device_id=peer, device_id_type=pl.DeviceIdType.MESH)
    pl.semaphore_wait(barrier, len(peers))


def remote(src, dst, sems, at, peer):
    send, recv = sems
    return pltpu.make_async_remote_copy(
        src_ref=src,
        dst_ref=dst,
        send_sem=send.at[at],
        recv_sem=recv.at[at],
        device_id=peer,
        device_id_type=pl.DeviceIdType.MESH,
    )


def at_ds(index, size):
    return pl.ds(pl.multiple_of(index * size, size), size)


def repeat(count, step):
    lax.fori_loop(0, count, lambda at, carry: (step(at), carry)[1], 0)


class RankSum:
    def __init__(self, place, result, own, away, near, chip_sum, far, part, z_part, sems):
        self.result = result
        self.own, self.away, self.near, self.chip_sum, self.far = own, away, near, chip_sum, far
        self.part, self.z_part = part, z_part
        rows, half = near.shape[1], near.shape[2]
        step = rows // 4
        self.columns = at_ds(place.core, half)
        self.rows = at_ds(place.y1 * 2 + place.y0, step)
        sibling = place.mp_peer(0, 1)
        self.cores = remote(away, near, sems, 0, sibling)
        self.scatter = []
        self.gather = []
        mine = result.at[:, self.rows, self.columns]
        for bits in range(1, 4):
            other = at_ds(flip(place.y1, bits & 2) * 2 + flip(place.y0, bits & 1), step)
            peer = place.mp_peer(bits)
            self.scatter.append(
                remote(chip_sum.at[:, other, :], far.at[bits - 1], sems, bits, peer)
            )
            self.gather.append(remote(mine, mine, sems, 3 + bits, peer))
        self.across = remote(part, z_part, sems, 7, place.level(4))
        whole = result.at[:, :, self.columns]
        self.back = remote(whole, whole, sems, 8, sibling)

    def set(self, which, own, away):
        self.own[which] = own
        self.away[which] = away.astype(BF)

    def start(self):
        self.cores.start()

    def step_chip(self):
        self.cores.wait()

        def add(which):
            self.chip_sum[which] = (self.own[which] + self.near[which].astype(F32)).astype(BF)

        repeat(2, add)
        for copy in self.scatter:
            copy.start()

    def step_across(self):
        total = self.chip_sum[:, self.rows, :].astype(F32)
        for copy in self.scatter:
            copy.wait()
        for at in range(3):
            total = total + self.far[at].astype(F32)
        self.part[...] = total.astype(BF)
        self.across.start()

    def step_sum(self):
        self.across.wait()
        total = self.part[...].astype(F32) + self.z_part[...].astype(F32)
        self.result[:, self.rows, self.columns] = total.astype(BF)
        for copy in self.gather:
            copy.start()

    def step_back(self):
        for copy in self.gather:
            copy.wait()
        self.back.start()

    def finish(self):
        self.back.wait()


class Spread:
    def __init__(self, place, held, sems):
        self.held, self.sems = held, sems
        self.blocked = len(held.shape) == 4
        self.rows = held.shape[-2] * (2 if self.blocked else 1) // CHUNKS
        self.one, self.two, self.three = place.level(1), place.level(2), place.mp_peer(3)
        self.four = place.level(4)
        self.direct = [
            remote(held.at[0], held.at[level], sems, at, peer)
            for at, (level, peer) in enumerate(((4, self.four), (1, self.one)))
        ]

    def piece(self, slot, chunk):
        if self.blocked:
            return self.held.at[slot, lax.div(chunk, 2), at_ds(lax.rem(chunk, 2), self.rows), :]
        return self.held.at[slot, at_ds(chunk, self.rows), :]

    def near(self, chunk):
        return remote(
            self.piece(0, chunk), self.piece(2, chunk), self.sems, 2 + chunk, self.two
        )

    def onward(self, chunk):
        return remote(
            self.piece(2, chunk), self.piece(3, chunk), self.sems, 2 + CHUNKS + chunk, self.three
        )

    def start_direct(self):
        for copy in self.direct:
            copy.start()

    def start_near(self, first, count):
        repeat(count, lambda at: self.near(first + at).start())

    def pass_on(self, chunk):
        chunk = jnp.int32(chunk)
        self.near(chunk).wait_recv()
        self.onward(chunk).start()

    def wait_direct(self):
        for copy in self.direct:
            copy.wait_recv()

    def wait_onward(self):
        repeat(CHUNKS, lambda chunk: self.onward(chunk).wait_recv())

    def close(self):
        for copy in self.direct:
            copy.wait_send()

        def finish(chunk):
            self.near(chunk).wait_send()
            self.onward(chunk).wait_send()

        repeat(CHUNKS, finish)


class Reduced:
    def __init__(self, place, grad, lead, first, second, third, relay, sems, credit, at):
        self.credit, self.at, self.lead = credit, at, lead
        blocks = pl.ds(lead, first.shape[1])
        self.grad, self.bufs = grad, (first, second, third)
        rows = grad.shape[2]
        x0, x1 = place.x0, place.x1
        cross = x0 + x1 - 2 * x0 * x1
        near, back = place.dp_peer(1), place.dp_peer(3)
        by_z = (place.level(4), place.far_z())
        self.passed = []
        self.greeted = (near, back)
        self.steps = [[] for _ in range(5)]
        self.kept = [[] for _ in range(3)]
        for h in range(2):
            keys = (cross, x1) if h == 0 else (x1, x0)
            peers = (near, back) if h == 0 else (back, near)
            offset, size = 0, rows
            for step in range(2):
                size = size // 2
                keep = pl.ds(pl.multiple_of(offset + keys[step] * size, size), size)
                send = pl.ds(pl.multiple_of(offset + (1 - keys[step]) * size, size), size)
                self.kept[step].append(keep)
                self.steps[step].append(
                    remote(
                        grad.at[h, blocks, send, :],
                        self.bufs[step].at[h],
                        sems,
                        (at, h, step),
                        peers[step],
                    )
                )
                own = grad.at[h, blocks, keep, :]
                self.steps[4 - step].append(
                    remote(own, own, sems, (at, h, 4 - step), peers[step])
                )
                offset = offset + keys[step] * size
            self.kept[2].append(self.kept[1][h])
            self.steps[2].append(
                remote(
                    grad.at[h, blocks, self.kept[1][h], :], relay.at[h], sems, (at, h, 2), by_z[h]
                )
            )
            self.passed.append(
                remote(relay.at[h], self.bufs[2].at[h], sems, (at, h, 5), by_z[1 - h])
            )

    def start(self, step):
        if step == 3:
            pl.semaphore_wait(self.credit.at[self.at], 2)
        for copy in self.steps[step]:
            copy.start()

    def turn(self, step):
        self.wait(step)
        self.start(step + 1)

    def relay(self):
        for copy, onward in zip(self.steps[2], self.passed):
            copy.wait_recv()
            onward.start()

    def wait(self, step):
        for h, copy in enumerate(self.steps[step]):
            if step == 2:
                copy.wait_send()
                self.passed[h].wait()
            else:
                copy.wait()
            if step < 3:
                keep, buf = self.kept[step][h], self.bufs[step]

                def add(n):
                    self.grad[h, self.lead + n, keep, :] = (
                        self.grad[h, self.lead + n, keep, :].astype(F32) + buf[h, n].astype(F32)
                    ).astype(BF)

                repeat(buf.shape[1], add)
        if step == 1:
            for peer in self.greeted:
                pl.semaphore_signal(
                    self.credit.at[self.at],
                    inc=1,
                    device_id=peer,
                    device_id_type=pl.DeviceIdType.MESH,
                )


def layer_kernel(
    tokens,
    out_grad,
    w1,
    index1,
    w2,
    table,
    first_left,
    first_right,
    second_left,
    second_right,
    output,
    tokens_grad,
    g_w1,
    g_fl,
    g_fr,
    g_w2,
    g_sl,
    g_sr,
    tokens_all,
    grads_all,
    w2_all,
    index_all,
    index_smem,
    hidden,
    hidden_t,
    pre_grad,
    tokens_t,
    rank_first_t,
    slope,
    own,
    away,
    chip_sum,
    part,
    near_a,
    far_a,
    z_a,
    ranks_a,
    near_b,
    far_b,
    z_b,
    ranks_b,
    swap,
    sent,
    out_in,
    *rest,
):
    bufs, rest = rest[:28], rest[28:]
    (
        tok_send,
        tok_recv,
        grad_send,
        grad_recv,
        rank_send_a,
        rank_recv_a,
        rank_send_b,
        rank_recv_b,
        w_send,
        w_recv,
        i_send,
        i_recv,
        dp_send,
        dp_recv,
        credit,
        swap_send,
        swap_recv,
        x_send,
        x_recv,
        inbox_free,
        local,
    ) = rest
    place = Place()
    rows = pre_grad.shape[0]
    half = first_left.shape[1] // 2
    width = w1.shape[2]
    mine = pl.ds(pl.multiple_of(place.core * half, half), half)
    other = pl.ds(pl.multiple_of((1 - place.core) * half, half), half)

    loads = [
        pltpu.make_async_copy(
            tokens.at[:, pl.ds(d * width, width)], tokens_all.at[0, d], local.at[d]
        )
        for d in range(2)
    ]
    loads.append(pltpu.make_async_copy(out_grad, grads_all.at[0], local.at[2]))
    loads.append(pltpu.make_async_copy(w2.at[:, 0], w2_all.at[0], local.at[3]))
    loads.append(pltpu.make_async_copy(table, index_all.at[0], local.at[4]))
    for load in loads:
        load.start()
    greet(
        [place.mp_peer(bits) for bits in range(1, 8)]
        + [place.mp_peer(0, 1)]
        + [place.dp_peer(1), place.dp_peer(3), place.far_z()]
    )
    spread_tok = Spread(place, tokens_all, (tok_send, tok_recv))
    spread_grad = Spread(place, grads_all, (grad_send, grad_recv))
    sums_a = RankSum(
        place, ranks_a, own, away, near_a, chip_sum, far_a, part, z_a, (rank_send_a, rank_recv_a)
    )
    sums_b = RankSum(
        place, ranks_b, own, away, near_b, chip_sum, far_b, part, z_b, (rank_send_b, rank_recv_b)
    )
    w_copies = [
        remote(w2.at[:, level], w2_all.at[level], (w_send, w_recv), level - 1, place.level(level))
        for level in (4, 2, 3, 1)
    ]
    i_copies = [
        remote(
            table,
            index_all.at[level],
            (i_send, i_recv),
            level - 1,
            place.level(level),
        )
        for level in range(1, 5)
    ]
    dp_sems = (dp_send, dp_recv)
    grads = ((g_w2, 0), (g_sl, 0), (g_w1, 0), (g_w1, 5), (g_fr, 0), (g_sr, 0), (g_fl, 0))
    r_w2, r_sl, r_w1a, r_w1b, r_fr, r_sr, r_fl = [
        Reduced(place, grad, lead, *bufs[4 * at : 4 * at + 4], dp_sems, credit, at)
        for at, (grad, lead) in enumerate(grads)
    ]

    def turn_tokens(level):
        def step(d):
            tokens_t[level, d] = tokens_all[level, d].T

        repeat(2, step)

    for load in loads:
        load.wait()
    spread_tok.start_near(0, CHUNKS)
    spread_tok.start_direct()
    for copy in i_copies:
        copy.start()
    both = jnp.concatenate([tokens_all[0, 0], tokens_all[0, 1]], axis=1)
    sums_a.set(0, nn(both, first_left[:, mine]), nn(both, first_left[:, other]))
    flow = grads_all[0]
    sums_a.set(1, nt(flow, second_right[mine, :]), nt(flow, second_right[other, :]))
    sums_a.start()
    turn_tokens(0)
    spread_tok.pass_on(0)
    sums_a.step_chip()
    spread_tok.pass_on(1)
    spread_tok.pass_on(2)
    spread_grad.start_near(0, 2)
    spread_grad.start_direct()
    spread_tok.pass_on(3)
    spread_grad.start_near(2, 2)
    for copy in w_copies:
        copy.start()
    sums_a.step_across()
    spread_tok.wait_direct()
    turn_tokens(1)
    sums_a.step_sum()
    turn_tokens(4)
    turn_tokens(2)
    sums_a.step_back()
    spread_grad.pass_on(0)
    spread_tok.wait_onward()
    turn_tokens(3)
    sums_a.finish()
    rank_first_t[...] = ranks_a[0].T

    def forward(f):
        columns = at_ds(f, width)
        picks = [tokens_all[level, index1[f, level]] for level in range(5)]
        pre = nn(jnp.concatenate(picks, axis=1), w1[f].reshape(5 * width, width))
        pre = pre + nn(ranks_a[0], first_right[:, columns])
        sigma = 1.0 / (1.0 + jnp.exp(-pre))
        active = (pre * sigma).astype(BF)
        hidden[f] = active
        hidden_t[f] = active.T
        slope[f] = sigma * (1.0 + pre * (1.0 - sigma))

    def forward_and_pass(f):
        forward(f)
        spread_grad.pass_on(f + 1)

    repeat(3, forward_and_pass)
    forward(jnp.int32(3))
    spread_tok.close()
    for peer in (place.level(1), place.level(2), place.mp_peer(3), place.level(4)):
        pl.semaphore_signal(inbox_free, inc=1, device_id=peer, device_id_type=pl.DeviceIdType.MESH)

    for copy in i_copies + w_copies:
        copy.wait()
    fetch = pltpu.make_async_copy(index_all, index_smem, local.at[0])
    fetch.start()
    fetch.wait()
    spread_grad.wait_direct()

    def second_left_part(d):
        g_sl[lax.div(d, 2), 0, at_ds(lax.rem(d, 2), width), :] = nn(hidden_t[d], ranks_a[1]).astype(BF)

    repeat(4, second_left_part)
    r_sl.start(0)

    def second_grads(at):
        level = at + lax.div(at, 3)
        for e in range(2):
            flow = grads_all[level, :, e * width : e * width + width]
            g_w2[e, level] = nn(hidden_t[index_smem[level, 4 + e, level]], flow).astype(BF)

    repeat(4, second_grads)
    spread_grad.wait_onward()
    for e in range(2):
        flow = grads_all[3, :, e * width : e * width + width]
        g_w2[e, 3] = nn(hidden_t[index_smem[3, 4 + e, 3]], flow).astype(BF)
    r_w2.start(0)

    def hidden_back(d):
        total = nt(ranks_a[1], second_left[at_ds(d, width), :])
        for level in range(5):
            weights = [w2_all[level, e] for e in range(2)]
            tiles = [tile_of(index_all[level, 4 + e : 5 + e, level : level + 1], d) for e in range(2)]
            total = total + nt(grads_all[level], masked(weights, tiles))
        pre_grad[:, at_ds(d, width)] = (total * slope[d]).astype(BF)

    repeat(4, hidden_back)
    spread_grad.close()
    r_sl.turn(0)
    r_w2.turn(0)

    units = jnp.concatenate([hidden[d] for d in range(4)], axis=1)
    sums_b.set(0, nn(units, second_left[:, mine]), nn(units, second_left[:, other]))
    sums_b.set(1, nt(pre_grad[...], first_right[mine, :]), nt(pre_grad[...], first_right[other, :]))
    sums_b.start()

    def first_grads(part):
        def step(h):
            f = 2 * h + part
            picks = [tokens_t[level, index1[f, level]] for level in range(5)]
            product = nn(
                jnp.concatenate(picks + [rank_first_t[...]], axis=0),
                pre_grad[:, at_ds(f, width)],
            ).astype(BF)
            for level in range(5):
                g_w1[h, part * 5 + level] = product[level * width : level * width + width]
            for r in range(2):
                low = (5 + r) * width
                g_fr[r, 0, :, at_ds(f, width)] = product[low : low + width]

        repeat(2, step)

    first_grads(0)
    r_w1a.start(0)
    sums_b.step_chip()
    first_grads(1)
    r_w1b.start(0)
    r_fr.start(0)
    r_sl.turn(1)
    r_w2.turn(1)

    def out_part(level, e):
        return nn(hidden[index_smem[level, 4 + e, level]], w2_all[level, e])

    def tok_part(level, d):
        weights = [w1[f, level] for f in range(4)]
        tiles = [tile_of(table[f : f + 1, level : level + 1], d) for f in range(4)]
        return nt(pre_grad[...], masked(weights, tiles))

    parts = (out_part, tok_part)

    def box(side, slot, block):
        return tokens_all.at[slot, block] if side else out_in.at[slot - 1, block]

    def remote_part(side, level, peer):
        return remote(
            sent.at[level - 1],
            tokens_all.at[level] if side else out_in.at[level - 1],
            (x_send, x_recv),
            (side, level),
            peer,
        )

    peers = {1: place.level(1), 2: place.level(2), 3: place.mp_peer(3), 4: place.level(4)}
    copies = [
        {level: remote_part(side, level, peer) for level, peer in peers.items()}
        for side in range(2)
    ]

    def send_parts(side):
        for level in (3, 4, 1):
            if side:
                copies[0][level].wait_send()

            def step(block, level=level):
                sent[level - 1, block] = parts[side](level, block).astype(BF)

            repeat(2, step)
            copies[side][level].start()

    def send_joined(side):
        copies[side][3].wait_recv()
        if side:
            copies[0][2].wait_send()

        def step(block):
            joined = parts[side](2, block) + box(side, 3, block)[...].astype(F32)
            sent[1, block] = joined.astype(BF)

        repeat(2, step)
        copies[side][2].start()

    def join(side, rank_part, result):
        for level in (1, 4, 2):
            copies[side][level].wait_recv()

        def step(block):
            total = parts[side](0, block) + rank_part(block)
            for level in (1, 4, 2):
                total = total + box(side, level, block)[...].astype(F32)
            result[:, at_ds(block, width)] = total.astype(BF)

        repeat(2, step)

    send_parts(0)
    r_w1a.turn(0)
    sums_b.step_across()
    r_sl.relay()
    r_w2.relay()
    send_joined(0)
    pl.semaphore_wait(inbox_free, 4)
    r_w1b.turn(0)
    r_sl.turn(2)
    r_w2.wait(2)
    quarter = r_w2.kept[2]
    swaps = [
        remote(
            g_w2.at[h, level, quarter[h], :],
            swap.at[h, level - 1],
            (swap_send, swap_recv),
            (h, level - 1),
            place.level(level),
        )
        for h in range(2)
        for level in range(1, 5)
    ]
    for copy in swaps:
        copy.start()
    sums_b.step_sum()
    send_parts(1)
    r_w1a.turn(1)
    r_fr.turn(0)
    sums_b.step_back()
    for copy in swaps:
        copy.wait()
    for h in range(2):
        for level in range(1, 5):
            g_w2[h, level, quarter[h], :] = swap[h, level - 1]
    r_w2.start(3)
    r_w1b.turn(1)
    r_w1a.relay()
    sums_b.finish()
    rank_second_t = ranks_b[0].T
    for h in range(2):
        g_sr[h, 0] = nn(rank_second_t[h * 256 : h * 256 + 256, :], grads_all[0]).astype(BF)
        g_fl[h, 0] = nn(tokens_t[0, h], ranks_b[1]).astype(BF)
    r_sr.start(0)
    r_fl.start(0)
    r_fr.turn(1)
    r_sl.turn(3)
    r_w1b.relay()
    send_joined(1)
    r_w1a.turn(2)
    r_w2.turn(3)
    r_fr.relay()
    r_sr.turn(0)
    r_fl.turn(0)
    join(0, lambda e: nn(ranks_b[0], second_right[:, at_ds(e, width)]), output)
    r_w1b.turn(2)
    r_sr.turn(1)
    r_fl.turn(1)
    r_fr.turn(2)
    r_w1a.turn(3)
    r_sr.relay()
    r_fl.relay()
    join(1, lambda d: nt(ranks_b[1], first_left[at_ds(d, width), :]), tokens_grad)
    r_sr.turn(2)
    r_fl.turn(2)
    r_w1b.turn(3)
    r_fr.turn(3)
    r_sr.turn(3)
    r_fl.turn(3)
    for grad in (r_sl, r_w2, r_w1a, r_w1b, r_fr, r_sr, r_fl):
        grad.wait(4)
    for level in range(1, 5):
        copies[1][level].wait_send()


def copy_kernel(*refs):
    count = len(refs) // 2
    for at in range(count):
        refs[count + at][...] = refs[at][...]


def body(
    tokens,
    out_grad,
    first_blocks,
    first_index,
    second_blocks,
    second_index,
    first_left,
    first_right,
    second_left,
    second_right,
):
    rows, features = tokens.shape
    rank = first_left.shape[1]
    units = first_right.shape[1]
    width = first_blocks.shape[2]
    vmem = pl.BlockSpec(memory_space=pltpu.VMEM)
    smem = pl.BlockSpec(memory_space=pltpu.SMEM)
    anywhere = pl.BlockSpec(memory_space=pl.ANY)
    dma = pltpu.SemaphoreType.DMA

    def shape(*extent):
        return jax.ShapeDtypeStruct(extent, BF)

    half = rank // 2

    table = jnp.concatenate([first_index, second_index], axis=0)
    table = jnp.pad(table, ((0, 8 - table.shape[0]), (0, 128 - table.shape[1])))

    grads = [
        (2, 5, width, width),
        (2, 1, units // 2, rank),
        (2, 10, width, width),
        (2, 1, rank // 2, units),
        (2, 1, rank // 2, features),
        (2, 1, features // 2, rank),
    ]
    pieces = grads[:2] + [(2, 5, width, width)] * 2 + grads[3:]
    inboxes = []
    for two, count, tall, wide in pieces:
        for step in (2, 4, 4, 4):
            inboxes.append(pltpu.VMEM((two, count, tall // step, wide), BF))
    scratch = [
        pltpu.VMEM((5, features // width, rows, width), BF),
        pltpu.VMEM((5, rows, features), BF),
        pltpu.VMEM((5, 2, width, width), BF),
        pltpu.VMEM((5, 8, 128), jnp.int32),
        pltpu.SMEM((5, 8, 128), jnp.int32),
        pltpu.VMEM((units // width, rows, width), BF),
        pltpu.VMEM((units // width, width, rows), BF),
        pltpu.VMEM((rows, units), BF),
        pltpu.VMEM((5, features // width, width, rows), BF),
        pltpu.VMEM((rank, rows), BF),
        pltpu.VMEM((units // width, rows, width), F32),
        pltpu.VMEM((2, rows, half), F32),
        pltpu.VMEM((2, rows, half), BF),
        pltpu.VMEM((2, rows, half), BF),
        pltpu.VMEM((2, rows // 4, half), BF),
    ]
    for _ in range(2):
        scratch += [
            pltpu.VMEM((2, rows, half), BF),
            pltpu.VMEM((3, 2, rows // 4, half), BF),
            pltpu.VMEM((2, rows // 4, half), BF),
            pltpu.VMEM((2, rows, rank), BF),
        ]
    scratch += [
        pltpu.VMEM((2, 4, width // 4, width), BF),
        pltpu.VMEM((4, features // width, rows, width), BF),
        pltpu.VMEM((4, features // width, rows, width), BF),
    ]
    semaphores = [dma((2 + 2 * CHUNKS,))] * 4 + [dma((16,))] * 4 + [dma((4,))] * 4
    semaphores += [dma((7, 2, 6))] * 2 + [pltpu.SemaphoreType.REGULAR((7,))]
    semaphores += [dma((2, 4))] * 2 + [dma((2, 5))] * 2
    semaphores += [pltpu.SemaphoreType.REGULAR, dma((5,))]
    order = (2, 5, 3, 0, 1, 4)
    results = pl.pallas_call(
        layer_kernel,
        out_shape=[shape(rows, features), shape(rows, features)]
        + [shape(*grads[at]) for at in order],
        in_specs=[anywhere, anywhere, vmem, smem, anywhere, vmem] + [vmem] * 4,
        out_specs=[vmem] * 8,
        scratch_shapes=scratch + inboxes + semaphores,
        compiler_params=pltpu.CompilerParams(
            collective_id=0, has_side_effects=True, vmem_limit_bytes=63 * 2**20
        ),
        name="layer_kernel",
    )(
        tokens,
        out_grad,
        first_blocks,
        first_index,
        second_blocks,
        table,
        first_left,
        first_right,
        second_left,
        second_right,
    )
    flat = [result.reshape(-1, result.shape[-1]) for result in results]
    steps = 4
    specs = [
        pl.BlockSpec((result.shape[0] // steps, result.shape[1]), lambda at: (at, 0))
        for result in flat
    ]
    output, tokens_grad, g_w1, g_fl, g_fr, g_w2, g_sl, g_sr = pl.pallas_call(
        copy_kernel,
        out_shape=[shape(*result.shape) for result in flat],
        grid=(steps,),
        in_specs=specs,
        out_specs=specs,
        compiler_params=pltpu.CompilerParams(vmem_limit_bytes=63 * 2**20),
        name="copy_kernel",
    )(*flat)
    return (
        output,
        tokens_grad,
        g_w1.reshape(first_blocks.shape),
        g_fl.reshape(first_left.shape),
        g_fr.reshape(first_right.shape),
        g_w2.reshape(second_blocks.shape),
        g_sl.reshape(second_left.shape),
        g_sr.reshape(second_right.shape),
    )


def solution(mesh):
    placed = (
        P("dp", "mp"),
        P("dp", "mp"),
        P("mp", None, None, None),
        P("mp", None),
        P("mp", None, None, None),
        P("mp", None),
        P("mp", None),
        P(None, "mp"),
        P("mp", None),
        P(None, "mp"),
    )
    return jax.shard_map(
        body,
        mesh=mesh,
        in_specs=placed,
        out_specs=(
            P("dp", "mp"),
            P("dp", "mp"),
            P("mp", None, None, None),
            P("mp", None),
            P(None, "mp"),
            P("mp", None, None, None),
            P("mp", None),
            P(None, "mp"),
        ),
        check_vma=False,
    )
```

```python
import jax
import jax.numpy as jnp
from jax import lax
from jax.experimental import pallas as pl
from jax.experimental.pallas import tpu as pltpu
from jax.sharding import PartitionSpec as P

BF = jnp.bfloat16
F32 = jnp.float32
CHUNKS = 4


def nn(left, right):
    return jnp.dot(left, right, preferred_element_type=F32)


def nt(left, right):
    return lax.dot_general(left, right, (((1,), (1,)), ((), ())), preferred_element_type=F32)


def flip(bit, by):
    return 1 - bit if by else bit


def tile_of(index, at):
    hot = (index == at).astype(F32)
    return jnp.broadcast_to(hot, (16, 128)).astype(BF)


def masked(weights, tiles):
    parts = []
    for weight, tile in zip(weights, tiles):
        wide = jnp.concatenate([tile, tile], axis=1)
        tall = weight.reshape(weight.shape[0] // 16, 16, weight.shape[1])
        parts.append((tall * wide[None]).reshape(weight.shape))
    return jnp.concatenate(parts, axis=1)


class Place:
    def __init__(self):
        self.dp = lax.axis_index("dp")
        self.mp = lax.axis_index("mp")
        self.core = lax.rem(self.mp, 2)
        chip = lax.div(self.mp, 2)
        self.chip = chip
        self.y0 = lax.rem(chip, 2)
        self.y1 = lax.rem(lax.div(chip, 2), 2)
        self.z = lax.div(chip, 4)
        self.x0 = lax.rem(self.dp, 2)
        self.x1 = lax.rem(lax.div(self.dp, 2), 2)
        self.z_hi = lax.div(self.dp, 4)

    def mp_peer(self, chip_bits, core_bit=0):
        y0 = flip(self.y0, chip_bits & 1)
        y1 = flip(self.y1, chip_bits & 2)
        z = flip(self.z, chip_bits & 4)
        return (self.dp, ((z * 2 + y1) * 2 + y0) * 2 + flip(self.core, core_bit))

    def chip_peer(self, chip_bits):
        y0 = flip(self.y0, chip_bits & 1)
        y1 = flip(self.y1, chip_bits & 2)
        z = flip(self.z, chip_bits & 4)
        return (z * 2 + y1) * 2 + y0

    def dp_peer(self, bits):
        x0 = flip(self.x0, bits & 1)
        x1 = flip(self.x1, bits & 2)
        z = flip(self.z_hi, bits & 4)
        return ((z * 2 + x1) * 2 + x0, self.mp)

    def far_z(self):
        return (self.dp_peer(4)[0], self.mp_peer(4)[1])

    def level(self, level):
        return [None, self.mp_peer(0, 1), self.mp_peer(1), self.mp_peer(2), self.mp_peer(4)][level]


def greet(peers):
    barrier = pltpu.get_barrier_semaphore()
    for peer in peers:
        pl.semaphore_signal(barrier, inc=1, device_id=peer, device_id_type=pl.DeviceIdType.MESH)
    pl.semaphore_wait(barrier, len(peers))


def remote(src, dst, sems, at, peer):
    send, recv = sems
    return pltpu.make_async_remote_copy(
        src_ref=src,
        dst_ref=dst,
        send_sem=send.at[at],
        recv_sem=recv.at[at],
        device_id=peer,
        device_id_type=pl.DeviceIdType.MESH,
    )


def at_ds(index, size):
    return pl.ds(pl.multiple_of(index * size, size), size)


def repeat(count, step):
    lax.fori_loop(0, count, lambda at, carry: (step(at), carry)[1], 0)


class RankSum:
    def __init__(self, place, result, own, away, near, chip_sum, far, part, z_part, sems):
        self.result = result
        self.own, self.away, self.near, self.chip_sum, self.far = own, away, near, chip_sum, far
        self.part, self.z_part = part, z_part
        rows, half = near.shape[1], near.shape[2]
        step = rows // 4
        self.columns = at_ds(place.core, half)
        self.rows = at_ds(place.y1 * 2 + place.y0, step)
        sibling = place.mp_peer(0, 1)
        self.cores = remote(away, near, sems, 0, sibling)
        self.scatter = []
        self.gather = []
        mine = result.at[:, self.rows, self.columns]
        for bits in range(1, 4):
            other = at_ds(flip(place.y1, bits & 2) * 2 + flip(place.y0, bits & 1), step)
            peer = place.mp_peer(bits)
            self.scatter.append(
                remote(chip_sum.at[:, other, :], far.at[bits - 1], sems, bits, peer)
            )
            self.gather.append(remote(mine, mine, sems, 3 + bits, peer))
        self.across = remote(part, z_part, sems, 7, place.level(4))
        whole = result.at[:, :, self.columns]
        self.back = remote(whole, whole, sems, 8, sibling)

    def set(self, which, own, away):
        self.own[which] = own
        self.away[which] = away.astype(BF)

    def start(self):
        self.cores.start()

    def step_chip(self):
        self.cores.wait()

        def add(which):
            self.chip_sum[which] = (self.own[which] + self.near[which].astype(F32)).astype(BF)

        repeat(2, add)
        for copy in self.scatter:
            copy.start()

    def step_across(self):
        total = self.chip_sum[:, self.rows, :].astype(F32)
        for copy in self.scatter:
            copy.wait()
        for at in range(3):
            total = total + self.far[at].astype(F32)
        self.part[...] = total.astype(BF)
        self.across.start()

    def step_sum(self):
        self.across.wait()
        total = self.part[...].astype(F32) + self.z_part[...].astype(F32)
        self.result[:, self.rows, self.columns] = total.astype(BF)
        for copy in self.gather:
            copy.start()

    def step_back(self):
        for copy in self.gather:
            copy.wait()
        self.back.start()

    def finish(self):
        self.back.wait()


class Spread:
    def __init__(self, place, held, sems):
        self.held, self.sems = held, sems
        self.blocked = len(held.shape) == 4
        self.rows = held.shape[-2] * (2 if self.blocked else 1) // CHUNKS
        self.one, self.two, self.three = place.level(1), place.level(2), place.mp_peer(3)
        self.four = place.level(4)
        self.direct = [
            remote(held.at[0], held.at[level], sems, at, peer)
            for at, (level, peer) in enumerate(((4, self.four), (1, self.one)))
        ]

    def piece(self, slot, chunk):
        if self.blocked:
            return self.held.at[slot, lax.div(chunk, 2), at_ds(lax.rem(chunk, 2), self.rows), :]
        return self.held.at[slot, at_ds(chunk, self.rows), :]

    def near(self, chunk):
        return remote(
            self.piece(0, chunk), self.piece(2, chunk), self.sems, 2 + chunk, self.two
        )

    def onward(self, chunk):
        return remote(
            self.piece(2, chunk), self.piece(3, chunk), self.sems, 2 + CHUNKS + chunk, self.three
        )

    def start_direct(self):
        for copy in self.direct:
            copy.start()

    def start_near(self, first, count):
        repeat(count, lambda at: self.near(first + at).start())

    def pass_on(self, chunk):
        chunk = jnp.int32(chunk)
        self.near(chunk).wait_recv()
        self.onward(chunk).start()

    def wait_slot(self, level):
        self.direct[0 if level == 4 else 1].wait_recv()

    def wait_onward(self):
        repeat(CHUNKS, lambda chunk: self.onward(chunk).wait_recv())

    def close(self):
        for copy in self.direct:
            copy.wait_send()

        def finish(chunk):
            self.near(chunk).wait_send()
            self.onward(chunk).wait_send()

        repeat(CHUNKS, finish)


class Reduced:
    def __init__(self, place, grad, lead, first, second, third, relay, sems, credit, at):
        self.credit, self.at, self.lead = credit, at, lead
        blocks = pl.ds(lead, first.shape[1])
        self.grad, self.bufs = grad, (first, second, third)
        rows = grad.shape[2]
        x0, x1 = place.x0, place.x1
        cross = x0 + x1 - 2 * x0 * x1
        near, back = place.dp_peer(1), place.dp_peer(3)
        by_z = (place.level(4), place.far_z())
        self.passed = []
        self.greeted = (near, back)
        self.steps = [[] for _ in range(5)]
        self.kept = [[] for _ in range(3)]
        for h in range(2):
            keys = (cross, x1) if h == 0 else (x1, x0)
            peers = (near, back) if h == 0 else (back, near)
            offset, size = 0, rows
            for step in range(2):
                size = size // 2
                keep = pl.ds(pl.multiple_of(offset + keys[step] * size, size), size)
                send = pl.ds(pl.multiple_of(offset + (1 - keys[step]) * size, size), size)
                self.kept[step].append(keep)
                self.steps[step].append(
                    remote(
                        grad.at[h, blocks, send, :],
                        self.bufs[step].at[h],
                        sems,
                        (at, h, step),
                        peers[step],
                    )
                )
                own = grad.at[h, blocks, keep, :]
                self.steps[4 - step].append(
                    remote(own, own, sems, (at, h, 4 - step), peers[step])
                )
                offset = offset + keys[step] * size
            self.kept[2].append(self.kept[1][h])
            self.steps[2].append(
                remote(
                    grad.at[h, blocks, self.kept[1][h], :], relay.at[h], sems, (at, h, 2), by_z[h]
                )
            )
            self.passed.append(
                remote(relay.at[h], self.bufs[2].at[h], sems, (at, h, 5), by_z[1 - h])
            )

    def start(self, step):
        if step == 3:
            pl.semaphore_wait(self.credit.at[self.at], 2)
        for copy in self.steps[step]:
            copy.start()

    def turn(self, step):
        self.wait(step)
        self.start(step + 1)

    def relay(self):
        for copy, onward in zip(self.steps[2], self.passed):
            copy.wait_recv()
            onward.start()

    def wait(self, step):
        for h, copy in enumerate(self.steps[step]):
            if step == 2:
                copy.wait_send()
                self.passed[h].wait()
            else:
                copy.wait()
            if step < 3:
                keep, buf = self.kept[step][h], self.bufs[step]

                def add(n):
                    self.grad[h, self.lead + n, keep, :] = (
                        self.grad[h, self.lead + n, keep, :].astype(F32) + buf[h, n].astype(F32)
                    ).astype(BF)

                repeat(buf.shape[1], add)
        if step == 1:
            for peer in self.greeted:
                pl.semaphore_signal(
                    self.credit.at[self.at],
                    inc=1,
                    device_id=peer,
                    device_id_type=pl.DeviceIdType.MESH,
                )


def layer_kernel(
    tokens,
    out_grad,
    w1,
    index1,
    w2,
    table,
    first_left,
    first_right,
    second_left,
    second_right,
    output,
    tokens_grad,
    g_w1,
    g_fl,
    g_fr,
    g_w2,
    g_sl,
    g_sr,
    tokens_all,
    grads_all,
    w2_all,
    index_all,
    index_smem,
    hidden,
    hidden_t,
    pre_grad,
    tokens_t,
    rank_first_t,
    slope,
    own,
    away,
    chip_sum,
    part,
    near_a,
    far_a,
    z_a,
    ranks_a,
    near_b,
    far_b,
    z_b,
    ranks_b,
    swap,
    sent,
    out_in,
    *rest,
):
    bufs, rest = rest[:28], rest[28:]
    (
        tok_send,
        tok_recv,
        grad_send,
        grad_recv,
        rank_send_a,
        rank_recv_a,
        rank_send_b,
        rank_recv_b,
        w_send,
        w_recv,
        i_send,
        i_recv,
        dp_send,
        dp_recv,
        credit,
        swap_send,
        swap_recv,
        x_send,
        x_recv,
        inbox_free,
        local,
    ) = rest
    place = Place()
    rows = pre_grad.shape[0]
    half = first_left.shape[1] // 2
    width = w1.shape[2]
    mine = pl.ds(pl.multiple_of(place.core * half, half), half)
    other = pl.ds(pl.multiple_of((1 - place.core) * half, half), half)

    loads = [
        pltpu.make_async_copy(
            tokens.at[:, pl.ds(d * width, width)], tokens_all.at[0, d], local.at[d]
        )
        for d in range(2)
    ]
    loads.append(pltpu.make_async_copy(out_grad, grads_all.at[0], local.at[2]))
    loads.append(pltpu.make_async_copy(w2.at[:, 0], w2_all.at[0], local.at[3]))
    loads.append(pltpu.make_async_copy(table, index_all.at[0], local.at[4]))
    for load in loads:
        load.start()
    greet(
        [place.mp_peer(bits) for bits in range(1, 8)]
        + [place.mp_peer(0, 1)]
        + [place.dp_peer(1), place.dp_peer(3), place.far_z()]
    )
    spread_tok = Spread(place, tokens_all, (tok_send, tok_recv))
    spread_grad = Spread(place, grads_all, (grad_send, grad_recv))
    sums_a = RankSum(
        place, ranks_a, own, away, near_a, chip_sum, far_a, part, z_a, (rank_send_a, rank_recv_a)
    )
    sums_b = RankSum(
        place, ranks_b, own, away, near_b, chip_sum, far_b, part, z_b, (rank_send_b, rank_recv_b)
    )
    w_copies = [
        remote(w2.at[:, level], w2_all.at[level], (w_send, w_recv), level - 1, place.level(level))
        for level in (4, 2, 3, 1)
    ]
    i_copies = [
        remote(
            table,
            index_all.at[level],
            (i_send, i_recv),
            level - 1,
            place.level(level),
        )
        for level in range(1, 5)
    ]
    dp_sems = (dp_send, dp_recv)
    grads = ((g_w2, 0), (g_sl, 0), (g_w1, 0), (g_w1, 5), (g_fr, 0), (g_sr, 0), (g_fl, 0))
    r_w2, r_sl, r_w1a, r_w1b, r_fr, r_sr, r_fl = [
        Reduced(place, grad, lead, *bufs[4 * at : 4 * at + 4], dp_sems, credit, at)
        for at, (grad, lead) in enumerate(grads)
    ]

    def turn_tokens(level):
        def step(d):
            tokens_t[level, d] = tokens_all[level, d].T

        repeat(2, step)

    for load in loads:
        load.wait()
    spread_tok.start_near(0, CHUNKS)
    spread_tok.start_direct()
    for copy in i_copies:
        copy.start()
    both = jnp.concatenate([tokens_all[0, 0], tokens_all[0, 1]], axis=1)
    sums_a.set(0, nn(both, first_left[:, mine]), nn(both, first_left[:, other]))
    flow = grads_all[0]
    sums_a.set(1, nt(flow, second_right[mine, :]), nt(flow, second_right[other, :]))
    sums_a.start()
    turn_tokens(0)
    spread_tok.pass_on(0)
    sums_a.step_chip()
    spread_tok.pass_on(1)
    spread_tok.wait_slot(1)
    turn_tokens(1)
    spread_tok.pass_on(2)
    spread_tok.pass_on(3)
    sums_a.step_across()
    spread_grad.start_near(0, 1)
    sums_a.step_sum()
    spread_grad.start_near(1, CHUNKS - 1)
    spread_grad.start_direct()
    for copy in w_copies:
        copy.start()
    spread_tok.wait_slot(4)
    turn_tokens(4)
    spread_tok.wait_onward()

    def block_part(f):
        picks = [tokens_all[level, index1[f, level]] for level in range(5)]
        slope[f] = nn(jnp.concatenate(picks, axis=1), w1[f].reshape(5 * width, width))

    repeat(4, block_part)
    sums_a.step_back()
    spread_grad.pass_on(0)
    sums_a.finish()

    def forward(f):
        pre = slope[f] + nn(ranks_a[0], first_right[:, at_ds(f, width)])
        sigma = 1.0 / (1.0 + jnp.exp(-pre))
        active = (pre * sigma).astype(BF)
        hidden[f] = active
        hidden_t[f] = active.T
        slope[f] = sigma * (1.0 + pre * (1.0 - sigma))

    def forward_and_pass(f):
        forward(f)
        spread_grad.pass_on(f + 1)

    repeat(3, forward_and_pass)
    forward(jnp.int32(3))
    spread_tok.close()
    for peer in (place.level(1), place.level(2), place.mp_peer(3), place.level(4)):
        pl.semaphore_signal(inbox_free, inc=1, device_id=peer, device_id_type=pl.DeviceIdType.MESH)

    for copy in i_copies:
        copy.wait()
    fetch = pltpu.make_async_copy(index_all, index_smem, local.at[0])
    fetch.start()
    fetch.wait()

    def second_left_part(d):
        g_sl[lax.div(d, 2), 0, at_ds(lax.rem(d, 2), width), :] = nn(hidden_t[d], ranks_a[1]).astype(BF)

    repeat(4, second_left_part)
    r_sl.start(0)

    def second_grads(at):
        level = at + lax.div(at, 3)
        for e in range(2):
            flow = grads_all[level, :, e * width : e * width + width]
            g_w2[e, level] = nn(hidden_t[index_smem[level, 4 + e, level]], flow).astype(BF)

    turn_tokens(2)
    turn_tokens(3)
    units = jnp.concatenate([hidden[d] for d in range(4)], axis=1)
    sums_b.set(0, nn(units, second_left[:, mine]), nn(units, second_left[:, other]))
    spread_grad.wait_slot(1)
    spread_grad.wait_slot(4)
    repeat(4, second_grads)
    spread_grad.wait_onward()
    for e in range(2):
        flow = grads_all[3, :, e * width : e * width + width]
        g_w2[e, 3] = nn(hidden_t[index_smem[3, 4 + e, 3]], flow).astype(BF)
    r_w2.start(0)

    def hidden_back(d):
        total = nt(ranks_a[1], second_left[at_ds(d, width), :])
        for level in range(5):
            weights = [w2_all[level, e] for e in range(2)]
            tiles = [tile_of(index_all[level, 4 + e : 5 + e, level : level + 1], d) for e in range(2)]
            total = total + nt(grads_all[level], masked(weights, tiles))
        pre_grad[:, at_ds(d, width)] = (total * slope[d]).astype(BF)

    rank_first_t[...] = ranks_a[0].T
    for copy in w_copies:
        copy.wait()
    repeat(4, hidden_back)
    spread_grad.close()
    r_sl.turn(0)
    r_w2.turn(0)

    sums_b.set(1, nt(pre_grad[...], first_right[mine, :]), nt(pre_grad[...], first_right[other, :]))
    sums_b.start()

    def first_grads(part):
        def step(h):
            f = 2 * h + part
            picks = [tokens_t[level, index1[f, level]] for level in range(5)]
            product = nn(
                jnp.concatenate(picks + [rank_first_t[...]], axis=0),
                pre_grad[:, at_ds(f, width)],
            ).astype(BF)
            for level in range(5):
                g_w1[h, part * 5 + level] = product[level * width : level * width + width]
            for r in range(2):
                low = (5 + r) * width
                g_fr[r, 0, :, at_ds(f, width)] = product[low : low + width]

        repeat(2, step)

    first_grads(0)
    r_w1a.start(0)
    sums_b.step_chip()
    first_grads(1)
    r_w1b.start(0)
    r_fr.start(0)
    r_sl.turn(1)
    r_w2.turn(1)

    def out_part(level, e):
        return nn(hidden[index_smem[level, 4 + e, level]], w2_all[level, e])

    def tok_part(level, d):
        weights = [w1[f, level] for f in range(4)]
        tiles = [tile_of(table[f : f + 1, level : level + 1], d) for f in range(4)]
        return nt(pre_grad[...], masked(weights, tiles))

    parts = (out_part, tok_part)

    def box(side, slot, block):
        return tokens_all.at[slot, block] if side else out_in.at[slot - 1, block]

    def remote_part(side, level, peer):
        return remote(
            sent.at[level - 1],
            tokens_all.at[level] if side else out_in.at[level - 1],
            (x_send, x_recv),
            (side, level),
            peer,
        )

    peers = {1: place.level(1), 2: place.level(2), 3: place.mp_peer(3), 4: place.level(4)}
    copies = [
        {level: remote_part(side, level, peer) for level, peer in peers.items()}
        for side in range(2)
    ]

    def send_parts(side):
        for level in (3, 4, 1):
            if side:
                copies[0][level].wait_send()

            def step(block, level=level):
                sent[level - 1, block] = parts[side](level, block).astype(BF)

            repeat(2, step)
            copies[side][level].start()

    def send_joined(side):
        copies[side][3].wait_recv()
        if side:
            copies[0][2].wait_send()

        def step(block):
            joined = parts[side](2, block) + box(side, 3, block)[...].astype(F32)
            sent[1, block] = joined.astype(BF)

        repeat(2, step)
        copies[side][2].start()

    def join(side, rank_part, result):
        for level in (1, 4, 2):
            copies[side][level].wait_recv()

        def step(block):
            total = parts[side](0, block) + rank_part(block)
            for level in (1, 4, 2):
                total = total + box(side, level, block)[...].astype(F32)
            result[:, at_ds(block, width)] = total.astype(BF)

        repeat(2, step)

    send_parts(0)
    r_w1a.turn(0)
    sums_b.step_across()
    r_sl.relay()
    r_w2.relay()
    send_joined(0)
    pl.semaphore_wait(inbox_free, 4)
    r_w1b.turn(0)
    r_sl.turn(2)
    r_w2.wait(2)
    quarter = r_w2.kept[2]
    swaps = [
        remote(
            g_w2.at[h, level, quarter[h], :],
            swap.at[h, level - 1],
            (swap_send, swap_recv),
            (h, level - 1),
            place.level(level),
        )
        for h in range(2)
        for level in range(1, 5)
    ]
    for copy in swaps:
        copy.start()
    sums_b.step_sum()
    send_parts(1)
    r_w1a.turn(1)
    r_fr.turn(0)
    sums_b.step_back()
    for copy in swaps:
        copy.wait()
    for h in range(2):
        for level in range(1, 5):
            g_w2[h, level, quarter[h], :] = swap[h, level - 1]
    r_w2.start(3)
    r_w1b.turn(1)
    r_w1a.relay()
    sums_b.finish()
    rank_second_t = ranks_b[0].T
    for h in range(2):
        g_sr[h, 0] = nn(rank_second_t[h * 256 : h * 256 + 256, :], grads_all[0]).astype(BF)
        g_fl[h, 0] = nn(tokens_t[0, h], ranks_b[1]).astype(BF)
    r_sr.start(0)
    r_fl.start(0)
    r_fr.turn(1)
    r_sl.turn(3)
    r_w1b.relay()
    send_joined(1)
    r_w1a.turn(2)
    r_w2.turn(3)
    r_fr.relay()
    r_sr.turn(0)
    r_fl.turn(0)
    join(0, lambda e: nn(ranks_b[0], second_right[:, at_ds(e, width)]), output)
    r_w1b.turn(2)
    r_sr.turn(1)
    r_fl.turn(1)
    r_fr.turn(2)
    r_w1a.turn(3)
    r_sr.relay()
    r_fl.relay()
    join(1, lambda d: nt(ranks_b[1], first_left[at_ds(d, width), :]), tokens_grad)
    r_sr.turn(2)
    r_fl.turn(2)
    r_w1b.turn(3)
    r_fr.turn(3)
    r_sr.turn(3)
    r_fl.turn(3)
    for grad in (r_sl, r_w2, r_w1a, r_w1b, r_fr, r_sr, r_fl):
        grad.wait(4)
    for level in range(1, 5):
        copies[1][level].wait_send()


def copy_kernel(*refs):
    count = len(refs) // 2
    for at in range(count):
        refs[count + at][...] = refs[at][...]


def body(
    tokens,
    out_grad,
    first_blocks,
    first_index,
    second_blocks,
    second_index,
    first_left,
    first_right,
    second_left,
    second_right,
):
    rows, features = tokens.shape
    rank = first_left.shape[1]
    units = first_right.shape[1]
    width = first_blocks.shape[2]
    vmem = pl.BlockSpec(memory_space=pltpu.VMEM)
    smem = pl.BlockSpec(memory_space=pltpu.SMEM)
    anywhere = pl.BlockSpec(memory_space=pl.ANY)
    dma = pltpu.SemaphoreType.DMA

    def shape(*extent):
        return jax.ShapeDtypeStruct(extent, BF)

    half = rank // 2

    table = jnp.concatenate([first_index, second_index], axis=0)
    table = jnp.pad(table, ((0, 8 - table.shape[0]), (0, 128 - table.shape[1])))

    grads = [
        (2, 5, width, width),
        (2, 1, units // 2, rank),
        (2, 10, width, width),
        (2, 1, rank // 2, units),
        (2, 1, rank // 2, features),
        (2, 1, features // 2, rank),
    ]
    pieces = grads[:2] + [(2, 5, width, width)] * 2 + grads[3:]
    inboxes = []
    for two, count, tall, wide in pieces:
        for step in (2, 4, 4, 4):
            inboxes.append(pltpu.VMEM((two, count, tall // step, wide), BF))
    scratch = [
        pltpu.VMEM((5, features // width, rows, width), BF),
        pltpu.VMEM((5, rows, features), BF),
        pltpu.VMEM((5, 2, width, width), BF),
        pltpu.VMEM((5, 8, 128), jnp.int32),
        pltpu.SMEM((5, 8, 128), jnp.int32),
        pltpu.VMEM((units // width, rows, width), BF),
        pltpu.VMEM((units // width, width, rows), BF),
        pltpu.VMEM((rows, units), BF),
        pltpu.VMEM((5, features // width, width, rows), BF),
        pltpu.VMEM((rank, rows), BF),
        pltpu.VMEM((units // width, rows, width), F32),
        pltpu.VMEM((2, rows, half), F32),
        pltpu.VMEM((2, rows, half), BF),
        pltpu.VMEM((2, rows, half), BF),
        pltpu.VMEM((2, rows // 4, half), BF),
    ]
    for _ in range(2):
        scratch += [
            pltpu.VMEM((2, rows, half), BF),
            pltpu.VMEM((3, 2, rows // 4, half), BF),
            pltpu.VMEM((2, rows // 4, half), BF),
            pltpu.VMEM((2, rows, rank), BF),
        ]
    scratch += [
        pltpu.VMEM((2, 4, width // 4, width), BF),
        pltpu.VMEM((4, features // width, rows, width), BF),
        pltpu.VMEM((4, features // width, rows, width), BF),
    ]
    semaphores = [dma((2 + 2 * CHUNKS,))] * 4 + [dma((16,))] * 4 + [dma((4,))] * 4
    semaphores += [dma((7, 2, 6))] * 2 + [pltpu.SemaphoreType.REGULAR((7,))]
    semaphores += [dma((2, 4))] * 2 + [dma((2, 5))] * 2
    semaphores += [pltpu.SemaphoreType.REGULAR, dma((5,))]
    order = (2, 5, 3, 0, 1, 4)
    results = pl.pallas_call(
        layer_kernel,
        out_shape=[shape(rows, features), shape(rows, features)]
        + [shape(*grads[at]) for at in order],
        in_specs=[anywhere, anywhere, vmem, smem, anywhere, vmem] + [vmem] * 4,
        out_specs=[vmem] * 8,
        scratch_shapes=scratch + inboxes + semaphores,
        compiler_params=pltpu.CompilerParams(
            collective_id=0, has_side_effects=True, vmem_limit_bytes=63 * 2**20
        ),
        name="layer_kernel",
    )(
        tokens,
        out_grad,
        first_blocks,
        first_index,
        second_blocks,
        table,
        first_left,
        first_right,
        second_left,
        second_right,
    )
    flat = [result.reshape(-1, result.shape[-1]) for result in results]
    steps = 4
    specs = [
        pl.BlockSpec((result.shape[0] // steps, result.shape[1]), lambda at: (at, 0))
        for result in flat
    ]
    output, tokens_grad, g_w1, g_fl, g_fr, g_w2, g_sl, g_sr = pl.pallas_call(
        copy_kernel,
        out_shape=[shape(*result.shape) for result in flat],
        grid=(steps,),
        in_specs=specs,
        out_specs=specs,
        compiler_params=pltpu.CompilerParams(vmem_limit_bytes=63 * 2**20),
        name="copy_kernel",
    )(*flat)
    return (
        output,
        tokens_grad,
        g_w1.reshape(first_blocks.shape),
        g_fl.reshape(first_left.shape),
        g_fr.reshape(first_right.shape),
        g_w2.reshape(second_blocks.shape),
        g_sl.reshape(second_left.shape),
        g_sr.reshape(second_right.shape),
    )


def solution(mesh):
    placed = (
        P("dp", "mp"),
        P("dp", "mp"),
        P("mp", None, None, None),
        P("mp", None),
        P("mp", None, None, None),
        P("mp", None),
        P("mp", None),
        P(None, "mp"),
        P("mp", None),
        P(None, "mp"),
    )
    return jax.shard_map(
        body,
        mesh=mesh,
        in_specs=placed,
        out_specs=(
            P("dp", "mp"),
            P("dp", "mp"),
            P("mp", None, None, None),
            P("mp", None),
            P(None, "mp"),
            P("mp", None, None, None),
            P("mp", None),
            P(None, "mp"),
        ),
        check_vma=False,
    )
```

```python
import jax
import jax.numpy as jnp
from jax import lax
from jax.experimental import pallas as pl
from jax.experimental.pallas import tpu as pltpu
from jax.sharding import PartitionSpec as P

BF = jnp.bfloat16
F32 = jnp.float32
CHUNKS = 4


def nn(left, right):
    return jnp.dot(left, right, preferred_element_type=F32)


def nt(left, right):
    return lax.dot_general(left, right, (((1,), (1,)), ((), ())), preferred_element_type=F32)


def flip(bit, by):
    return 1 - bit if by else bit


def tile_of(index, at):
    hot = (index == at).astype(F32)
    return jnp.broadcast_to(hot, (16, 128)).astype(BF)


def masked(weights, tiles):
    parts = []
    for weight, tile in zip(weights, tiles):
        wide = jnp.concatenate([tile, tile], axis=1)
        tall = weight.reshape(weight.shape[0] // 16, 16, weight.shape[1])
        parts.append((tall * wide[None]).reshape(weight.shape))
    return jnp.concatenate(parts, axis=1)


class Place:
    def __init__(self):
        self.dp = lax.axis_index("dp")
        self.mp = lax.axis_index("mp")
        self.core = lax.rem(self.mp, 2)
        chip = lax.div(self.mp, 2)
        self.chip = chip
        self.y0 = lax.rem(chip, 2)
        self.y1 = lax.rem(lax.div(chip, 2), 2)
        self.z = lax.div(chip, 4)
        self.x0 = lax.rem(self.dp, 2)
        self.x1 = lax.rem(lax.div(self.dp, 2), 2)
        self.z_hi = lax.div(self.dp, 4)

    def mp_peer(self, chip_bits, core_bit=0):
        y0 = flip(self.y0, chip_bits & 1)
        y1 = flip(self.y1, chip_bits & 2)
        z = flip(self.z, chip_bits & 4)
        return (self.dp, ((z * 2 + y1) * 2 + y0) * 2 + flip(self.core, core_bit))

    def chip_peer(self, chip_bits):
        y0 = flip(self.y0, chip_bits & 1)
        y1 = flip(self.y1, chip_bits & 2)
        z = flip(self.z, chip_bits & 4)
        return (z * 2 + y1) * 2 + y0

    def dp_peer(self, bits):
        x0 = flip(self.x0, bits & 1)
        x1 = flip(self.x1, bits & 2)
        z = flip(self.z_hi, bits & 4)
        return ((z * 2 + x1) * 2 + x0, self.mp)

    def far_z(self):
        return (self.dp_peer(4)[0], self.mp_peer(4)[1])

    def level(self, level):
        return [None, self.mp_peer(0, 1), self.mp_peer(1), self.mp_peer(2), self.mp_peer(4)][level]


def greet(peers):
    barrier = pltpu.get_barrier_semaphore()
    for peer in peers:
        pl.semaphore_signal(barrier, inc=1, device_id=peer, device_id_type=pl.DeviceIdType.MESH)
    pl.semaphore_wait(barrier, len(peers))


def remote(src, dst, sems, at, peer):
    send, recv = sems
    return pltpu.make_async_remote_copy(
        src_ref=src,
        dst_ref=dst,
        send_sem=send.at[at],
        recv_sem=recv.at[at],
        device_id=peer,
        device_id_type=pl.DeviceIdType.MESH,
    )


def at_ds(index, size):
    return pl.ds(pl.multiple_of(index * size, size), size)


def repeat(count, step):
    lax.fori_loop(0, count, lambda at, carry: (step(at), carry)[1], 0)


class RankSum:
    def __init__(self, place, result, own, away, near, chip_sum, far, part, z_part, sems):
        self.result = result
        self.own, self.away, self.near, self.chip_sum, self.far = own, away, near, chip_sum, far
        self.part, self.z_part = part, z_part
        rows, half = near.shape[1], near.shape[2]
        step = rows // 4
        self.columns = at_ds(place.core, half)
        self.rows = at_ds(place.y1 * 2 + place.y0, step)
        sibling = place.mp_peer(0, 1)
        self.cores = remote(away, near, sems, 0, sibling)
        self.scatter = []
        self.gather = []
        mine = result.at[:, self.rows, self.columns]
        for bits in range(1, 4):
            other = at_ds(flip(place.y1, bits & 2) * 2 + flip(place.y0, bits & 1), step)
            peer = place.mp_peer(bits)
            self.scatter.append(
                remote(chip_sum.at[:, other, :], far.at[bits - 1], sems, bits, peer)
            )
            self.gather.append(remote(mine, mine, sems, 3 + bits, peer))
        self.across = remote(part, z_part, sems, 7, place.level(4))
        whole = result.at[:, :, self.columns]
        self.back = remote(whole, whole, sems, 8, sibling)

    def set(self, which, own, away):
        self.own[which] = own
        self.away[which] = away.astype(BF)

    def start(self):
        self.cores.start()

    def step_chip(self):
        self.cores.wait()

        def add(which):
            self.chip_sum[which] = (self.own[which] + self.near[which].astype(F32)).astype(BF)

        repeat(2, add)
        for copy in self.scatter:
            copy.start()

    def step_across(self):
        total = self.chip_sum[:, self.rows, :].astype(F32)
        for copy in self.scatter:
            copy.wait()
        for at in range(3):
            total = total + self.far[at].astype(F32)
        self.part[...] = total.astype(BF)
        self.across.start()

    def step_sum(self):
        self.across.wait()
        total = self.part[...].astype(F32) + self.z_part[...].astype(F32)
        self.result[:, self.rows, self.columns] = total.astype(BF)
        for copy in self.gather:
            copy.start()

    def step_back(self):
        for copy in self.gather:
            copy.wait()
        self.back.start()

    def finish(self):
        self.back.wait()


class Spread:
    def __init__(self, place, held, sems):
        self.held, self.sems = held, sems
        self.blocked = len(held.shape) == 4
        self.rows = held.shape[-2] * (2 if self.blocked else 1) // CHUNKS
        self.one, self.two, self.three = place.level(1), place.level(2), place.mp_peer(3)
        self.four = place.level(4)
        self.direct = [
            remote(held.at[0], held.at[level], sems, at, peer)
            for at, (level, peer) in enumerate(((4, self.four), (1, self.one)))
        ]

    def piece(self, slot, chunk):
        if self.blocked:
            return self.held.at[slot, lax.div(chunk, 2), at_ds(lax.rem(chunk, 2), self.rows), :]
        return self.held.at[slot, at_ds(chunk, self.rows), :]

    def near(self, chunk):
        return remote(
            self.piece(0, chunk), self.piece(2, chunk), self.sems, 2 + chunk, self.two
        )

    def onward(self, chunk):
        return remote(
            self.piece(2, chunk), self.piece(3, chunk), self.sems, 2 + CHUNKS + chunk, self.three
        )

    def start_direct(self):
        for copy in self.direct:
            copy.start()

    def start_near(self, first, count):
        repeat(count, lambda at: self.near(first + at).start())

    def pass_on(self, chunk):
        chunk = jnp.int32(chunk)
        self.near(chunk).wait_recv()
        self.onward(chunk).start()

    def wait_slot(self, level):
        self.direct[0 if level == 4 else 1].wait_recv()

    def wait_onward(self):
        repeat(CHUNKS, lambda chunk: self.onward(chunk).wait_recv())

    def close(self):
        for copy in self.direct:
            copy.wait_send()

        def finish(chunk):
            self.near(chunk).wait_send()
            self.onward(chunk).wait_send()

        repeat(CHUNKS, finish)


class Reduced:
    def __init__(self, place, grad, lead, first, second, third, relay, sems, credit, at):
        self.credit, self.at, self.lead = credit, at, lead
        blocks = pl.ds(lead, first.shape[1])
        self.grad, self.bufs = grad, (first, second, third)
        rows = grad.shape[2]
        x0, x1 = place.x0, place.x1
        cross = x0 + x1 - 2 * x0 * x1
        near, back = place.dp_peer(1), place.dp_peer(3)
        by_z = (place.level(4), place.far_z())
        self.passed = []
        self.greeted = (near, back)
        self.steps = [[] for _ in range(5)]
        self.kept = [[] for _ in range(3)]
        for h in range(2):
            keys = (cross, x1) if h == 0 else (x1, x0)
            peers = (near, back) if h == 0 else (back, near)
            offset, size = 0, rows
            for step in range(2):
                size = size // 2
                keep = pl.ds(pl.multiple_of(offset + keys[step] * size, size), size)
                send = pl.ds(pl.multiple_of(offset + (1 - keys[step]) * size, size), size)
                self.kept[step].append(keep)
                self.steps[step].append(
                    remote(
                        grad.at[h, blocks, send, :],
                        self.bufs[step].at[h],
                        sems,
                        (at, h, step),
                        peers[step],
                    )
                )
                own = grad.at[h, blocks, keep, :]
                self.steps[4 - step].append(
                    remote(own, own, sems, (at, h, 4 - step), peers[step])
                )
                offset = offset + keys[step] * size
            self.kept[2].append(self.kept[1][h])
            self.steps[2].append(
                remote(
                    grad.at[h, blocks, self.kept[1][h], :], relay.at[h], sems, (at, h, 2), by_z[h]
                )
            )
            self.passed.append(
                remote(relay.at[h], self.bufs[2].at[h], sems, (at, h, 5), by_z[1 - h])
            )

    def start(self, step):
        if step == 3:
            pl.semaphore_wait(self.credit.at[self.at], 2)
        for copy in self.steps[step]:
            copy.start()

    def turn(self, step):
        self.wait(step)
        self.start(step + 1)

    def relay(self):
        for copy, onward in zip(self.steps[2], self.passed):
            copy.wait_recv()
            onward.start()

    def wait(self, step):
        for h, copy in enumerate(self.steps[step]):
            if step == 2:
                copy.wait_send()
                self.passed[h].wait()
            else:
                copy.wait()
            if step < 3:
                keep, buf = self.kept[step][h], self.bufs[step]

                def add(n):
                    self.grad[h, self.lead + n, keep, :] = (
                        self.grad[h, self.lead + n, keep, :].astype(F32) + buf[h, n].astype(F32)
                    ).astype(BF)

                repeat(buf.shape[1], add)
        if step == 1:
            for peer in self.greeted:
                pl.semaphore_signal(
                    self.credit.at[self.at],
                    inc=1,
                    device_id=peer,
                    device_id_type=pl.DeviceIdType.MESH,
                )


def layer_kernel(
    tokens,
    out_grad,
    w1,
    index1,
    w2,
    table,
    first_left,
    first_right,
    second_left,
    second_right,
    output,
    tokens_grad,
    g_w1,
    g_fl,
    g_fr,
    g_w2,
    g_sl,
    g_sr,
    tokens_all,
    grads_all,
    w2_all,
    index_all,
    index_smem,
    hidden,
    hidden_t,
    pre_grad,
    tokens_t,
    rank_first_t,
    slope,
    own,
    away,
    chip_sum,
    part,
    near_a,
    far_a,
    z_a,
    ranks_a,
    near_b,
    far_b,
    z_b,
    ranks_b,
    swap,
    sent,
    out_in,
    *rest,
):
    bufs, rest = rest[:28], rest[28:]
    (
        tok_send,
        tok_recv,
        grad_send,
        grad_recv,
        rank_send_a,
        rank_recv_a,
        rank_send_b,
        rank_recv_b,
        w_send,
        w_recv,
        i_send,
        i_recv,
        dp_send,
        dp_recv,
        credit,
        swap_send,
        swap_recv,
        x_send,
        x_recv,
        inbox_free,
        local,
    ) = rest
    place = Place()
    rows = pre_grad.shape[0]
    half = first_left.shape[1] // 2
    width = w1.shape[2]
    mine = pl.ds(pl.multiple_of(place.core * half, half), half)
    other = pl.ds(pl.multiple_of((1 - place.core) * half, half), half)

    loads = [
        pltpu.make_async_copy(
            tokens.at[:, pl.ds(d * width, width)], tokens_all.at[0, d], local.at[d]
        )
        for d in range(2)
    ]
    loads.append(pltpu.make_async_copy(out_grad, grads_all.at[0], local.at[2]))
    loads.append(pltpu.make_async_copy(w2.at[:, 0], w2_all.at[0], local.at[3]))
    loads.append(pltpu.make_async_copy(table, index_all.at[0], local.at[4]))
    for load in loads:
        load.start()
    greet(
        [place.mp_peer(bits) for bits in range(1, 8)]
        + [place.mp_peer(0, 1)]
        + [place.dp_peer(1), place.dp_peer(3), place.far_z()]
    )
    spread_tok = Spread(place, tokens_all, (tok_send, tok_recv))
    spread_grad = Spread(place, grads_all, (grad_send, grad_recv))
    sums_a = RankSum(
        place, ranks_a, own, away, near_a, chip_sum, far_a, part, z_a, (rank_send_a, rank_recv_a)
    )
    sums_b = RankSum(
        place, ranks_b, own, away, near_b, chip_sum, far_b, part, z_b, (rank_send_b, rank_recv_b)
    )
    w_copies = [
        remote(w2.at[:, level], w2_all.at[level], (w_send, w_recv), level - 1, place.level(level))
        for level in (4, 2, 3, 1)
    ]
    i_copies = [
        remote(
            table,
            index_all.at[level],
            (i_send, i_recv),
            level - 1,
            place.level(level),
        )
        for level in range(1, 5)
    ]
    dp_sems = (dp_send, dp_recv)
    grads = ((g_w2, 0), (g_sl, 0), (g_w1, 0), (g_w1, 5), (g_fr, 0), (g_sr, 0), (g_fl, 0))
    r_w2, r_sl, r_w1a, r_w1b, r_fr, r_sr, r_fl = [
        Reduced(place, grad, lead, *bufs[4 * at : 4 * at + 4], dp_sems, credit, at)
        for at, (grad, lead) in enumerate(grads)
    ]

    def turn_tokens(level):
        def step(d):
            tokens_t[level, d] = tokens_all[level, d].T

        repeat(2, step)

    for load in loads:
        load.wait()
    spread_tok.start_near(0, CHUNKS)
    spread_tok.start_direct()
    for copy in i_copies:
        copy.start()
    both = jnp.concatenate([tokens_all[0, 0], tokens_all[0, 1]], axis=1)
    sums_a.set(0, nn(both, first_left[:, mine]), nn(both, first_left[:, other]))
    flow = grads_all[0]
    sums_a.set(1, nt(flow, second_right[mine, :]), nt(flow, second_right[other, :]))
    sums_a.start()
    turn_tokens(0)
    spread_tok.pass_on(0)
    sums_a.step_chip()
    spread_tok.pass_on(1)
    spread_tok.wait_slot(1)
    turn_tokens(1)
    spread_tok.pass_on(2)
    spread_tok.pass_on(3)
    sums_a.step_across()
    spread_grad.start_near(0, 1)
    sums_a.step_sum()
    spread_grad.start_near(1, CHUNKS - 1)
    spread_grad.start_direct()
    for copy in w_copies:
        copy.start()
    spread_tok.wait_slot(4)
    turn_tokens(4)
    spread_tok.wait_onward()

    def block_part(f):
        picks = [tokens_all[level, index1[f, level]] for level in range(5)]
        slope[f] = nn(jnp.concatenate(picks, axis=1), w1[f].reshape(5 * width, width))

    repeat(4, block_part)
    sums_a.step_back()
    spread_grad.pass_on(0)
    sums_a.finish()

    def forward(f):
        pre = slope[f] + nn(ranks_a[0], first_right[:, at_ds(f, width)])
        sigma = 1.0 / (1.0 + jnp.exp(-pre))
        active = (pre * sigma).astype(BF)
        hidden[f] = active
        hidden_t[f] = active.T
        slope[f] = sigma * (1.0 + pre * (1.0 - sigma))

    def forward_and_pass(f):
        forward(f)
        spread_grad.pass_on(f + 1)

    repeat(3, forward_and_pass)
    forward(jnp.int32(3))
    def out_part(level, e):
        return nn(hidden[index_smem[level, 4 + e, level]], w2_all[level, e])

    def tok_part(level, d):
        weights = [w1[f, level] for f in range(4)]
        tiles = [tile_of(table[f : f + 1, level : level + 1], d) for f in range(4)]
        return nt(pre_grad[...], masked(weights, tiles))

    parts = (out_part, tok_part)

    def box(side, slot, block):
        return tokens_all.at[slot, block] if side else out_in.at[slot - 1, block]

    def remote_part(side, level, peer):
        return remote(
            sent.at[level - 1],
            tokens_all.at[level] if side else out_in.at[level - 1],
            (x_send, x_recv),
            (side, level),
            peer,
        )

    peers = {1: place.level(1), 2: place.level(2), 3: place.mp_peer(3), 4: place.level(4)}
    copies = [
        {level: remote_part(side, level, peer) for level, peer in peers.items()}
        for side in range(2)
    ]

    def send_part(side, level):
        if side:
            copies[0][level].wait_send()

        def step(block):
            sent[level - 1, block] = parts[side](level, block).astype(BF)

        repeat(2, step)
        copies[side][level].start()

    def send_joined(side):
        copies[side][3].wait_recv()
        if side:
            copies[0][2].wait_send()

        def step(block):
            joined = parts[side](2, block) + box(side, 3, block)[...].astype(F32)
            sent[1, block] = joined.astype(BF)

        repeat(2, step)
        copies[side][2].start()

    def join(side, rank_part, result):
        for level in (1, 4, 2):
            copies[side][level].wait_recv()

        def step(block):
            total = parts[side](0, block) + rank_part(block)
            for level in (1, 4, 2):
                total = total + box(side, level, block)[...].astype(F32)
            result[:, at_ds(block, width)] = total.astype(BF)

        repeat(2, step)

    for copy in i_copies:
        copy.wait()
    fetch = pltpu.make_async_copy(index_all, index_smem, local.at[0])
    fetch.start()
    fetch.wait()

    def second_left_part(d):
        g_sl[lax.div(d, 2), 0, at_ds(lax.rem(d, 2), width), :] = nn(hidden_t[d], ranks_a[1]).astype(BF)

    repeat(4, second_left_part)
    r_sl.start(0)

    def second_grads(at):
        level = at + lax.div(at, 3)
        for e in range(2):
            flow = grads_all[level, :, e * width : e * width + width]
            g_w2[e, level] = nn(hidden_t[index_smem[level, 4 + e, level]], flow).astype(BF)

    turn_tokens(2)
    turn_tokens(3)
    spread_tok.close()
    for peer in peers.values():
        pl.semaphore_signal(inbox_free, inc=1, device_id=peer, device_id_type=pl.DeviceIdType.MESH)
    units = jnp.concatenate([hidden[d] for d in range(4)], axis=1)
    sums_b.set(0, nn(units, second_left[:, mine]), nn(units, second_left[:, other]))
    spread_grad.wait_slot(1)
    spread_grad.wait_slot(4)
    repeat(4, second_grads)
    spread_grad.wait_onward()
    for e in range(2):
        flow = grads_all[3, :, e * width : e * width + width]
        g_w2[e, 3] = nn(hidden_t[index_smem[3, 4 + e, 3]], flow).astype(BF)
    r_w2.start(0)

    def hidden_back(d):
        total = nt(ranks_a[1], second_left[at_ds(d, width), :])
        for level in range(5):
            weights = [w2_all[level, e] for e in range(2)]
            tiles = [tile_of(index_all[level, 4 + e : 5 + e, level : level + 1], d) for e in range(2)]
            total = total + nt(grads_all[level], masked(weights, tiles))
        pre_grad[:, at_ds(d, width)] = (total * slope[d]).astype(BF)

    for copy in w_copies:
        copy.wait()
    for level in (3, 4, 1):
        send_part(0, level)
    rank_first_t[...] = ranks_a[0].T
    repeat(4, hidden_back)
    spread_grad.close()
    r_sl.turn(0)
    r_w2.turn(0)

    sums_b.set(1, nt(pre_grad[...], first_right[mine, :]), nt(pre_grad[...], first_right[other, :]))
    sums_b.start()

    def first_grads(part):
        def step(h):
            f = 2 * h + part
            picks = [tokens_t[level, index1[f, level]] for level in range(5)]
            product = nn(
                jnp.concatenate(picks + [rank_first_t[...]], axis=0),
                pre_grad[:, at_ds(f, width)],
            ).astype(BF)
            for level in range(5):
                g_w1[h, part * 5 + level] = product[level * width : level * width + width]
            for r in range(2):
                low = (5 + r) * width
                g_fr[r, 0, :, at_ds(f, width)] = product[low : low + width]

        repeat(2, step)

    first_grads(0)
    r_w1a.start(0)
    sums_b.step_chip()
    first_grads(1)
    r_w1b.start(0)
    r_fr.start(0)
    r_sl.turn(1)
    r_w2.turn(1)

    send_joined(0)
    sums_b.step_across()
    r_w1a.turn(0)
    pl.semaphore_wait(inbox_free, 4)
    send_part(1, 3)
    r_sl.relay()
    r_w2.relay()
    sums_b.step_sum()
    r_w1b.turn(0)
    send_part(1, 4)
    r_sl.turn(2)
    r_w2.wait(2)
    quarter = r_w2.kept[2]
    swaps = [
        remote(
            g_w2.at[h, level, quarter[h], :],
            swap.at[h, level - 1],
            (swap_send, swap_recv),
            (h, level - 1),
            place.level(level),
        )
        for h in range(2)
        for level in range(1, 5)
    ]
    for copy in swaps:
        copy.start()
    r_fr.turn(0)
    r_w1a.turn(1)
    sums_b.step_back()
    for copy in swaps:
        copy.wait()
    for h in range(2):
        for level in range(1, 5):
            g_w2[h, level, quarter[h], :] = swap[h, level - 1]
    r_w2.start(3)
    sums_b.finish()
    rank_second_t = ranks_b[0].T
    for h in range(2):
        g_sr[h, 0] = nn(rank_second_t[h * 256 : h * 256 + 256, :], grads_all[0]).astype(BF)
        g_fl[h, 0] = nn(tokens_t[0, h], ranks_b[1]).astype(BF)
    r_sr.start(0)
    r_fl.start(0)
    r_w1a.relay()
    r_w1b.turn(1)
    r_sl.turn(3)
    r_fr.turn(1)
    r_w1b.relay()
    r_w1a.turn(2)
    r_sr.turn(0)
    r_fl.turn(0)
    r_w2.turn(3)
    r_fr.relay()
    r_w1b.turn(2)
    r_sr.turn(1)
    r_fl.turn(1)
    r_fr.turn(2)
    r_w1a.turn(3)
    send_part(1, 1)
    r_sr.relay()
    r_fl.relay()
    send_joined(1)
    r_w1b.turn(3)
    r_sr.turn(2)
    r_fl.turn(2)
    r_fr.turn(3)
    join(0, lambda e: nn(ranks_b[0], second_right[:, at_ds(e, width)]), output)
    r_sr.turn(3)
    r_fl.turn(3)
    join(1, lambda d: nt(ranks_b[1], first_left[at_ds(d, width), :]), tokens_grad)
    for grad in (r_sl, r_w2, r_w1a, r_w1b, r_fr, r_sr, r_fl):
        grad.wait(4)
    for level in range(1, 5):
        copies[1][level].wait_send()


def copy_kernel(*refs):
    count = len(refs) // 2
    for at in range(count):
        refs[count + at][...] = refs[at][...]


def body(
    tokens,
    out_grad,
    first_blocks,
    first_index,
    second_blocks,
    second_index,
    first_left,
    first_right,
    second_left,
    second_right,
):
    rows, features = tokens.shape
    rank = first_left.shape[1]
    units = first_right.shape[1]
    width = first_blocks.shape[2]
    vmem = pl.BlockSpec(memory_space=pltpu.VMEM)
    smem = pl.BlockSpec(memory_space=pltpu.SMEM)
    anywhere = pl.BlockSpec(memory_space=pl.ANY)
    dma = pltpu.SemaphoreType.DMA

    def shape(*extent):
        return jax.ShapeDtypeStruct(extent, BF)

    half = rank // 2

    table = jnp.concatenate([first_index, second_index], axis=0)
    table = jnp.pad(table, ((0, 8 - table.shape[0]), (0, 128 - table.shape[1])))

    grads = [
        (2, 5, width, width),
        (2, 1, units // 2, rank),
        (2, 10, width, width),
        (2, 1, rank // 2, units),
        (2, 1, rank // 2, features),
        (2, 1, features // 2, rank),
    ]
    pieces = grads[:2] + [(2, 5, width, width)] * 2 + grads[3:]
    inboxes = []
    for two, count, tall, wide in pieces:
        for step in (2, 4, 4, 4):
            inboxes.append(pltpu.VMEM((two, count, tall // step, wide), BF))
    scratch = [
        pltpu.VMEM((5, features // width, rows, width), BF),
        pltpu.VMEM((5, rows, features), BF),
        pltpu.VMEM((5, 2, width, width), BF),
        pltpu.VMEM((5, 8, 128), jnp.int32),
        pltpu.SMEM((5, 8, 128), jnp.int32),
        pltpu.VMEM((units // width, rows, width), BF),
        pltpu.VMEM((units // width, width, rows), BF),
        pltpu.VMEM((rows, units), BF),
        pltpu.VMEM((5, features // width, width, rows), BF),
        pltpu.VMEM((rank, rows), BF),
        pltpu.VMEM((units // width, rows, width), F32),
        pltpu.VMEM((2, rows, half), F32),
        pltpu.VMEM((2, rows, half), BF),
        pltpu.VMEM((2, rows, half), BF),
        pltpu.VMEM((2, rows // 4, half), BF),
    ]
    for _ in range(2):
        scratch += [
            pltpu.VMEM((2, rows, half), BF),
            pltpu.VMEM((3, 2, rows // 4, half), BF),
            pltpu.VMEM((2, rows // 4, half), BF),
            pltpu.VMEM((2, rows, rank), BF),
        ]
    scratch += [
        pltpu.VMEM((2, 4, width // 4, width), BF),
        pltpu.VMEM((4, features // width, rows, width), BF),
        pltpu.VMEM((4, features // width, rows, width), BF),
    ]
    semaphores = [dma((2 + 2 * CHUNKS,))] * 4 + [dma((16,))] * 4 + [dma((4,))] * 4
    semaphores += [dma((7, 2, 6))] * 2 + [pltpu.SemaphoreType.REGULAR((7,))]
    semaphores += [dma((2, 4))] * 2 + [dma((2, 5))] * 2
    semaphores += [pltpu.SemaphoreType.REGULAR, dma((5,))]
    order = (2, 5, 3, 0, 1, 4)
    results = pl.pallas_call(
        layer_kernel,
        out_shape=[shape(rows, features), shape(rows, features)]
        + [shape(*grads[at]) for at in order],
        in_specs=[anywhere, anywhere, vmem, smem, anywhere, vmem] + [vmem] * 4,
        out_specs=[vmem] * 8,
        scratch_shapes=scratch + inboxes + semaphores,
        compiler_params=pltpu.CompilerParams(
            collective_id=0, has_side_effects=True, vmem_limit_bytes=63 * 2**20
        ),
        name="layer_kernel",
    )(
        tokens,
        out_grad,
        first_blocks,
        first_index,
        second_blocks,
        table,
        first_left,
        first_right,
        second_left,
        second_right,
    )
    flat = [result.reshape(-1, result.shape[-1]) for result in results]
    steps = 4
    specs = [
        pl.BlockSpec((result.shape[0] // steps, result.shape[1]), lambda at: (at, 0))
        for result in flat
    ]
    output, tokens_grad, g_w1, g_fl, g_fr, g_w2, g_sl, g_sr = pl.pallas_call(
        copy_kernel,
        out_shape=[shape(*result.shape) for result in flat],
        grid=(steps,),
        in_specs=specs,
        out_specs=specs,
        compiler_params=pltpu.CompilerParams(vmem_limit_bytes=63 * 2**20),
        name="copy_kernel",
    )(*flat)
    return (
        output,
        tokens_grad,
        g_w1.reshape(first_blocks.shape),
        g_fl.reshape(first_left.shape),
        g_fr.reshape(first_right.shape),
        g_w2.reshape(second_blocks.shape),
        g_sl.reshape(second_left.shape),
        g_sr.reshape(second_right.shape),
    )


def solution(mesh):
    placed = (
        P("dp", "mp"),
        P("dp", "mp"),
        P("mp", None, None, None),
        P("mp", None),
        P("mp", None, None, None),
        P("mp", None),
        P("mp", None),
        P(None, "mp"),
        P("mp", None),
        P(None, "mp"),
    )
    return jax.shard_map(
        body,
        mesh=mesh,
        in_specs=placed,
        out_specs=(
            P("dp", "mp"),
            P("dp", "mp"),
            P("mp", None, None, None),
            P("mp", None),
            P(None, "mp"),
            P("mp", None, None, None),
            P("mp", None),
            P(None, "mp"),
        ),
        check_vma=False,
    )
```

```python
import jax
import jax.numpy as jnp
from jax import lax
from jax.experimental import pallas as pl
from jax.experimental.pallas import tpu as pltpu
from jax.sharding import PartitionSpec as P

BF = jnp.bfloat16
F32 = jnp.float32
CHUNKS = 4


def nn(left, right):
    return jnp.dot(left, right, preferred_element_type=F32)


def nt(left, right):
    return lax.dot_general(left, right, (((1,), (1,)), ((), ())), preferred_element_type=F32)


def flip(bit, by):
    return 1 - bit if by else bit


def tile_of(index, at):
    hot = (index == at).astype(F32)
    return jnp.broadcast_to(hot, (16, 128)).astype(BF)


def masked(weights, tiles):
    parts = []
    for weight, tile in zip(weights, tiles):
        wide = jnp.concatenate([tile, tile], axis=1)
        tall = weight.reshape(weight.shape[0] // 16, 16, weight.shape[1])
        parts.append((tall * wide[None]).reshape(weight.shape))
    return jnp.concatenate(parts, axis=1)


class Place:
    def __init__(self):
        self.dp = lax.axis_index("dp")
        self.mp = lax.axis_index("mp")
        self.core = lax.rem(self.mp, 2)
        chip = lax.div(self.mp, 2)
        self.chip = chip
        self.y0 = lax.rem(chip, 2)
        self.y1 = lax.rem(lax.div(chip, 2), 2)
        self.z = lax.div(chip, 4)
        self.x0 = lax.rem(self.dp, 2)
        self.x1 = lax.rem(lax.div(self.dp, 2), 2)
        self.z_hi = lax.div(self.dp, 4)

    def mp_peer(self, chip_bits, core_bit=0):
        y0 = flip(self.y0, chip_bits & 1)
        y1 = flip(self.y1, chip_bits & 2)
        z = flip(self.z, chip_bits & 4)
        return (self.dp, ((z * 2 + y1) * 2 + y0) * 2 + flip(self.core, core_bit))

    def chip_peer(self, chip_bits):
        y0 = flip(self.y0, chip_bits & 1)
        y1 = flip(self.y1, chip_bits & 2)
        z = flip(self.z, chip_bits & 4)
        return (z * 2 + y1) * 2 + y0

    def dp_peer(self, bits):
        x0 = flip(self.x0, bits & 1)
        x1 = flip(self.x1, bits & 2)
        z = flip(self.z_hi, bits & 4)
        return ((z * 2 + x1) * 2 + x0, self.mp)

    def far_z(self):
        return (self.dp_peer(4)[0], self.mp_peer(4)[1])

    def level(self, level):
        return [None, self.mp_peer(0, 1), self.mp_peer(1), self.mp_peer(2), self.mp_peer(4)][level]


def greet(peers):
    barrier = pltpu.get_barrier_semaphore()
    for peer in peers:
        pl.semaphore_signal(barrier, inc=1, device_id=peer, device_id_type=pl.DeviceIdType.MESH)
    pl.semaphore_wait(barrier, len(peers))


def remote(src, dst, sems, at, peer):
    send, recv = sems
    return pltpu.make_async_remote_copy(
        src_ref=src,
        dst_ref=dst,
        send_sem=send.at[at],
        recv_sem=recv.at[at],
        device_id=peer,
        device_id_type=pl.DeviceIdType.MESH,
    )


def at_ds(index, size):
    return pl.ds(pl.multiple_of(index * size, size), size)


def repeat(count, step):
    lax.fori_loop(0, count, lambda at, carry: (step(at), carry)[1], 0)


class RankSum:
    def __init__(self, place, result, own, away, near, chip_sum, far, part, z_part, sems):
        self.result = result
        self.own, self.away, self.near, self.chip_sum, self.far = own, away, near, chip_sum, far
        self.part, self.z_part = part, z_part
        rows, half = near.shape[1], near.shape[2]
        step = rows // 4
        self.columns = at_ds(place.core, half)
        self.rows = at_ds(place.y1 * 2 + place.y0, step)
        sibling = place.mp_peer(0, 1)
        self.cores = remote(away, near, sems, 0, sibling)
        self.scatter = []
        self.gather = []
        mine = result.at[:, self.rows, self.columns]
        for bits in range(1, 4):
            other = at_ds(flip(place.y1, bits & 2) * 2 + flip(place.y0, bits & 1), step)
            peer = place.mp_peer(bits)
            self.scatter.append(
                remote(chip_sum.at[:, other, :], far.at[bits - 1], sems, bits, peer)
            )
            self.gather.append(remote(mine, mine, sems, 3 + bits, peer))
        self.across = remote(part, z_part, sems, 7, place.level(4))
        whole = result.at[:, :, self.columns]
        self.back = remote(whole, whole, sems, 8, sibling)

    def set(self, which, own, away):
        self.own[which] = own
        self.away[which] = away.astype(BF)

    def start(self):
        self.cores.start()

    def step_chip(self):
        self.cores.wait()

        def add(which):
            self.chip_sum[which] = (self.own[which] + self.near[which].astype(F32)).astype(BF)

        repeat(2, add)
        for copy in self.scatter:
            copy.start()

    def step_across(self):
        total = self.chip_sum[:, self.rows, :].astype(F32)
        for copy in self.scatter:
            copy.wait()
        for at in range(3):
            total = total + self.far[at].astype(F32)
        self.part[...] = total.astype(BF)
        self.across.start()

    def step_sum(self):
        self.across.wait()
        total = self.part[...].astype(F32) + self.z_part[...].astype(F32)
        self.result[:, self.rows, self.columns] = total.astype(BF)
        for copy in self.gather:
            copy.start()

    def step_back(self):
        for copy in self.gather:
            copy.wait()
        self.back.start()

    def finish(self):
        self.back.wait()


class Spread:
    def __init__(self, place, held, sems):
        self.held, self.sems = held, sems
        self.blocked = len(held.shape) == 4
        self.rows = held.shape[-2] * (2 if self.blocked else 1) // CHUNKS
        self.one, self.two, self.three = place.level(1), place.level(2), place.mp_peer(3)
        self.four = place.level(4)
        self.direct = [
            remote(held.at[0], held.at[level], sems, at, peer)
            for at, (level, peer) in enumerate(((4, self.four), (1, self.one)))
        ]

    def piece(self, slot, chunk):
        if self.blocked:
            return self.held.at[slot, lax.div(chunk, 2), at_ds(lax.rem(chunk, 2), self.rows), :]
        return self.held.at[slot, at_ds(chunk, self.rows), :]

    def near(self, chunk):
        return remote(
            self.piece(0, chunk), self.piece(2, chunk), self.sems, 2 + chunk, self.two
        )

    def onward(self, chunk):
        return remote(
            self.piece(2, chunk), self.piece(3, chunk), self.sems, 2 + CHUNKS + chunk, self.three
        )

    def start_direct(self):
        for copy in self.direct:
            copy.start()

    def start_near(self, first, count):
        repeat(count, lambda at: self.near(first + at).start())

    def pass_on(self, chunk):
        chunk = jnp.int32(chunk)
        self.near(chunk).wait_recv()
        self.onward(chunk).start()

    def wait_slot(self, level):
        self.direct[0 if level == 4 else 1].wait_recv()

    def wait_onward(self):
        repeat(CHUNKS, lambda chunk: self.onward(chunk).wait_recv())

    def close(self):
        for copy in self.direct:
            copy.wait_send()

        def finish(chunk):
            self.near(chunk).wait_send()
            self.onward(chunk).wait_send()

        repeat(CHUNKS, finish)


class Reduced:
    def __init__(self, place, grad, lead, first, second, third, relay, sems, credit, at):
        self.credit, self.at, self.lead = credit, at, lead
        blocks = pl.ds(lead, first.shape[1])
        self.grad, self.bufs = grad, (first, second, third)
        rows = grad.shape[2]
        x0, x1 = place.x0, place.x1
        cross = x0 + x1 - 2 * x0 * x1
        near, back = place.dp_peer(1), place.dp_peer(3)
        by_z = (place.level(4), place.far_z())
        self.passed = []
        self.greeted = (near, back)
        self.steps = [[] for _ in range(5)]
        self.kept = [[] for _ in range(3)]
        for h in range(2):
            keys = (cross, x1) if h == 0 else (x1, x0)
            peers = (near, back) if h == 0 else (back, near)
            offset, size = 0, rows
            for step in range(2):
                size = size // 2
                keep = pl.ds(pl.multiple_of(offset + keys[step] * size, size), size)
                send = pl.ds(pl.multiple_of(offset + (1 - keys[step]) * size, size), size)
                self.kept[step].append(keep)
                self.steps[step].append(
                    remote(
                        grad.at[h, blocks, send, :],
                        self.bufs[step].at[h],
                        sems,
                        (at, h, step),
                        peers[step],
                    )
                )
                own = grad.at[h, blocks, keep, :]
                self.steps[4 - step].append(
                    remote(own, own, sems, (at, h, 4 - step), peers[step])
                )
                offset = offset + keys[step] * size
            self.kept[2].append(self.kept[1][h])
            self.steps[2].append(
                remote(
                    grad.at[h, blocks, self.kept[1][h], :], relay.at[h], sems, (at, h, 2), by_z[h]
                )
            )
            self.passed.append(
                remote(relay.at[h], self.bufs[2].at[h], sems, (at, h, 5), by_z[1 - h])
            )

    def start(self, step):
        if step == 3:
            pl.semaphore_wait(self.credit.at[self.at], 2)
        for copy in self.steps[step]:
            copy.start()

    def turn(self, step):
        self.wait(step)
        self.start(step + 1)

    def relay(self):
        for copy, onward in zip(self.steps[2], self.passed):
            copy.wait_recv()
            onward.start()

    def wait(self, step):
        for h, copy in enumerate(self.steps[step]):
            if step == 2:
                copy.wait_send()
                self.passed[h].wait()
            else:
                copy.wait()
            if step < 3:
                keep, buf = self.kept[step][h], self.bufs[step]

                def add(n):
                    self.grad[h, self.lead + n, keep, :] = (
                        self.grad[h, self.lead + n, keep, :].astype(F32) + buf[h, n].astype(F32)
                    ).astype(BF)

                repeat(buf.shape[1], add)
        if step == 1:
            for peer in self.greeted:
                pl.semaphore_signal(
                    self.credit.at[self.at],
                    inc=1,
                    device_id=peer,
                    device_id_type=pl.DeviceIdType.MESH,
                )


def layer_kernel(
    tokens,
    out_grad,
    w1,
    index1,
    w2,
    table,
    first_left,
    first_right,
    second_left,
    second_right,
    output,
    tokens_grad,
    g_w1,
    g_fl,
    g_fr,
    g_w2,
    g_sl,
    g_sr,
    tokens_all,
    grads_all,
    w2_all,
    index_all,
    index_smem,
    hidden,
    hidden_t,
    pre_grad,
    tokens_t,
    rank_first_t,
    slope,
    own,
    away,
    chip_sum,
    part,
    near_a,
    far_a,
    z_a,
    ranks_a,
    near_b,
    far_b,
    z_b,
    ranks_b,
    swap,
    sent,
    out_in,
    *rest,
):
    bufs, rest = rest[:28], rest[28:]
    (
        tok_send,
        tok_recv,
        grad_send,
        grad_recv,
        rank_send_a,
        rank_recv_a,
        rank_send_b,
        rank_recv_b,
        w_send,
        w_recv,
        i_send,
        i_recv,
        dp_send,
        dp_recv,
        credit,
        swap_send,
        swap_recv,
        x_send,
        x_recv,
        inbox_free,
        local,
    ) = rest
    place = Place()
    rows = pre_grad.shape[0]
    half = first_left.shape[1] // 2
    width = w1.shape[2]
    mine = pl.ds(pl.multiple_of(place.core * half, half), half)
    other = pl.ds(pl.multiple_of((1 - place.core) * half, half), half)

    loads = [
        pltpu.make_async_copy(
            tokens.at[:, pl.ds(d * width, width)], tokens_all.at[0, d], local.at[d]
        )
        for d in range(2)
    ]
    loads.append(pltpu.make_async_copy(out_grad, grads_all.at[0], local.at[2]))
    loads.append(pltpu.make_async_copy(w2.at[:, 0], w2_all.at[0], local.at[3]))
    loads.append(pltpu.make_async_copy(table, index_all.at[0], local.at[4]))
    for load in loads:
        load.start()
    greet(
        [place.mp_peer(bits) for bits in range(1, 8)]
        + [place.mp_peer(0, 1)]
        + [place.dp_peer(1), place.dp_peer(3), place.far_z()]
    )
    spread_tok = Spread(place, tokens_all, (tok_send, tok_recv))
    spread_grad = Spread(place, grads_all, (grad_send, grad_recv))
    sums_a = RankSum(
        place, ranks_a, own, away, near_a, chip_sum, far_a, part, z_a, (rank_send_a, rank_recv_a)
    )
    sums_b = RankSum(
        place, ranks_b, own, away, near_b, chip_sum, far_b, part, z_b, (rank_send_b, rank_recv_b)
    )
    w_copies = [
        remote(w2.at[:, level], w2_all.at[level], (w_send, w_recv), level - 1, place.level(level))
        for level in (4, 2, 3, 1)
    ]
    i_copies = [
        remote(
            table,
            index_all.at[level],
            (i_send, i_recv),
            level - 1,
            place.level(level),
        )
        for level in range(1, 5)
    ]
    dp_sems = (dp_send, dp_recv)
    grads = ((g_w2, 0), (g_sl, 0), (g_w1, 0), (g_w1, 5), (g_fr, 0), (g_sr, 0), (g_fl, 0))
    r_w2, r_sl, r_w1a, r_w1b, r_fr, r_sr, r_fl = [
        Reduced(place, grad, lead, *bufs[4 * at : 4 * at + 4], dp_sems, credit, at)
        for at, (grad, lead) in enumerate(grads)
    ]

    def turn_tokens(level):
        def step(d):
            tokens_t[level, d] = tokens_all[level, d].T

        repeat(2, step)

    for load in loads:
        load.wait()
    spread_tok.start_near(0, CHUNKS)
    spread_tok.start_direct()
    for copy in i_copies:
        copy.start()
    both = jnp.concatenate([tokens_all[0, 0], tokens_all[0, 1]], axis=1)
    sums_a.set(0, nn(both, first_left[:, mine]), nn(both, first_left[:, other]))
    flow = grads_all[0]
    sums_a.set(1, nt(flow, second_right[mine, :]), nt(flow, second_right[other, :]))
    sums_a.start()
    turn_tokens(0)
    spread_tok.pass_on(0)
    sums_a.step_chip()
    spread_tok.pass_on(1)
    spread_tok.wait_slot(1)
    turn_tokens(1)
    spread_tok.pass_on(2)
    spread_tok.pass_on(3)
    sums_a.step_across()
    spread_grad.start_near(0, 1)
    sums_a.step_sum()
    spread_grad.start_near(1, CHUNKS - 1)
    spread_grad.start_direct()
    for copy in w_copies:
        copy.start()
    spread_tok.wait_slot(4)
    turn_tokens(4)
    spread_tok.wait_onward()

    def block_part(f):
        picks = [tokens_all[level, index1[f, level]] for level in range(5)]
        slope[f] = nn(jnp.concatenate(picks, axis=1), w1[f].reshape(5 * width, width))

    repeat(4, block_part)
    sums_a.step_back()
    spread_grad.pass_on(0)
    sums_a.finish()

    def forward(f):
        pre = slope[f] + nn(ranks_a[0], first_right[:, at_ds(f, width)])
        sigma = 1.0 / (1.0 + jnp.exp(-pre))
        active = (pre * sigma).astype(BF)
        hidden[f] = active
        hidden_t[f] = active.T
        slope[f] = sigma * (1.0 + pre * (1.0 - sigma))

    def forward_and_pass(f):
        forward(f)
        spread_grad.pass_on(f + 1)

    repeat(3, forward_and_pass)
    forward(jnp.int32(3))
    def out_part(level, e):
        return nn(hidden[index_smem[level, 4 + e, level]], w2_all[level, e])

    def tok_part(level, d):
        weights = [w1[f, level] for f in range(4)]
        tiles = [tile_of(table[f : f + 1, level : level + 1], d) for f in range(4)]
        return nt(pre_grad[...], masked(weights, tiles))

    parts = (out_part, tok_part)

    def box(side, slot, block):
        return tokens_all.at[slot, block] if side else out_in.at[slot - 1, block]

    def remote_part(side, level, peer):
        return remote(
            sent.at[level - 1],
            tokens_all.at[level] if side else out_in.at[level - 1],
            (x_send, x_recv),
            (side, level),
            peer,
        )

    peers = {1: place.level(1), 2: place.level(2), 3: place.mp_peer(3), 4: place.level(4)}
    copies = [
        {level: remote_part(side, level, peer) for level, peer in peers.items()}
        for side in range(2)
    ]

    def send_part(side, level):
        if side:
            copies[0][level].wait_send()

        def step(block):
            sent[level - 1, block] = parts[side](level, block).astype(BF)

        repeat(2, step)
        copies[side][level].start()

    def send_joined(side):
        copies[side][3].wait_recv()
        if side:
            copies[0][2].wait_send()

        def step(block):
            joined = parts[side](2, block) + box(side, 3, block)[...].astype(F32)
            sent[1, block] = joined.astype(BF)

        repeat(2, step)
        copies[side][2].start()

    def join(side, rank_part, result):
        for level in (1, 4, 2):
            copies[side][level].wait_recv()

        def step(block):
            total = parts[side](0, block) + rank_part(block)
            for level in (1, 4, 2):
                total = total + box(side, level, block)[...].astype(F32)
            result[:, at_ds(block, width)] = total.astype(BF)

        repeat(2, step)

    for copy in i_copies:
        copy.wait()
    fetch = pltpu.make_async_copy(index_all, index_smem, local.at[0])
    fetch.start()
    fetch.wait()

    def second_left_part(d):
        g_sl[lax.div(d, 2), 0, at_ds(lax.rem(d, 2), width), :] = nn(hidden_t[d], ranks_a[1]).astype(BF)

    repeat(4, second_left_part)
    r_sl.start(0)

    def second_grads(at):
        level = at + lax.div(at, 3)
        for e in range(2):
            flow = grads_all[level, :, e * width : e * width + width]
            g_w2[e, level] = nn(hidden_t[index_smem[level, 4 + e, level]], flow).astype(BF)

    turn_tokens(2)
    turn_tokens(3)
    spread_tok.close()
    for peer in peers.values():
        pl.semaphore_signal(inbox_free, inc=1, device_id=peer, device_id_type=pl.DeviceIdType.MESH)
    spread_grad.wait_slot(1)
    spread_grad.wait_slot(4)
    repeat(4, second_grads)
    spread_grad.wait_onward()
    for e in range(2):
        flow = grads_all[3, :, e * width : e * width + width]
        g_w2[e, 3] = nn(hidden_t[index_smem[3, 4 + e, 3]], flow).astype(BF)
    r_w2.start(0)

    def flow_of(level, e):
        return sent.at[level, e] if level < 4 else chip_sum.at[e]

    def hidden_back(d):
        own[0] = nt(ranks_a[1], second_left[at_ds(d, width), :])
        tiles = [
            [
                jnp.broadcast_to(
                    (index_all[level, 4 + e : 5 + e, level : level + 1] == d).astype(F32), (8, 128)
                )
                for e in range(2)
            ]
            for level in range(5)
        ]

        def step(at):
            part = at_ds(at, 64)
            for side in range(2):
                lanes = pl.ds(side * 128, 128)
                total = own[0, part, lanes].reshape(8, 8, 128)
                for level in range(5):
                    for e in range(2):
                        flow = flow_of(level, e)[part, lanes].astype(F32).reshape(8, 8, 128)
                        total = total + flow * tiles[level][e][None]
                total = total.reshape(64, 128) * slope[d, part, lanes]
                pre_grad[part, at_ds(2 * d + side, 128)] = total.astype(BF)

        repeat(rows // 64, step)

    for copy in w_copies:
        copy.wait()
    for level in range(5):
        for e in range(2):
            flow = nt(grads_all[level, :, e * width : e * width + width], w2_all[level, e])
            flow_of(level, e)[...] = flow.astype(BF)
    rank_first_t[...] = ranks_a[0].T
    repeat(4, hidden_back)
    spread_grad.close()
    r_sl.turn(0)
    r_w2.turn(0)

    def first_grads(part):
        def step(h):
            f = 2 * h + part
            picks = [tokens_t[level, index1[f, level]] for level in range(5)]
            product = nn(
                jnp.concatenate(picks + [rank_first_t[...]], axis=0),
                pre_grad[:, at_ds(f, width)],
            ).astype(BF)
            for level in range(5):
                g_w1[h, part * 5 + level] = product[level * width : level * width + width]
            for r in range(2):
                low = (5 + r) * width
                g_fr[r, 0, :, at_ds(f, width)] = product[low : low + width]

        repeat(2, step)

    first_grads(0)
    r_w1a.start(0)
    first_grads(1)
    r_w1b.start(0)
    r_fr.start(0)
    r_sl.turn(1)
    r_w2.turn(1)

    units = jnp.concatenate([hidden[d] for d in range(4)], axis=1)
    sums_b.set(0, nn(units, second_left[:, mine]), nn(units, second_left[:, other]))
    sums_b.set(1, nt(pre_grad[...], first_right[mine, :]), nt(pre_grad[...], first_right[other, :]))
    sums_b.start()
    send_part(0, 3)
    r_w1a.turn(0)
    r_sl.relay()
    r_w2.relay()
    sums_b.step_chip()
    send_part(0, 4)
    send_part(0, 1)
    r_w1b.turn(0)
    sums_b.step_across()
    r_sl.turn(2)
    r_w2.wait(2)
    quarter = r_w2.kept[2]
    swaps = [
        remote(
            g_w2.at[h, level, quarter[h], :],
            swap.at[h, level - 1],
            (swap_send, swap_recv),
            (h, level - 1),
            place.level(level),
        )
        for h in range(2)
        for level in range(1, 5)
    ]
    for copy in swaps:
        copy.start()
    r_fr.turn(0)
    r_w1a.turn(1)
    sums_b.step_sum()
    pl.semaphore_wait(inbox_free, 4)
    send_part(1, 3)
    for copy in swaps:
        copy.wait()
    for h in range(2):
        for level in range(1, 5):
            g_w2[h, level, quarter[h], :] = swap[h, level - 1]
    r_w2.start(3)
    r_w1b.turn(1)
    r_w1a.relay()
    sums_b.step_back()
    send_joined(0)
    r_sl.turn(3)
    r_fr.turn(1)
    r_w1b.relay()
    sums_b.finish()
    rank_second_t = ranks_b[0].T
    for h in range(2):
        g_sr[h, 0] = nn(rank_second_t[h * 256 : h * 256 + 256, :], grads_all[0]).astype(BF)
        g_fl[h, 0] = nn(tokens_t[0, h], ranks_b[1]).astype(BF)
    r_sr.start(0)
    r_fl.start(0)
    r_w1a.turn(2)
    send_part(1, 4)
    r_sr.turn(0)
    r_fl.turn(0)
    r_w2.turn(3)
    r_fr.relay()
    r_w1b.turn(2)
    r_sr.turn(1)
    r_fl.turn(1)
    r_fr.turn(2)
    r_w1a.turn(3)
    send_part(1, 1)
    r_sr.relay()
    r_fl.relay()
    send_joined(1)
    r_w1b.turn(3)
    r_sr.turn(2)
    r_fl.turn(2)
    r_fr.turn(3)
    join(0, lambda e: nn(ranks_b[0], second_right[:, at_ds(e, width)]), output)
    r_sr.turn(3)
    r_fl.turn(3)
    join(1, lambda d: nt(ranks_b[1], first_left[at_ds(d, width), :]), tokens_grad)
    for grad in (r_sl, r_w2, r_w1a, r_w1b, r_fr, r_sr, r_fl):
        grad.wait(4)
    for level in range(1, 5):
        copies[1][level].wait_send()


def copy_kernel(*refs):
    count = len(refs) // 2
    for at in range(count):
        refs[count + at][...] = refs[at][...]


def body(
    tokens,
    out_grad,
    first_blocks,
    first_index,
    second_blocks,
    second_index,
    first_left,
    first_right,
    second_left,
    second_right,
):
    rows, features = tokens.shape
    rank = first_left.shape[1]
    units = first_right.shape[1]
    width = first_blocks.shape[2]
    vmem = pl.BlockSpec(memory_space=pltpu.VMEM)
    smem = pl.BlockSpec(memory_space=pltpu.SMEM)
    anywhere = pl.BlockSpec(memory_space=pl.ANY)
    dma = pltpu.SemaphoreType.DMA

    def shape(*extent):
        return jax.ShapeDtypeStruct(extent, BF)

    half = rank // 2

    table = jnp.concatenate([first_index, second_index], axis=0)
    table = jnp.pad(table, ((0, 8 - table.shape[0]), (0, 128 - table.shape[1])))

    grads = [
        (2, 5, width, width),
        (2, 1, units // 2, rank),
        (2, 10, width, width),
        (2, 1, rank // 2, units),
        (2, 1, rank // 2, features),
        (2, 1, features // 2, rank),
    ]
    pieces = grads[:2] + [(2, 5, width, width)] * 2 + grads[3:]
    inboxes = []
    for two, count, tall, wide in pieces:
        for step in (2, 4, 4, 4):
            inboxes.append(pltpu.VMEM((two, count, tall // step, wide), BF))
    scratch = [
        pltpu.VMEM((5, features // width, rows, width), BF),
        pltpu.VMEM((5, rows, features), BF),
        pltpu.VMEM((5, 2, width, width), BF),
        pltpu.VMEM((5, 8, 128), jnp.int32),
        pltpu.SMEM((5, 8, 128), jnp.int32),
        pltpu.VMEM((units // width, rows, width), BF),
        pltpu.VMEM((units // width, width, rows), BF),
        pltpu.VMEM((rows, units), BF),
        pltpu.VMEM((5, features // width, width, rows), BF),
        pltpu.VMEM((rank, rows), BF),
        pltpu.VMEM((units // width, rows, width), F32),
        pltpu.VMEM((2, rows, half), F32),
        pltpu.VMEM((2, rows, half), BF),
        pltpu.VMEM((2, rows, half), BF),
        pltpu.VMEM((2, rows // 4, half), BF),
    ]
    for _ in range(2):
        scratch += [
            pltpu.VMEM((2, rows, half), BF),
            pltpu.VMEM((3, 2, rows // 4, half), BF),
            pltpu.VMEM((2, rows // 4, half), BF),
            pltpu.VMEM((2, rows, rank), BF),
        ]
    scratch += [
        pltpu.VMEM((2, 4, width // 4, width), BF),
        pltpu.VMEM((4, features // width, rows, width), BF),
        pltpu.VMEM((4, features // width, rows, width), BF),
    ]
    semaphores = [dma((2 + 2 * CHUNKS,))] * 4 + [dma((16,))] * 4 + [dma((4,))] * 4
    semaphores += [dma((7, 2, 6))] * 2 + [pltpu.SemaphoreType.REGULAR((7,))]
    semaphores += [dma((2, 4))] * 2 + [dma((2, 5))] * 2
    semaphores += [pltpu.SemaphoreType.REGULAR, dma((5,))]
    order = (2, 5, 3, 0, 1, 4)
    results = pl.pallas_call(
        layer_kernel,
        out_shape=[shape(rows, features), shape(rows, features)]
        + [shape(*grads[at]) for at in order],
        in_specs=[anywhere, anywhere, vmem, smem, anywhere, vmem] + [vmem] * 4,
        out_specs=[vmem] * 8,
        scratch_shapes=scratch + inboxes + semaphores,
        compiler_params=pltpu.CompilerParams(
            collective_id=0, has_side_effects=True, vmem_limit_bytes=63 * 2**20
        ),
        name="layer_kernel",
    )(
        tokens,
        out_grad,
        first_blocks,
        first_index,
        second_blocks,
        table,
        first_left,
        first_right,
        second_left,
        second_right,
    )
    flat = [result.reshape(-1, result.shape[-1]) for result in results]
    steps = 4
    specs = [
        pl.BlockSpec((result.shape[0] // steps, result.shape[1]), lambda at: (at, 0))
        for result in flat
    ]
    output, tokens_grad, g_w1, g_fl, g_fr, g_w2, g_sl, g_sr = pl.pallas_call(
        copy_kernel,
        out_shape=[shape(*result.shape) for result in flat],
        grid=(steps,),
        in_specs=specs,
        out_specs=specs,
        compiler_params=pltpu.CompilerParams(vmem_limit_bytes=63 * 2**20),
        name="copy_kernel",
    )(*flat)
    return (
        output,
        tokens_grad,
        g_w1.reshape(first_blocks.shape),
        g_fl.reshape(first_left.shape),
        g_fr.reshape(first_right.shape),
        g_w2.reshape(second_blocks.shape),
        g_sl.reshape(second_left.shape),
        g_sr.reshape(second_right.shape),
    )


def solution(mesh):
    placed = (
        P("dp", "mp"),
        P("dp", "mp"),
        P("mp", None, None, None),
        P("mp", None),
        P("mp", None, None, None),
        P("mp", None),
        P("mp", None),
        P(None, "mp"),
        P("mp", None),
        P(None, "mp"),
    )
    return jax.shard_map(
        body,
        mesh=mesh,
        in_specs=placed,
        out_specs=(
            P("dp", "mp"),
            P("dp", "mp"),
            P("mp", None, None, None),
            P("mp", None),
            P(None, "mp"),
            P("mp", None, None, None),
            P("mp", None),
            P(None, "mp"),
        ),
        check_vma=False,
    )
```

```python
import jax
import jax.numpy as jnp
from jax import lax
from jax.experimental import pallas as pl
from jax.experimental.pallas import tpu as pltpu
from jax.sharding import PartitionSpec as P

BF = jnp.bfloat16
F32 = jnp.float32
CHUNKS = 4


def nn(left, right):
    return jnp.dot(left, right, preferred_element_type=F32)


def nt(left, right):
    return lax.dot_general(left, right, (((1,), (1,)), ((), ())), preferred_element_type=F32)


def flip(bit, by):
    return 1 - bit if by else bit


def tile_of(index, at):
    hot = (index == at).astype(F32)
    return jnp.broadcast_to(hot, (16, 128)).astype(BF)


def masked(weights, tiles):
    parts = []
    for weight, tile in zip(weights, tiles):
        wide = jnp.concatenate([tile, tile], axis=1)
        tall = weight.reshape(weight.shape[0] // 16, 16, weight.shape[1])
        parts.append((tall * wide[None]).reshape(weight.shape))
    return jnp.concatenate(parts, axis=1)


class Place:
    def __init__(self):
        self.dp = lax.axis_index("dp")
        self.mp = lax.axis_index("mp")
        self.core = lax.rem(self.mp, 2)
        chip = lax.div(self.mp, 2)
        self.chip = chip
        self.y0 = lax.rem(chip, 2)
        self.y1 = lax.rem(lax.div(chip, 2), 2)
        self.z = lax.div(chip, 4)
        self.x0 = lax.rem(self.dp, 2)
        self.x1 = lax.rem(lax.div(self.dp, 2), 2)
        self.z_hi = lax.div(self.dp, 4)

    def mp_peer(self, chip_bits, core_bit=0):
        y0 = flip(self.y0, chip_bits & 1)
        y1 = flip(self.y1, chip_bits & 2)
        z = flip(self.z, chip_bits & 4)
        return (self.dp, ((z * 2 + y1) * 2 + y0) * 2 + flip(self.core, core_bit))

    def chip_peer(self, chip_bits):
        y0 = flip(self.y0, chip_bits & 1)
        y1 = flip(self.y1, chip_bits & 2)
        z = flip(self.z, chip_bits & 4)
        return (z * 2 + y1) * 2 + y0

    def dp_peer(self, bits):
        x0 = flip(self.x0, bits & 1)
        x1 = flip(self.x1, bits & 2)
        z = flip(self.z_hi, bits & 4)
        return ((z * 2 + x1) * 2 + x0, self.mp)

    def far_z(self):
        return (self.dp_peer(4)[0], self.mp_peer(4)[1])

    def level(self, level):
        return [None, self.mp_peer(0, 1), self.mp_peer(1), self.mp_peer(2), self.mp_peer(4)][level]


def greet(peers):
    barrier = pltpu.get_barrier_semaphore()
    for peer in peers:
        pl.semaphore_signal(barrier, inc=1, device_id=peer, device_id_type=pl.DeviceIdType.MESH)
    pl.semaphore_wait(barrier, len(peers))


def remote(src, dst, sems, at, peer):
    send, recv = sems
    return pltpu.make_async_remote_copy(
        src_ref=src,
        dst_ref=dst,
        send_sem=send.at[at],
        recv_sem=recv.at[at],
        device_id=peer,
        device_id_type=pl.DeviceIdType.MESH,
    )


def at_ds(index, size):
    return pl.ds(pl.multiple_of(index * size, size), size)


def repeat(count, step):
    lax.fori_loop(0, count, lambda at, carry: (step(at), carry)[1], 0)


class RankSum:
    def __init__(self, place, result, own, away, near, chip_sum, far, part, z_part, sems):
        self.result = result
        self.own, self.away, self.near, self.chip_sum, self.far = own, away, near, chip_sum, far
        self.part, self.z_part = part, z_part
        rows, half = near.shape[1], near.shape[2]
        step = rows // 4
        self.columns = at_ds(place.core, half)
        self.rows = at_ds(place.y1 * 2 + place.y0, step)
        sibling = place.mp_peer(0, 1)
        self.cores = remote(away, near, sems, 0, sibling)
        self.scatter = []
        self.gather = []
        mine = result.at[:, self.rows, self.columns]
        for bits in range(1, 4):
            other = at_ds(flip(place.y1, bits & 2) * 2 + flip(place.y0, bits & 1), step)
            peer = place.mp_peer(bits)
            self.scatter.append(
                remote(chip_sum.at[:, other, :], far.at[bits - 1], sems, bits, peer)
            )
            self.gather.append(remote(mine, mine, sems, 3 + bits, peer))
        self.across = remote(part, z_part, sems, 7, place.level(4))
        whole = result.at[:, :, self.columns]
        self.back = remote(whole, whole, sems, 8, sibling)

    def set(self, which, own, away):
        self.own[which] = own
        self.away[which] = away.astype(BF)

    def start(self):
        self.cores.start()

    def step_chip(self):
        self.cores.wait()

        def add(which):
            self.chip_sum[which] = (self.own[which] + self.near[which].astype(F32)).astype(BF)

        repeat(2, add)
        for copy in self.scatter:
            copy.start()

    def step_across(self):
        total = self.chip_sum[:, self.rows, :].astype(F32)
        for copy in self.scatter:
            copy.wait()
        for at in range(3):
            total = total + self.far[at].astype(F32)
        self.part[...] = total.astype(BF)
        self.across.start()

    def step_sum(self):
        self.across.wait()
        total = self.part[...].astype(F32) + self.z_part[...].astype(F32)
        self.result[:, self.rows, self.columns] = total.astype(BF)
        for copy in self.gather:
            copy.start()

    def step_back(self):
        for copy in self.gather:
            copy.wait()
        self.back.start()

    def finish(self):
        self.back.wait()


class Spread:
    def __init__(self, place, held, sems):
        self.held, self.sems = held, sems
        self.blocked = len(held.shape) == 4
        self.rows = held.shape[-2] * (2 if self.blocked else 1) // CHUNKS
        self.one, self.two, self.three = place.level(1), place.level(2), place.mp_peer(3)
        self.four = place.level(4)
        self.direct = [
            remote(held.at[0], held.at[level], sems, at, peer)
            for at, (level, peer) in enumerate(((4, self.four), (1, self.one)))
        ]

    def piece(self, slot, chunk):
        if self.blocked:
            return self.held.at[slot, lax.div(chunk, 2), at_ds(lax.rem(chunk, 2), self.rows), :]
        return self.held.at[slot, at_ds(chunk, self.rows), :]

    def near(self, chunk):
        return remote(
            self.piece(0, chunk), self.piece(2, chunk), self.sems, 2 + chunk, self.two
        )

    def onward(self, chunk):
        return remote(
            self.piece(2, chunk), self.piece(3, chunk), self.sems, 2 + CHUNKS + chunk, self.three
        )

    def start_direct(self):
        for copy in self.direct:
            copy.start()

    def start_near(self, first, count):
        repeat(count, lambda at: self.near(first + at).start())

    def pass_on(self, chunk):
        chunk = jnp.int32(chunk)
        self.near(chunk).wait_recv()
        self.onward(chunk).start()

    def wait_slot(self, level):
        self.direct[0 if level == 4 else 1].wait_recv()

    def wait_onward(self):
        repeat(CHUNKS, lambda chunk: self.onward(chunk).wait_recv())

    def close(self):
        for copy in self.direct:
            copy.wait_send()

        def finish(chunk):
            self.near(chunk).wait_send()
            self.onward(chunk).wait_send()

        repeat(CHUNKS, finish)


class Reduced:
    def __init__(self, place, grad, lead, first, second, third, relay, sems, credit, at):
        self.credit, self.at, self.lead = credit, at, lead
        blocks = pl.ds(lead, first.shape[1])
        self.grad, self.bufs = grad, (first, second, third)
        rows = grad.shape[2]
        x0, x1 = place.x0, place.x1
        cross = x0 + x1 - 2 * x0 * x1
        near, back = place.dp_peer(1), place.dp_peer(3)
        by_z = (place.level(4), place.far_z())
        self.passed = []
        self.greeted = (near, back)
        self.steps = [[] for _ in range(5)]
        self.kept = [[] for _ in range(3)]
        for h in range(2):
            keys = (cross, x1) if h == 0 else (x1, x0)
            peers = (near, back) if h == 0 else (back, near)
            offset, size = 0, rows
            for step in range(2):
                size = size // 2
                keep = pl.ds(pl.multiple_of(offset + keys[step] * size, size), size)
                send = pl.ds(pl.multiple_of(offset + (1 - keys[step]) * size, size), size)
                self.kept[step].append(keep)
                self.steps[step].append(
                    remote(
                        grad.at[h, blocks, send, :],
                        self.bufs[step].at[h],
                        sems,
                        (at, h, step),
                        peers[step],
                    )
                )
                own = grad.at[h, blocks, keep, :]
                self.steps[4 - step].append(
                    remote(own, own, sems, (at, h, 4 - step), peers[step])
                )
                offset = offset + keys[step] * size
            self.kept[2].append(self.kept[1][h])
            self.steps[2].append(
                remote(
                    grad.at[h, blocks, self.kept[1][h], :], relay.at[h], sems, (at, h, 2), by_z[h]
                )
            )
            self.passed.append(
                remote(relay.at[h], self.bufs[2].at[h], sems, (at, h, 5), by_z[1 - h])
            )

    def start(self, step):
        if step == 3:
            pl.semaphore_wait(self.credit.at[self.at], 2)
        for copy in self.steps[step]:
            copy.start()

    def turn(self, step):
        self.wait(step)
        self.start(step + 1)

    def relay(self):
        for copy, onward in zip(self.steps[2], self.passed):
            copy.wait_recv()
            onward.start()

    def wait(self, step):
        for h, copy in enumerate(self.steps[step]):
            if step == 2:
                copy.wait_send()
                self.passed[h].wait()
            else:
                copy.wait()
            if step < 3:
                keep, buf = self.kept[step][h], self.bufs[step]

                def add(n):
                    self.grad[h, self.lead + n, keep, :] = (
                        self.grad[h, self.lead + n, keep, :].astype(F32) + buf[h, n].astype(F32)
                    ).astype(BF)

                repeat(buf.shape[1], add)
        if step == 1:
            for peer in self.greeted:
                pl.semaphore_signal(
                    self.credit.at[self.at],
                    inc=1,
                    device_id=peer,
                    device_id_type=pl.DeviceIdType.MESH,
                )


def layer_kernel(
    tokens,
    out_grad,
    w1,
    index1,
    w2,
    table,
    first_left,
    first_right,
    second_left,
    second_right,
    output,
    tokens_grad,
    g_w1,
    g_fl,
    g_fr,
    g_w2,
    g_sl,
    g_sr,
    tokens_all,
    grads_all,
    w2_all,
    index_all,
    index_smem,
    hidden,
    hidden_t,
    pre_grad,
    tokens_t,
    rank_first_t,
    slope,
    own,
    away,
    chip_sum,
    part,
    near_a,
    far_a,
    z_a,
    ranks_a,
    near_b,
    far_b,
    z_b,
    ranks_b,
    swap,
    sent,
    out_in,
    *rest,
):
    bufs, rest = rest[:28], rest[28:]
    (
        tok_send,
        tok_recv,
        grad_send,
        grad_recv,
        rank_send_a,
        rank_recv_a,
        rank_send_b,
        rank_recv_b,
        w_send,
        w_recv,
        i_send,
        i_recv,
        dp_send,
        dp_recv,
        credit,
        swap_send,
        swap_recv,
        x_send,
        x_recv,
        inbox_free,
        local,
    ) = rest
    place = Place()
    rows = pre_grad.shape[0]
    half = first_left.shape[1] // 2
    width = w1.shape[2]
    mine = pl.ds(pl.multiple_of(place.core * half, half), half)
    other = pl.ds(pl.multiple_of((1 - place.core) * half, half), half)

    loads = [
        pltpu.make_async_copy(
            tokens.at[:, pl.ds(d * width, width)], tokens_all.at[0, d], local.at[d]
        )
        for d in range(2)
    ]
    loads.append(pltpu.make_async_copy(out_grad, grads_all.at[0], local.at[2]))
    loads.append(pltpu.make_async_copy(w2.at[:, 0], w2_all.at[0], local.at[3]))
    loads.append(pltpu.make_async_copy(table, index_all.at[0], local.at[4]))
    for load in loads:
        load.start()
    greet(
        [place.mp_peer(bits) for bits in range(1, 8)]
        + [place.mp_peer(0, 1)]
        + [place.dp_peer(1), place.dp_peer(3), place.far_z()]
    )
    spread_tok = Spread(place, tokens_all, (tok_send, tok_recv))
    spread_grad = Spread(place, grads_all, (grad_send, grad_recv))
    sums_a = RankSum(
        place, ranks_a, own, away, near_a, chip_sum, far_a, part, z_a, (rank_send_a, rank_recv_a)
    )
    sums_b = RankSum(
        place, ranks_b, own, away, near_b, chip_sum, far_b, part, z_b, (rank_send_b, rank_recv_b)
    )
    w_copies = [
        remote(w2.at[:, level], w2_all.at[level], (w_send, w_recv), level - 1, place.level(level))
        for level in (4, 2, 3, 1)
    ]
    i_copies = [
        remote(
            table,
            index_all.at[level],
            (i_send, i_recv),
            level - 1,
            place.level(level),
        )
        for level in range(1, 5)
    ]
    dp_sems = (dp_send, dp_recv)
    grads = ((g_w2, 0), (g_sl, 0), (g_w1, 0), (g_w1, 5), (g_fr, 0), (g_sr, 0), (g_fl, 0))
    r_w2, r_sl, r_w1a, r_w1b, r_fr, r_sr, r_fl = [
        Reduced(place, grad, lead, *bufs[4 * at : 4 * at + 4], dp_sems, credit, at)
        for at, (grad, lead) in enumerate(grads)
    ]

    def turn_tokens(level):
        def step(d):
            tokens_t[level, d] = tokens_all[level, d].T

        repeat(2, step)

    for load in loads:
        load.wait()
    spread_tok.start_near(0, CHUNKS)
    spread_tok.start_direct()
    for copy in i_copies:
        copy.start()
    both = jnp.concatenate([tokens_all[0, 0], tokens_all[0, 1]], axis=1)
    sums_a.set(0, nn(both, first_left[:, mine]), nn(both, first_left[:, other]))
    flow = grads_all[0]
    sums_a.set(1, nt(flow, second_right[mine, :]), nt(flow, second_right[other, :]))
    sums_a.start()
    turn_tokens(0)
    spread_tok.pass_on(0)
    sums_a.step_chip()
    spread_tok.pass_on(1)
    spread_tok.wait_slot(1)
    turn_tokens(1)
    spread_tok.pass_on(2)
    spread_tok.pass_on(3)
    sums_a.step_across()
    spread_grad.start_near(0, 1)
    sums_a.step_sum()
    spread_grad.start_near(1, CHUNKS - 1)
    spread_grad.start_direct()
    for copy in w_copies:
        copy.start()
    spread_tok.wait_slot(4)
    turn_tokens(4)
    spread_tok.wait_onward()

    def block_part(f):
        picks = [tokens_all[level, index1[f, level]] for level in range(5)]
        slope[f] = nn(jnp.concatenate(picks, axis=1), w1[f].reshape(5 * width, width))

    repeat(4, block_part)
    sums_a.step_back()
    spread_grad.pass_on(0)
    sums_a.finish()

    def forward(f):
        pre = slope[f] + nn(ranks_a[0], first_right[:, at_ds(f, width)])
        sigma = 1.0 / (1.0 + jnp.exp(-pre))
        active = (pre * sigma).astype(BF)
        hidden[f] = active
        hidden_t[f] = active.T
        slope[f] = sigma * (1.0 + pre * (1.0 - sigma))

    def forward_and_pass(f):
        forward(f)
        spread_grad.pass_on(f + 1)

    repeat(3, forward_and_pass)
    forward(jnp.int32(3))
    def out_part(level, e):
        return nn(hidden[index_smem[level, 4 + e, level]], w2_all[level, e])

    def tok_part(level, d):
        weights = [w1[f, level] for f in range(4)]
        tiles = [tile_of(table[f : f + 1, level : level + 1], d) for f in range(4)]
        return nt(pre_grad[...], masked(weights, tiles))

    parts = (out_part, tok_part)

    def box(side, slot, block):
        return tokens_all.at[slot, block] if side else out_in.at[slot - 1, block]

    def remote_part(side, level, peer):
        return remote(
            sent.at[level - 1],
            tokens_all.at[level] if side else out_in.at[level - 1],
            (x_send, x_recv),
            (side, level),
            peer,
        )

    peers = {1: place.level(1), 2: place.level(2), 3: place.mp_peer(3), 4: place.level(4)}
    copies = [
        {level: remote_part(side, level, peer) for level, peer in peers.items()}
        for side in range(2)
    ]

    def send_part(side, level):
        if side:
            copies[0][level].wait_send()

        def step(block):
            sent[level - 1, block] = parts[side](level, block).astype(BF)

        repeat(2, step)
        copies[side][level].start()

    def send_joined(side):
        copies[side][3].wait_recv()
        if side:
            copies[0][2].wait_send()

        def step(block):
            joined = parts[side](2, block) + box(side, 3, block)[...].astype(F32)
            sent[1, block] = joined.astype(BF)

        repeat(2, step)
        copies[side][2].start()

    def join(side, rank_part, result):
        for level in (1, 4, 2):
            copies[side][level].wait_recv()

        def step(block):
            total = parts[side](0, block) + rank_part(block)
            for level in (1, 4, 2):
                total = total + box(side, level, block)[...].astype(F32)
            result[:, at_ds(block, width)] = total.astype(BF)

        repeat(2, step)

    for copy in i_copies:
        copy.wait()
    fetch = pltpu.make_async_copy(index_all, index_smem, local.at[0])
    fetch.start()
    fetch.wait()

    def second_left_part(d):
        g_sl[lax.div(d, 2), 0, at_ds(lax.rem(d, 2), width), :] = nn(hidden_t[d], ranks_a[1]).astype(BF)

    repeat(4, second_left_part)
    r_sl.start(0)

    def second_grads(at):
        level = at + lax.div(at, 3)
        for e in range(2):
            flow = grads_all[level, :, e * width : e * width + width]
            g_w2[e, level] = nn(hidden_t[index_smem[level, 4 + e, level]], flow).astype(BF)

    turn_tokens(2)
    turn_tokens(3)
    spread_tok.close()
    for peer in peers.values():
        pl.semaphore_signal(inbox_free, inc=1, device_id=peer, device_id_type=pl.DeviceIdType.MESH)
    spread_grad.wait_slot(1)
    spread_grad.wait_slot(4)
    repeat(4, second_grads)
    spread_grad.wait_onward()
    for e in range(2):
        flow = grads_all[3, :, e * width : e * width + width]
        g_w2[e, 3] = nn(hidden_t[index_smem[3, 4 + e, 3]], flow).astype(BF)
    r_w2.start(0)

    def flow_of(level, e):
        return sent.at[level, e] if level < 4 else chip_sum.at[e]

    def hidden_back(d):
        own[0] = nt(ranks_a[1], second_left[at_ds(d, width), :])
        tiles = [
            [
                jnp.broadcast_to(
                    (index_all[level, 4 + e : 5 + e, level : level + 1] == d).astype(F32), (8, 128)
                )
                for e in range(2)
            ]
            for level in range(5)
        ]

        def step(at):
            part = at_ds(at, 64)
            for side in range(2):
                lanes = pl.ds(side * 128, 128)
                total = own[0, part, lanes].reshape(8, 8, 128)
                for level in range(5):
                    for e in range(2):
                        flow = flow_of(level, e)[part, lanes].astype(F32).reshape(8, 8, 128)
                        total = total + flow * tiles[level][e][None]
                total = total.reshape(64, 128) * slope[d, part, lanes]
                pre_grad[part, at_ds(2 * d + side, 128)] = total.astype(BF)

        repeat(rows // 64, step)

    for copy in w_copies:
        copy.wait()
    for level in range(5):
        for e in range(2):
            flow = nt(grads_all[level, :, e * width : e * width + width], w2_all[level, e])
            flow_of(level, e)[...] = flow.astype(BF)
    rank_first_t[...] = ranks_a[0].T
    repeat(4, hidden_back)
    spread_grad.close()
    r_sl.turn(0)
    r_w2.turn(0)

    for level in (3, 4, 1):
        send_part(0, level)
    units = jnp.concatenate([hidden[d] for d in range(4)], axis=1)
    sums_b.set(0, nn(units, second_left[:, mine]), nn(units, second_left[:, other]))
    sums_b.set(1, nt(pre_grad[...], first_right[mine, :]), nt(pre_grad[...], first_right[other, :]))
    sums_b.start()

    def first_grads(part):
        def step(h):
            f = 2 * h + part
            picks = [tokens_t[level, index1[f, level]] for level in range(5)]
            product = nn(
                jnp.concatenate(picks + [rank_first_t[...]], axis=0),
                pre_grad[:, at_ds(f, width)],
            ).astype(BF)
            for level in range(5):
                g_w1[h, part * 5 + level] = product[level * width : level * width + width]
            for r in range(2):
                low = (5 + r) * width
                g_fr[r, 0, :, at_ds(f, width)] = product[low : low + width]

        repeat(2, step)

    first_grads(0)
    r_w1a.start(0)
    sums_b.step_chip()
    first_grads(1)
    r_w1b.start(0)
    r_fr.start(0)
    r_sl.turn(1)
    r_w2.turn(1)

    send_joined(0)
    sums_b.step_across()
    r_w1a.turn(0)
    pl.semaphore_wait(inbox_free, 4)
    send_part(1, 3)
    r_sl.relay()
    r_w2.relay()
    sums_b.step_sum()
    r_w1b.turn(0)
    send_part(1, 4)
    r_sl.turn(2)
    r_w2.wait(2)
    quarter = r_w2.kept[2]
    swaps = [
        remote(
            g_w2.at[h, level, quarter[h], :],
            swap.at[h, level - 1],
            (swap_send, swap_recv),
            (h, level - 1),
            place.level(level),
        )
        for h in range(2)
        for level in range(1, 5)
    ]
    for copy in swaps:
        copy.start()
    r_fr.turn(0)
    r_w1a.turn(1)
    sums_b.step_back()
    for copy in swaps:
        copy.wait()
    for h in range(2):
        for level in range(1, 5):
            g_w2[h, level, quarter[h], :] = swap[h, level - 1]
    r_w2.start(3)
    sums_b.finish()
    rank_second_t = ranks_b[0].T
    for h in range(2):
        g_sr[h, 0] = nn(rank_second_t[h * 256 : h * 256 + 256, :], grads_all[0]).astype(BF)
        g_fl[h, 0] = nn(tokens_t[0, h], ranks_b[1]).astype(BF)
    r_sr.start(0)
    r_fl.start(0)
    r_w1a.relay()
    r_w1b.turn(1)
    r_sl.turn(3)
    r_fr.turn(1)
    r_w1b.relay()
    r_w1a.turn(2)
    r_sr.turn(0)
    r_fl.turn(0)
    r_w2.turn(3)
    r_fr.relay()
    r_w1b.turn(2)
    r_sr.turn(1)
    r_fl.turn(1)
    r_fr.turn(2)
    r_w1a.turn(3)
    send_part(1, 1)
    r_sr.relay()
    r_fl.relay()
    send_joined(1)
    r_w1b.turn(3)
    r_sr.turn(2)
    r_fl.turn(2)
    r_fr.turn(3)
    join(0, lambda e: nn(ranks_b[0], second_right[:, at_ds(e, width)]), output)
    r_sr.turn(3)
    r_fl.turn(3)
    join(1, lambda d: nt(ranks_b[1], first_left[at_ds(d, width), :]), tokens_grad)
    for grad in (r_sl, r_w2, r_w1a, r_w1b, r_fr, r_sr, r_fl):
        grad.wait(4)
    for level in range(1, 5):
        copies[1][level].wait_send()


def copy_kernel(*refs):
    count = len(refs) // 2
    for at in range(count):
        refs[count + at][...] = refs[at][...]


def body(
    tokens,
    out_grad,
    first_blocks,
    first_index,
    second_blocks,
    second_index,
    first_left,
    first_right,
    second_left,
    second_right,
):
    rows, features = tokens.shape
    rank = first_left.shape[1]
    units = first_right.shape[1]
    width = first_blocks.shape[2]
    vmem = pl.BlockSpec(memory_space=pltpu.VMEM)
    smem = pl.BlockSpec(memory_space=pltpu.SMEM)
    anywhere = pl.BlockSpec(memory_space=pl.ANY)
    dma = pltpu.SemaphoreType.DMA

    def shape(*extent):
        return jax.ShapeDtypeStruct(extent, BF)

    half = rank // 2

    table = jnp.concatenate([first_index, second_index], axis=0)
    table = jnp.pad(table, ((0, 8 - table.shape[0]), (0, 128 - table.shape[1])))

    grads = [
        (2, 5, width, width),
        (2, 1, units // 2, rank),
        (2, 10, width, width),
        (2, 1, rank // 2, units),
        (2, 1, rank // 2, features),
        (2, 1, features // 2, rank),
    ]
    pieces = grads[:2] + [(2, 5, width, width)] * 2 + grads[3:]
    inboxes = []
    for two, count, tall, wide in pieces:
        for step in (2, 4, 4, 4):
            inboxes.append(pltpu.VMEM((two, count, tall // step, wide), BF))
    scratch = [
        pltpu.VMEM((5, features // width, rows, width), BF),
        pltpu.VMEM((5, rows, features), BF),
        pltpu.VMEM((5, 2, width, width), BF),
        pltpu.VMEM((5, 8, 128), jnp.int32),
        pltpu.SMEM((5, 8, 128), jnp.int32),
        pltpu.VMEM((units // width, rows, width), BF),
        pltpu.VMEM((units // width, width, rows), BF),
        pltpu.VMEM((rows, units), BF),
        pltpu.VMEM((5, features // width, width, rows), BF),
        pltpu.VMEM((rank, rows), BF),
        pltpu.VMEM((units // width, rows, width), F32),
        pltpu.VMEM((2, rows, half), F32),
        pltpu.VMEM((2, rows, half), BF),
        pltpu.VMEM((2, rows, half), BF),
        pltpu.VMEM((2, rows // 4, half), BF),
    ]
    for _ in range(2):
        scratch += [
            pltpu.VMEM((2, rows, half), BF),
            pltpu.VMEM((3, 2, rows // 4, half), BF),
            pltpu.VMEM((2, rows // 4, half), BF),
            pltpu.VMEM((2, rows, rank), BF),
        ]
    scratch += [
        pltpu.VMEM((2, 4, width // 4, width), BF),
        pltpu.VMEM((4, features // width, rows, width), BF),
        pltpu.VMEM((4, features // width, rows, width), BF),
    ]
    semaphores = [dma((2 + 2 * CHUNKS,))] * 4 + [dma((16,))] * 4 + [dma((4,))] * 4
    semaphores += [dma((7, 2, 6))] * 2 + [pltpu.SemaphoreType.REGULAR((7,))]
    semaphores += [dma((2, 4))] * 2 + [dma((2, 5))] * 2
    semaphores += [pltpu.SemaphoreType.REGULAR, dma((5,))]
    order = (2, 5, 3, 0, 1, 4)
    results = pl.pallas_call(
        layer_kernel,
        out_shape=[shape(rows, features), shape(rows, features)]
        + [shape(*grads[at]) for at in order],
        in_specs=[anywhere, anywhere, vmem, smem, anywhere, vmem] + [vmem] * 4,
        out_specs=[vmem] * 8,
        scratch_shapes=scratch + inboxes + semaphores,
        compiler_params=pltpu.CompilerParams(
            collective_id=0, has_side_effects=True, vmem_limit_bytes=63 * 2**20
        ),
        name="layer_kernel",
    )(
        tokens,
        out_grad,
        first_blocks,
        first_index,
        second_blocks,
        table,
        first_left,
        first_right,
        second_left,
        second_right,
    )
    flat = [result.reshape(-1, result.shape[-1]) for result in results]
    steps = 4
    specs = [
        pl.BlockSpec((result.shape[0] // steps, result.shape[1]), lambda at: (at, 0))
        for result in flat
    ]
    output, tokens_grad, g_w1, g_fl, g_fr, g_w2, g_sl, g_sr = pl.pallas_call(
        copy_kernel,
        out_shape=[shape(*result.shape) for result in flat],
        grid=(steps,),
        in_specs=specs,
        out_specs=specs,
        compiler_params=pltpu.CompilerParams(vmem_limit_bytes=63 * 2**20),
        name="copy_kernel",
    )(*flat)
    return (
        output,
        tokens_grad,
        g_w1.reshape(first_blocks.shape),
        g_fl.reshape(first_left.shape),
        g_fr.reshape(first_right.shape),
        g_w2.reshape(second_blocks.shape),
        g_sl.reshape(second_left.shape),
        g_sr.reshape(second_right.shape),
    )


def solution(mesh):
    placed = (
        P("dp", "mp"),
        P("dp", "mp"),
        P("mp", None, None, None),
        P("mp", None),
        P("mp", None, None, None),
        P("mp", None),
        P("mp", None),
        P(None, "mp"),
        P("mp", None),
        P(None, "mp"),
    )
    return jax.shard_map(
        body,
        mesh=mesh,
        in_specs=placed,
        out_specs=(
            P("dp", "mp"),
            P("dp", "mp"),
            P("mp", None, None, None),
            P("mp", None),
            P(None, "mp"),
            P("mp", None, None, None),
            P("mp", None),
            P(None, "mp"),
        ),
        check_vma=False,
    )
```
